128 devices in a mesh: ctx: 32 (over y_lo, x, z), wsh: 4 (over y_hi, core).
Axes of the slice: x: 4, y: 4 (y_hi: 2, y_lo: 2; y = y_hi * 2 + y_lo), z: 4, core: 2. Of those that a mesh axis runs over, the one named last changes fastest.
Arguments:
- tokens: bfloat16 [4, 4096, 2048], P('wsh', 'ctx'), may hold values from -6 to 6
- cotangent: bfloat16 [4, 4096, 2048], P('wsh', 'ctx'), may hold values from -6 to 6
- block_pairs: int32 [4, 32, 2], replicated, may hold values from 0 to 63, as said below
- offsets: int32 [4], replicated, may hold values from 0 to 31
- qkv_master: float32 [2048, 4, 640], P('ctx', 'wsh'), may hold values from -0.125 to 0.125
- qkv_first: float32 [2048, 4, 640], P('ctx', 'wsh'), as said below
- qkv_second: float32 [2048, 4, 640], P('ctx', 'wsh'), as said below
- proj_master: float32 [2048, 2048], P('wsh', 'ctx'), may hold values from -3 to 3
- proj_first: float32 [2048, 2048], P('wsh', 'ctx'), as said below
- proj_second: float32 [2048, 2048], P('wsh', 'ctx'), as said below
- inner_master: float32 [2048, 2, 5632], P('ctx', None, 'wsh'), may hold values from -0.125 to 0.125
- inner_first: float32 [2048, 2, 5632], P('ctx', None, 'wsh'), as said below
- inner_second: float32 [2048, 2, 5632], P('ctx', None, 'wsh'), as said below
- down_master: float32 [5632, 2048], P('wsh', 'ctx'), may hold values from -0.078125 to 0.078125
- down_first: float32 [5632, 2048], P('wsh', 'ctx'), as said below
- down_second: float32 [5632, 2048], P('wsh', 'ctx'), as said below
- gains: float32 [2048, 2], replicated, may hold values from 0.5 to 1.5
- gain_first: float32 [2048, 2], replicated, as said below
- gain_second: float32 [2048, 2], replicated, as said below
Outputs:
- output: float32 [4, 4096, 2048], P('wsh', 'ctx')
- input_grad: float32 [4, 4096, 2048], P('wsh', 'ctx')
- qkv_new: float32 [2048, 4, 640], P('ctx', 'wsh')
- qkv_moment: float32 [2048, 4, 640], P('ctx', 'wsh')
- qkv_square: float32 [2048, 4, 640], P('ctx', 'wsh')
- proj_new: float32 [2048, 2048], P('wsh', 'ctx')
- proj_moment: float32 [2048, 2048], P('wsh', 'ctx')
- proj_square: float32 [2048, 2048], P('wsh', 'ctx')
- inner_new: float32 [2048, 2, 5632], P('ctx', None, 'wsh')
- inner_moment: float32 [2048, 2, 5632], P('ctx', None, 'wsh')
- inner_square: float32 [2048, 2, 5632], P('ctx', None, 'wsh')
- down_new: float32 [5632, 2048], P('wsh', 'ctx')
- down_moment: float32 [5632, 2048], P('wsh', 'ctx')
- down_square: float32 [5632, 2048], P('wsh', 'ctx')
- gain_new: float32 [2048, 2], replicated
- gain_moment: float32 [2048, 2], replicated
- gain_square: float32 [2048, 2], replicated
The draws below stay inside these ranges and needn't reach their ends.
Inputs may be any that keep to these rules, and one draw needn't show every extreme that they name: `block_pairs`: for each sequence, entry [s, c, 0] is a block p below 32 and entry [s, c, 1] is its mirror 64 - 1 - p; every block of a sequence appears once. `qkv_first`: both signs. `qkv_second`: positive. `proj_first`: both signs. `proj_second`: positive. `inner_first`: both signs. `inner_second`: positive. `down_first`: both signs. `down_second`: positive. `gain_first`: both signs. `gain_second`: positive.
All inputs are finite; a program needn't handle non-finite values.
Results may differ from the reference program's by a relative error of at most 0.02.
Values may be sent and summed in bfloat16 or wider, within the bound.
A program may use at most 192 MiB of HBM per device.

```python
import math
import jax
import jax.numpy as jnp
from jax import lax

D = 2048
H = 32
KVH = 4
HD = 64
FF = 5632
SEQS = 4
BLK = 64
STEP = 7
NBLK = 64
SEQ = 4096
TOKENS = 16384
QKVG = 640


def signed_state(rand_key, array_shape, spread):
    return spread * jax.random.uniform(rand_key, array_shape, jnp.float32, -2.0, 2.0)


def square_state(rand_key, array_shape, square):
    return square * jnp.exp(jax.random.uniform(rand_key, array_shape, jnp.float32, 0.0, math.log(4.0)))


def permute_one(subkey):
    return jax.random.permutation(subkey, NBLK // 2)


def draw_block_pairs(key, part):
    key = jax.random.fold_in(key, 1)
    orders = jax.vmap(permute_one)(jax.random.split(key, SEQS))
    return jnp.stack([orders, NBLK - 1 - orders], -1).astype(jnp.int32)


def draw_qkv_first(key, part):
    key = jax.random.fold_in(key, 2)
    return signed_state(key, (D, KVH, QKVG), math.sqrt(0.36 * TOKENS))


def draw_qkv_second(key, part):
    key = jax.random.fold_in(key, 3)
    return square_state(key, (D, KVH, QKVG), 0.36 * TOKENS)


def draw_proj_first(key, part):
    key = jax.random.fold_in(key, 4)
    return signed_state(key, (H * HD, D), math.sqrt(5.4 * SEQS))


def draw_proj_second(key, part):
    key = jax.random.fold_in(key, 5)
    return square_state(key, (H * HD, D), 5.4 * SEQS)


def draw_inner_first(key, part):
    key = jax.random.fold_in(key, 6)
    return signed_state(key, (D, 2, FF), math.sqrt(TOKENS / 9.0))


def draw_inner_second(key, part):
    key = jax.random.fold_in(key, 7)
    return square_state(key, (D, 2, FF), TOKENS / 9.0)


def draw_down_first(key, part):
    key = jax.random.fold_in(key, 8)
    return signed_state(key, (FF, D), math.sqrt(0.36 * TOKENS))


def draw_down_second(key, part):
    key = jax.random.fold_in(key, 9)
    return square_state(key, (FF, D), 0.36 * TOKENS)


def draw_gain_first(key, part):
    key = jax.random.fold_in(key, 10)
    return signed_state(key, (D, 2), math.sqrt(TOKENS / 2.0))


def draw_gain_second(key, part):
    key = jax.random.fold_in(key, 11)
    return square_state(key, (D, 2), TOKENS / 2.0)


def with_ends(values, key, smallest, top_value):
    spot = [jax.random.randint(jax.random.fold_in(key, axis), (), 0, length) for axis, length in enumerate(values.shape)]
    main_axis = values.shape.index(max(values.shape))
    next_to = spot[:main_axis] + [(spot[main_axis] + 1) % values.shape[main_axis]] + spot[main_axis + 1:]
    return values.at[tuple(spot)].set(smallest).at[tuple(next_to)].set(top_value)


def shard_levels(key, extent, cuts, least, largest):
    def one(dim, parts):
        heights = jax.random.uniform(jax.random.fold_in(jax.random.fold_in(key, 6), dim), (parts,), jnp.float32, least / len(cuts), largest / len(cuts))
        return jnp.repeat(jnp.exp(heights), extent[dim] // parts).reshape((-1,) + (1,) * (len(extent) - dim - 1))

    level = one(*cuts[0])
    for cut in cuts[1:]:
        level = level * one(*cut)
    return level


def noise(own_key, dims, deviation, most, cuts=(), kind=jnp.bfloat16):
    array = deviation * jax.random.normal(own_key, dims, jnp.float32)
    if cuts:
        array = array * shard_levels(own_key, dims, cuts, -0.22, 0.18)
    return jnp.clip(array, -most, most).astype(kind)


def setup_inputs(seed: int = 0) -> dict:
    arg_keys = jax.random.split(jax.random.key(seed), 20)
    tokens = noise(arg_keys[0], (SEQS, SEQ, D), 1.0, 6.0, ((0, 4), (1, 32)))
    cotangent = noise(arg_keys[1], (SEQS, SEQ, D), 1.0, 6.0, ((0, 4), (1, 32)))
    block_pairs = draw_block_pairs(jax.random.fold_in(arg_keys[19], 71), 0)
    offsets = with_ends(jax.random.randint(arg_keys[3], (4,), 0, NBLK // 2), jax.random.fold_in(arg_keys[3], 1), 0, (NBLK // 2) - 1).astype(jnp.int32)
    qkv_master = noise(arg_keys[4], (D, KVH, QKVG), D ** -0.5, 0.125, ((0, 32), (1, 4)), jnp.float32)
    qkv_first = draw_qkv_first(jax.random.fold_in(arg_keys[19], 71), 0)
    qkv_second = draw_qkv_second(jax.random.fold_in(arg_keys[19], 71), 0)
    proj_master = noise(arg_keys[7], (H * HD, D), (max(H * HD * 8 // SEQ, 1)) ** -0.5, 3.0, ((0, 4), (1, 32)), jnp.float32)
    proj_first = draw_proj_first(jax.random.fold_in(arg_keys[19], 71), 0)
    proj_second = draw_proj_second(jax.random.fold_in(arg_keys[19], 71), 0)
    inner_master = noise(arg_keys[10], (D, 2, FF), D ** -0.5, 0.125, ((0, 32), (2, 4)), jnp.float32)
    inner_first = draw_inner_first(jax.random.fold_in(arg_keys[19], 71), 0)
    inner_second = draw_inner_second(jax.random.fold_in(arg_keys[19], 71), 0)
    down_master = noise(arg_keys[13], (FF, D), FF ** -0.5, 0.078125, ((0, 4), (1, 32)), jnp.float32)
    down_first = draw_down_first(jax.random.fold_in(arg_keys[19], 71), 0)
    down_second = draw_down_second(jax.random.fold_in(arg_keys[19], 71), 0)
    gains = jnp.clip(1.0 + 0.1 * jax.random.normal(arg_keys[16], (D, 2), jnp.float32), 0.5, 1.5)
    gain_first = draw_gain_first(jax.random.fold_in(arg_keys[19], 71), 0)
    gain_second = draw_gain_second(jax.random.fold_in(arg_keys[19], 71), 0)
    return dict(tokens=tokens, cotangent=cotangent, block_pairs=block_pairs, offsets=offsets, qkv_master=qkv_master, qkv_first=qkv_first, qkv_second=qkv_second, proj_master=proj_master, proj_first=proj_first, proj_second=proj_second, inner_master=inner_master, inner_first=inner_first, inner_second=inner_second, down_master=down_master, down_first=down_first, down_second=down_second, gains=gains, gain_first=gain_first, gain_second=gain_second)


NORM_EPS = 1e-05
ROPE_BASE = 10000.0
BETA_FIRST = 0.5
BETA_SECOND = 0.5
ADAM_EPS = 1e-08
WEIGHT_DECAY = 0.1
GAIN_RATE = 0.4

@jax.custom_vjp
def low(v):
    return lax.optimization_barrier(v.astype(jnp.bfloat16)).astype(jnp.float32)

@jax.custom_vjp
def low_back(v):
    return v

def low_keep(v):
    return (low(v), None)

def low_pass(kept, grad):
    return (grad,)

def back_keep(v):
    return (v, None)

def back_low(kept, grad):
    return (low(grad),)
low.defvjp(low_keep, low_pass)
low_back.defvjp(back_keep, back_low)

def rope_tables(positions):
    half_width = HD // 2
    inverse = ROPE_BASE ** (-(jnp.arange(half_width, dtype=jnp.float32) * 2.0 / HD))
    angles = positions.astype(jnp.float32)[..., None] * inverse
    angles = jnp.concatenate([angles, angles], -1)
    return (jnp.cos(angles), jnp.sin(angles))

def rotate(vectors, cosine_table, sine_table):
    half_width = vectors.shape[-1] // 2
    turned = jnp.concatenate([-vectors[..., half_width:], vectors[..., :half_width]], -1)
    return vectors * cosine_table + turned * sine_table

def one_sequence(tokens_row, qkv_weight, proj_weight, inner_weight, down_weight, gain_pair, positions):
    highest = lax.Precision.HIGHEST
    group_size = H // KVH
    scaling = HD ** (-0.5)
    block_ids = positions // BLK
    first_scale = lax.rsqrt(lax.optimization_barrier(jnp.mean(tokens_row * tokens_row, -1, keepdims=True)) + NORM_EPS)
    normed = low(tokens_row * first_scale * gain_pair[:, 0])
    projected = low_back(jnp.einsum('td,dgc->tgc', normed, low(qkv_weight), precision=highest))
    cosine_table, sine_table = rope_tables(positions)
    query_width = group_size * HD
    queries = projected[..., :query_width].reshape(SEQ, KVH, group_size, HD)
    queries = low(rotate(queries, cosine_table[:, None, None, :], sine_table[:, None, None, :]))
    key_rows = low(rotate(projected[..., query_width:query_width + HD], cosine_table[:, None, :], sine_table[:, None, :]))
    values = low(projected[..., query_width + HD:])
    query_rows = SEQ // 8

    def attend(block_item):
        query_part, query_blocks = block_item
        scores = low_back(jnp.einsum('qgjh,kgh->gjqk', query_part, key_rows, precision=highest) * scaling)
        allowed = block_ids[None, None, None, :] <= query_blocks[None, None, :, None]
        weights = jnp.where(allowed, jnp.exp(scores), 0.0)
        totals = lax.optimization_barrier(jnp.sum(weights, -1))
        summed = low_back(jnp.einsum('gjqk,kgh->qgjh', low(weights), values, precision=highest))
        return summed / jnp.transpose(totals, (2, 0, 1))[..., None]
    attended = lax.map(jax.checkpoint(attend), (queries.reshape(8, query_rows, KVH, group_size, HD), block_ids.reshape(8, query_rows)))
    attended = low(attended.reshape(SEQ, H * HD))
    middle = tokens_row + low_back(jnp.dot(attended, low(proj_weight), precision=highest))
    second_scale = lax.rsqrt(lax.optimization_barrier(jnp.mean(middle * middle, -1, keepdims=True)) + NORM_EPS)
    normed_two = low(middle * second_scale * gain_pair[:, 1])
    gate_up = low_back(jnp.einsum('td,duf->tuf', normed_two, low(inner_weight), precision=highest))
    activated = low(jax.nn.silu(gate_up[:, 0]) * gate_up[:, 1])
    return middle + low_back(jnp.dot(activated, low(down_weight), precision=highest))

def adamw_step(master, first_state, second_state, gradient, rate_value):
    first_new = BETA_FIRST * first_state + (1.0 - BETA_FIRST) * gradient
    second_new = BETA_SECOND * second_state + (1.0 - BETA_SECOND) * gradient * gradient
    first_fix = 1.0 - BETA_FIRST ** STEP
    second_fix = 1.0 - BETA_SECOND ** STEP
    update = first_new / first_fix / (jnp.sqrt(second_new / second_fix) + ADAM_EPS)
    return (master - rate_value * (update + WEIGHT_DECAY * master), first_new, second_new)

def reference(tokens, cotangent, block_pairs, offsets, qkv_master, qkv_first, qkv_second, proj_master, proj_first, proj_second, inner_master, inner_first, inner_second, down_master, down_first, down_second, gains, gain_first, gain_second):
    piece_rows = D // (NBLK // 2)
    shifts = offsets.astype(jnp.int32) * piece_rows
    natural = (jnp.roll(qkv_master, shifts[0], axis=0), jnp.roll(proj_master, shifts[1], axis=1), jnp.roll(inner_master, shifts[2], axis=0), jnp.roll(down_master, shifts[3], axis=1), gains)
    positions = (block_pairs[:, :, :, None] * BLK + jnp.arange(BLK, dtype=jnp.int32)).reshape(SEQS, SEQ).astype(jnp.int32)

    def per_sequence(grad_sums, sequence_item):
        tokens_row, cotangent_row, position_row = sequence_item

        def forward(row_values, *params):
            return one_sequence(row_values, *params, position_row)
        result, pullback = jax.vjp(forward, tokens_row.astype(jnp.float32), *natural)
        gradients = pullback(cotangent_row.astype(jnp.float32))
        return (jax.tree.map(jnp.add, grad_sums, tuple(gradients[1:])), (result, gradients[0]))
    zero_grads = jax.tree.map(jnp.zeros_like, natural)
    grad_sums, (outputs, input_grads) = lax.scan(per_sequence, zero_grads, (tokens, cotangent, positions))
    qkv_grad = jnp.roll(grad_sums[0], -shifts[0], axis=0)
    proj_grad = jnp.roll(grad_sums[1], -shifts[1], axis=1)
    inner_grad = jnp.roll(grad_sums[2], -shifts[2], axis=0)
    down_grad = jnp.roll(grad_sums[3], -shifts[3], axis=1)
    rate_rows = 2.0 / D ** 0.5
    rate_proj = 2.0 / max(H * HD * 8 // SEQ, 1) ** 0.5
    rate_down = 2.0 / FF ** 0.5
    qkv_new, qkv_moment, qkv_square = adamw_step(qkv_master, qkv_first, qkv_second, qkv_grad, rate_rows)
    proj_new, proj_moment, proj_square = adamw_step(proj_master, proj_first, proj_second, proj_grad, rate_proj)
    inner_new, inner_moment, inner_square = adamw_step(inner_master, inner_first, inner_second, inner_grad, rate_rows)
    down_new, down_moment, down_square = adamw_step(down_master, down_first, down_second, down_grad, rate_down)
    gain_new, gain_moment, gain_square = adamw_step(gains, gain_first, gain_second, grad_sums[4], GAIN_RATE)
    return (outputs, input_grads, qkv_new, qkv_moment, qkv_square, proj_new, proj_moment, proj_square, inner_new, inner_moment, inner_square, down_new, down_moment, down_square, gain_new, gain_moment, gain_square)
```

```python
import math

import jax
import jax.numpy as jnp
from jax import lax
from jax.experimental import pallas as pl
from jax.experimental.pallas import tpu as pltpu
from jax.sharding import PartitionSpec as P
MESH = pl.DeviceIdType.MESH
F32, BF = jnp.float32, jnp.bfloat16
VM, HB, SM = pltpu.VMEM, pl.ANY, pltpu.SMEM

D = 2048
HD = 64
FF = 5632
BLK = 64
STEP = 7
NORM_EPS = 1e-05
ROPE_BASE = 10000.0
BETA_FIRST = 0.5
BETA_SECOND = 0.5
ADAM_EPS = 1e-08
WEIGHT_DECAY = 0.1
GAIN_RATE = 0.4

AG_SEMS = 81
RS_SEMS = 81


class Place:
    def __init__(self):
        c = lax.axis_index("ctx")
        w = lax.axis_index("wsh")
        self.c, self.w = c, w
        self.yl, self.x, self.z = c // 16, (c // 4) % 4, c % 4
        self.yh, self.co = w // 2, w % 2

    def at(self, yl, x, z):
        return yl * 16 + x * 4 + z

    def ctx(self, idx):
        return (idx, self.w)

    def step(self, axis, k):
        if axis == "x":
            return self.ctx(self.at(self.yl, (self.x + k + 4) % 4, self.z))
        return self.ctx(self.at(self.yl, self.x, (self.z + k + 4) % 4))

    def mate(self):
        return self.ctx(self.at(1 - self.yl, self.x, self.z))

    def over(self):
        return (self.c, (1 - self.yh) * 2 + self.co)

    def twin(self):
        return (self.c, self.yh * 2 + 1 - self.co)

    def piece(self, half, v, dp, dq):
        yl = self.yl if v == 0 else 1 - self.yl
        if half == 0:
            return self.at(yl, (self.x + dp + 4) % 4, (self.z + dq + 4) % 4)
        return self.at(yl, (self.x + dq + 4) % 4, (self.z + dp + 4) % 4)


def greet(place, ctx=True, wsh=True):
    bar = pltpu.get_barrier_semaphore()
    peers = []
    if ctx:
        peers += [place.step("x", 1), place.step("x", -1), place.step("z", 1), place.step("z", -1), place.mate()]
    if wsh:
        peers += [place.over(), place.twin()]
    for peer in peers:
        pl.semaphore_signal(bar, inc=1, device_id=peer, device_id_type=MESH)
    pl.semaphore_wait(bar, len(peers))


class Wire:
    def __init__(self, ssem, rsem):
        self.ssem, self.rsem, self.sent = ssem, rsem, []

    def send(self, k, src, dst, to):
        cp = pltpu.make_async_remote_copy(src, dst, self.ssem.at[k], self.rsem.at[k], device_id=to, device_id_type=MESH)
        cp.start()
        self.sent.append(cp)

    def arrive(self, k, view, frm):
        pltpu.make_async_remote_copy(view, view, self.ssem.at[k], self.rsem.at[k], device_id=frm, device_id_type=MESH).wait_recv()

    def drain(self):
        for cp in self.sent:
            cp.wait_send()
        self.sent = []


AXES = (("x", "z"), ("z", "x"))
GROUPS = (0, -1, 1, 2)


def gather_steps(pc, src, dst, ssem, rsem, lsem):
    wire = Wire(ssem, rsem)
    R = src.shape[0]
    H, S = R // 2, R // 4

    def part(v, h, dp, dq, lo=0, n=None):
        return dst.at[pc.piece(h, v, dp, dq), pl.ds(h * H + lo, H if n is None else n)]

    def key(v, h, k):
        return (v * 2 + h) * 20 + k

    local = pltpu.make_async_copy(src, dst.at[pc.c], lsem)
    local.start()
    wire.send(80, src, dst.at[pc.c], pc.mate())

    def first(v, h):
        A, B = AXES[h]
        view = src.at[pl.ds(h * H, H)] if v == 0 else part(v, h, 0, 0)
        there = part(v, h, 0, 0)
        wire.send(key(v, h, 0), view, there, pc.step(A, 1))
        wire.send(key(v, h, 1), view, there, pc.step(A, -1))
        wire.send(key(v, h, 4), view, there, pc.step(B, 1))
        wire.send(key(v, h, 5), view, there, pc.step(B, -1))

    def along(v, h, gi):
        A, B = AXES[h]
        view = part(v, h, GROUPS[gi], 0)
        wire.send(key(v, h, 4 + 4 * gi), view, view, pc.step(B, 1))
        wire.send(key(v, h, 5 + 4 * gi), view, view, pc.step(B, -1))

    def spread1(v, h):
        A, B = AXES[h]
        wire.arrive(key(v, h, 0), part(v, h, -1, 0), pc.step(A, -1))
        s = part(v, h, -1, 0, 0, S)
        wire.send(key(v, h, 2), s, s, pc.step(A, 1))
        along(v, h, 1)
        wire.arrive(key(v, h, 1), part(v, h, 1, 0), pc.step(A, 1))
        s = part(v, h, 1, 0, S, S)
        wire.send(key(v, h, 3), s, s, pc.step(A, -1))
        along(v, h, 2)

    def spread2(v, h):
        A, B = AXES[h]
        wire.arrive(key(v, h, 2), part(v, h, 2, 0, 0, S), pc.step(A, -1))
        wire.arrive(key(v, h, 3), part(v, h, 2, 0, S, S), pc.step(A, 1))
        along(v, h, 3)

    def pass_on(v, h, gi):
        A, B = AXES[h]
        g = GROUPS[gi]
        k = 4 + 4 * gi
        wire.arrive(key(v, h, k), part(v, h, g, -1), pc.step(B, -1))
        s = part(v, h, g, -1, 0, S)
        wire.send(key(v, h, k + 2), s, s, pc.step(B, 1))
        wire.arrive(key(v, h, k + 1), part(v, h, g, 1), pc.step(B, 1))
        s = part(v, h, g, 1, S, S)
        wire.send(key(v, h, k + 3), s, s, pc.step(B, -1))

    for h in (0, 1):
        first(0, h)
    yield
    wire.arrive(80, dst.at[pc.piece(0, 1, 0, 0)], pc.mate())
    for h in (0, 1):
        first(1, h)
    yield
    for v in (0, 1):
        for h in (0, 1):
            spread1(v, h)
        yield
    for v in (0, 1):
        for h in (0, 1):
            spread2(v, h)
        yield
    for gi in range(4):
        for v in (0, 1):
            for h in (0, 1):
                pass_on(v, h, gi)
            yield
    for gi in range(4):
        for v in (0, 1):
            for h in (0, 1):
                A, B = AXES[h]
                k = 4 + 4 * gi
                wire.arrive(key(v, h, k + 2), part(v, h, GROUPS[gi], 2, 0, S), pc.step(B, -1))
                wire.arrive(key(v, h, k + 3), part(v, h, GROUPS[gi], 2, S, S), pc.step(B, 1))
        yield
    wire.drain()
    local.wait()


def scatter_steps(pc, part, buf, ssem, rsem, finish):
    wire = Wire(ssem, rsem)
    R = part.shape[1]
    H, S = R // 2, R // 4

    def key(v, h, k):
        return (v * 2 + h) * 20 + k

    def box(v, h, gi, which):
        base = ((v * 2 + h) * 5 + gi) * (R + H)
        off, n = ((0, S), (S, S), (2 * S, H), (2 * S + H, H))[which]
        return buf.at[pl.ds(base + off, n)]

    def mine(v, h, dp, dq, lo=0, n=None):
        return part.at[pc.piece(h, v, dp, dq), pl.ds(h * H + lo, H if n is None else n)]

    def add(to, *more):
        total = to[...].astype(F32)
        for m in more:
            total = total + m[...].astype(F32)
        to[...] = total.astype(BF)

    def where(stage, gi, d):
        return (GROUPS[gi], d) if stage == 1 else (d, 0)

    def ring_axis(stage, h):
        return AXES[h][1] if stage == 1 else AXES[h][0]

    def raw(v, h, gi, stage):
        X = ring_axis(stage, h)
        k = 4 * gi
        wire.send(key(v, h, k), mine(v, h, *where(stage, gi, -2), 0, S), box(v, h, gi, 0), pc.step(X, -1))
        wire.send(key(v, h, k + 1), mine(v, h, *where(stage, gi, 2), S, S), box(v, h, gi, 1), pc.step(X, 1))

    def mid(v, h, gi, stage):
        X = ring_axis(stage, h)
        k = 4 * gi
        wire.arrive(key(v, h, k), box(v, h, gi, 0), pc.step(X, 1))
        add(mine(v, h, *where(stage, gi, -1), 0, S), box(v, h, gi, 0))
        wire.send(key(v, h, k + 2), mine(v, h, *where(stage, gi, -1)), box(v, h, gi, 2), pc.step(X, -1))
        wire.arrive(key(v, h, k + 1), box(v, h, gi, 1), pc.step(X, -1))
        add(mine(v, h, *where(stage, gi, 1), S, S), box(v, h, gi, 1))
        wire.send(key(v, h, k + 3), mine(v, h, *where(stage, gi, 1)), box(v, h, gi, 3), pc.step(X, 1))

    def end(v, h, gi, stage):
        X = ring_axis(stage, h)
        k = 4 * gi
        wire.arrive(key(v, h, k + 2), box(v, h, gi, 2), pc.step(X, 1))
        wire.arrive(key(v, h, k + 3), box(v, h, gi, 3), pc.step(X, -1))
        add(mine(v, h, *where(stage, gi, 0)), box(v, h, gi, 2), box(v, h, gi, 3))

    order = (3, 1, 2, 0)
    for gi in order:
        for v in (1, 0):
            for h in (0, 1):
                raw(v, h, gi, 1)
    yield
    for gi in order:
        for v in (1, 0):
            for h in (0, 1):
                mid(v, h, gi, 1)
            yield
    for v in (1, 0):
        for gi in order:
            for h in (0, 1):
                end(v, h, gi, 1)
            if gi == 3:
                for h in (0, 1):
                    raw(v, h, 4, 2)
            yield
        if v == 1:
            for h in (0, 1):
                mid(1, h, 4, 2)
            yield
    for h in (0, 1):
        end(1, h, 4, 2)
    theirs = part.at[pc.piece(0, 1, 0, 0)]
    tail = buf.at[pl.ds(30 * R, R)]
    wire.send(80, theirs, tail, pc.mate())
    yield
    for h in (0, 1):
        mid(0, h, 4, 2)
    yield
    for h in (0, 1):
        end(0, h, 4, 2)
    yield
    wire.arrive(80, tail, pc.mate())
    finish(part.at[pc.c], tail)
    wire.drain()


def run_all(*gens):
    live = list(gens)
    while live:
        for g in list(live):
            try:
                next(g)
            except StopIteration:
                live.remove(g)


def fold_steps(pc, part, b0, b1, sb, b2, ssem, rsem, base, chunks, each):
    wire = Wire(ssem, rsem)
    n = part.shape[1] // chunks
    rows = [pl.ds(k * n, n) for k in range(chunks)]
    far_twin = (1 - pc.yh) * 2 + 1 - pc.co
    near_twin = pc.yh * 2 + 1 - pc.co
    far = (1 - pc.yh) * 2 + pc.co
    for k in range(chunks):
        wire.send(base + k, part.at[far_twin, rows[k]], b0.at[rows[k]], pc.twin())
    for k in range(chunks):
        wire.send(base + chunks + k, part.at[near_twin, rows[k]], b1.at[rows[k]], pc.twin())
    yield
    for k in range(chunks):
        wire.arrive(base + k, b0.at[rows[k]], pc.twin())
        sb[rows[k]] = (part[far, rows[k]].astype(F32) + b0[rows[k]].astype(F32)).astype(BF)
        wire.send(base + 2 * chunks + k, sb.at[rows[k]], b2.at[rows[k]], pc.over())
    yield
    for k in range(chunks):
        wire.arrive(base + chunks + k, b1.at[rows[k]], pc.twin())
        near = part[pc.w, rows[k]].astype(F32) + b1[rows[k]].astype(F32)
        wire.arrive(base + 2 * chunks + k, b2.at[rows[k]], pc.over())
        each(k, near + b2[rows[k]].astype(F32))
        yield
    wire.drain()


class Share:
    def __init__(self, pc, dst, ssem, rsem, base, chunks):
        self.wire = Wire(ssem, rsem)
        self.pc, self.dst, self.base, self.chunks = pc, dst, base, chunks
        self.n = dst.shape[1] // chunks

    def at(self, w, k):
        return self.dst.at[w, pl.ds(k * self.n, self.n)]

    def send(self, k):
        pc = self.pc
        self.wire.send(self.base + k, self.at(pc.w, k), self.at(pc.w, k), pc.over())
        self.wire.send(self.base + self.chunks + k, self.at(pc.w, k), self.at(pc.w, k), pc.twin())

    def finish_steps(self):
        pc, n = self.pc, self.chunks
        over = (1 - pc.yh) * 2 + pc.co
        for k in range(n):
            self.wire.arrive(self.base + k, self.at(over, k), pc.over())
            self.wire.send(self.base + 2 * n + k, self.at(over, k), self.at(over, k), pc.twin())
            yield
        for k in range(n):
            self.wire.arrive(self.base + n + k, self.at(pc.yh * 2 + 1 - pc.co, k), pc.twin())
        for k in range(n):
            self.wire.arrive(self.base + 2 * n + k, self.at((1 - pc.yh) * 2 + 1 - pc.co, k), pc.twin())
        self.wire.drain()


def turn(value, table, row, buf):
    count = value.shape[1] // 128
    swapped = [pltpu.roll(value[:, m * 128 : (m + 1) * 128], 64, 1) for m in range(count)]
    low = lax.broadcasted_iota(jnp.int32, swapped[0].shape, 1) < 64
    for m in range(count):
        buf[0, m] = value[:, m * 128 : (m + 1) * 128]
        buf[1, m] = jnp.where(low, swapped[m], swapped[(m + 1) % count])
    odd = table[row, count]
    return jnp.concatenate([buf[odd, table[row, m]] for m in range(count)], axis=1)


def turn_table(pieces):
    pieces = jnp.stack(pieces) % 32
    blocks = (jnp.arange(16, dtype=jnp.int32)[None] - (pieces[:, None] + 1) // 2) % 16
    return jnp.concatenate([blocks, pieces[:, None] % 2], 1).astype(jnp.int32)


def dma(n):
    return pltpu.SemaphoreType.DMA((n,))


def params(cid):
    return pltpu.CompilerParams(collective_id=cid, has_side_effects=True, vmem_limit_bytes=62 << 20)


def vm(shape, dtype):
    return pltpu.VMEM(shape, dtype)


def sds(shape, dtype):
    return jax.ShapeDtypeStruct(shape, dtype)


def spec(space):
    return pl.BlockSpec(memory_space=space)


CHUNKS = 4
ONE = pltpu.SemaphoreType.DMA(())


def open_kernel(a_ref, w_ref, all_ref, full_ref, gs, gr, gl, ss, sr):
    pc = Place()
    all_ref[pc.w] = a_ref[...]
    greet(pc)
    share = Share(pc, all_ref, ss, sr, 0, CHUNKS)
    for k in range(CHUNKS):
        share.send(k)
    run_all(gather_steps(pc, w_ref, full_ref, gs, gr, gl), share.finish_steps())


def open_call(a, w):
    return pl.pallas_call(
        open_kernel,
        out_shape=(sds((4,) + a.shape, BF), sds((32,) + w.shape, BF)),
        in_specs=[spec(VM), spec(HB)],
        out_specs=(spec(VM), spec(HB)),
        scratch_shapes=[dma(AG_SEMS), dma(AG_SEMS), ONE, dma(3 * CHUNKS), dma(3 * CHUNKS)],
        compiler_params=params(0),
        name="open_gather",
    )(a, w)


def upper_lanes(shape):
    return lax.broadcasted_iota(jnp.int32, shape, 1) >= 64


def head_tile(pair, odd, upper):
    moved = pair if odd == upper else pltpu.roll(pair, 64, 1)
    lanes = upper_lanes(pair.shape)
    return jnp.where(lanes if upper else jnp.logical_not(lanes), moved, 0.0)


def dot_nt(a, b):
    return lax.dot_general(a, b, (((1,), (1,)), ((), ())), preferred_element_type=F32)


def dot_nn(a, b):
    return lax.dot_general(a, b, (((1,), (0,)), ((), ())), preferred_element_type=F32)


def dot_tn(a, b):
    return lax.dot_general(a, b, (((0,), (0,)), ((), ())), preferred_element_type=F32)


def attend_kernel(
    pick_ref, home_ref, q_ref, kv_ref, w_ref, t_ref,
    o_ref, inv_ref, nat_ref, full_ref, tail_ref,
    kvg, qt, acc, ks, kr, kl, gs, gr, gl, ss, sr,
):
    pc = Place()
    tail_ref[pc.w] = t_ref[...]
    greet(pc)
    keys = gather_steps(pc, kv_ref, kvg, ks, kr, kl)
    weights = gather_steps(pc, w_ref, full_ref, gs, gr, gl)
    share = Share(pc, tail_ref, ss, sr, 0, CHUNKS)
    rest = share.finish_steps()
    next(keys)
    next(keys)
    next(weights)
    for k in range(CHUNKS):
        share.send(k)
    for s in range(4):
        for j in range(2):
            for m in range(4):
                pair = q_ref[pl.ds(s * 128 + j * 64, 64), pl.ds(m * 128, 128)].astype(F32)
                qt[s, j, pl.ds(m * 128, 64)] = head_tile(pair, False, False).astype(BF)
                qt[s, j, pl.ds(m * 128 + 64, 64)] = head_tile(pair, True, False).astype(BF)
    run_all(keys)

    def poll(count):
        for _ in range(count):
            next(weights, None)
        next(rest, None)

    lanes = lax.broadcasted_iota(jnp.int32, (512, 256), 1)
    wide = lax.broadcasted_iota(jnp.int32, (256, 128), 1) < 64

    def tile(queries, keys_values, limit=None):
        e = jnp.exp(dot_nt(queries, keys_values))
        if limit is not None:
            e = jnp.where(lanes < limit, e, 0.0)
        ones_values = jnp.where(wide, jnp.ones_like(keys_values), keys_values)
        return dot_nn(e.astype(BF), ones_values)

    for s in range(4):

        def order(t, carry, s=s):
            for r in range(4):
                at = s * 64 + t * 4 + r
                nat_ref[s, t, pl.ds(r * 64, 64)] = kvg[home_ref[0, at], home_ref[1, at]]
            return carry

        lax.fori_loop(0, 16, order, 0)
        acc[...] = jnp.zeros_like(acc)

        def body(i, carry, s=s):
            which = pick_ref[0, s * 9 + i]
            high_part = tile(qt[s, 1], nat_ref[s, i])
            picked = tile(qt[s, which], nat_ref[s, pick_ref[1, s * 9 + i]], pick_ref[2, s * 9 + i])
            to_low = jnp.broadcast_to(which, picked.shape) == 0
            acc[0] += jnp.where(to_low, picked, 0.0)
            acc[1] += high_part + jnp.where(to_low, 0.0, picked)
            return carry

        lax.fori_loop(0, 4, body, 0)
        poll(2)
        lax.fori_loop(4, 8, body, 0)
        acc[1] += tile(qt[s, 1], nat_ref[s, pick_ref[1, s * 9 + 8]], pick_ref[2, s * 9 + 8])
        for j in range(2):
            for m2 in range(4):
                even = acc[j, pl.ds(m2 * 128, 64)]
                odd = acc[j, pl.ds(m2 * 128 + 64, 64)]
                up = upper_lanes(even.shape)
                bottom = jnp.where(up, pltpu.roll(odd, 64, 1), even)
                top = jnp.where(up, odd, pltpu.roll(even, 64, 1))
                inverse = 1.0 / bottom
                rows, cols = pl.ds(s * 128 + j * 64, 64), pl.ds(m2 * 128, 128)
                inv_ref[rows, cols] = inverse
                o_ref[rows, cols] = top * inverse
        poll(2)
    run_all(weights, rest)


def attend_call(pick, home, q, kv, w, t):
    return pl.pallas_call(
        attend_kernel,
        out_shape=(
            sds((512, 512), F32),
            sds((512, 512), F32),
            sds((4, 16, 256, 128), BF),
            sds((32,) + w.shape, BF),
            sds((4,) + t.shape, BF),
        ),
        in_specs=[spec(SM), spec(SM), spec(VM), spec(VM), spec(HB), spec(VM)],
        out_specs=(spec(VM), spec(VM), spec(VM), spec(HB), spec(VM)),
        scratch_shapes=[
            vm((32, 8, 64, 128), BF), vm((4, 2, 512, 128), BF), vm((2, 512, 128), F32),
            dma(AG_SEMS), dma(AG_SEMS), ONE, dma(AG_SEMS), dma(AG_SEMS), ONE, dma(3 * CHUNKS), dma(3 * CHUNKS),
        ],
        compiler_params=params(1),
        name="attend_forward",
    )(pick, home, q, kv, w, t)


def scale_of(v):
    return lax.rsqrt(jnp.mean(v * v, -1, keepdims=True) + NORM_EPS)


def middle_kernel(
    off_ref, part_ref, x_ref, gain_ref, w_ref, mid_ref, all_ref, full_ref,
    b0, b1, sb, b2, tb, gs, gr, gl, fs, fr, ss, sr,
):
    pc = Place()
    greet(pc)
    share = Share(pc, all_ref, ss, sr, 0, CHUNKS)

    def each(k, total):
        rows = pl.ds(k * 32, 32)
        mid = x_ref[rows].astype(F32) + turn(total, off_ref, 0, tb)
        mid_ref[rows] = mid
        normed = mid * scale_of(mid) * gain_ref[...]
        all_ref[pc.w, rows] = turn(normed, off_ref, 1, tb).astype(BF)
        share.send(k)

    fold = fold_steps(pc, part_ref, b0, b1, sb, b2, fs, fr, 0, CHUNKS, each)
    weights = gather_steps(pc, w_ref, full_ref, gs, gr, gl)
    next(fold)
    next(weights)
    next(fold)
    next(weights)
    run_all(fold, weights, share.finish_steps())


def fold_scratch():
    return [vm((128, 2048), BF) for _ in range(4)] + [vm((2, 16, 32, 128), F32)]


def middle_call(off, part, x, gain, w):
    return pl.pallas_call(
        middle_kernel,
        out_shape=(sds((128, 2048), F32), sds((4, 128, 2048), BF), sds((32,) + w.shape, BF)),
        in_specs=[spec(SM), spec(VM), spec(VM), spec(VM), spec(HB)],
        out_specs=(spec(VM), spec(VM), spec(HB)),
        scratch_shapes=fold_scratch() + [dma(AG_SEMS), dma(AG_SEMS), ONE] + [dma(3 * CHUNKS)] * 4,
        compiler_params=params(2),
        name="middle_rows",
    )(off, part, x, gain, w)


def back_kernel(
    off_ref, part_ref, mid_ref, up_ref, gain_ref, g_ref, dmid_ref, all_ref, own_ref,
    b0, b1, sb, b2, tb, part, buf, gs, gr, gl, fs, fr, ss, sr,
):
    pc = Place()
    load = pltpu.make_async_copy(g_ref, part, gl)
    load.start()
    greet(pc)
    share = Share(pc, all_ref, ss, sr, 0, CHUNKS)

    def each(k, total):
        rows = pl.ds(k * 32, 32)
        mid = mid_ref[rows]
        weighted = turn(total, off_ref, 0, tb) * gain_ref[...]
        r = scale_of(mid)
        mean = jnp.mean(weighted * mid, -1, keepdims=True)
        dmid = up_ref[rows].astype(F32) + r * weighted - mid * (r * r * r) * mean
        dmid_ref[rows] = dmid
        all_ref[pc.w, rows] = turn(dmid, off_ref, 1, tb).astype(BF)
        share.send(k)

    def finish(own, other):
        own_ref[...] = own[...].astype(F32) + other[...].astype(F32)

    fold = fold_steps(pc, part_ref, b0, b1, sb, b2, fs, fr, 0, CHUNKS, each)
    next(fold)
    load.wait()
    grads = scatter_steps(pc, part, buf, gs, gr, finish)
    next(grads)
    next(fold)
    run_all(fold, grads, share.finish_steps())


def back_call(off, part, mid, up, gain, g):
    return pl.pallas_call(
        back_kernel,
        out_shape=(sds((128, 2048), F32), sds((4, 128, 2048), BF), sds(g.shape[1:], F32)),
        in_specs=[spec(SM), spec(VM), spec(VM), spec(VM), spec(VM), spec(HB)],
        out_specs=(spec(VM), spec(VM), spec(VM)),
        scratch_shapes=fold_scratch()
        + [vm(g.shape, BF), vm((31 * g.shape[1], g.shape[2]), BF), dma(RS_SEMS), dma(RS_SEMS), ONE]
        + [dma(3 * CHUNKS)] * 4,
        compiler_params=params(3),
        name="middle_back",
    )(off, part, mid, up, gain, g)


def attend_back_kernel(
    pick_ref, pair_ref, q_ref, do_ref, o_ref, inv_ref, nat_ref, gp_ref, gi_ref, down_ref,
    dq_ref, dkv_ref, own_ref, sum_ref,
    part, buf, pkv, bkv, qt, gt, dl, dnat, dqa, b0, b1, sb, b2,
    gs, gr, gl, ks, kr, fs, fr,
):
    pc = Place()
    cut = gp_ref.shape[2]
    loads = [
        pltpu.make_async_copy(gp_ref, part.at[:, :, pl.ds(0, cut)], gl.at[0]),
        pltpu.make_async_copy(gi_ref, part.at[:, :, pl.ds(cut, gi_ref.shape[2])], gl.at[1]),
    ]
    for load in loads:
        load.start()
    greet(pc)

    def finish(own, other):
        own_ref[...] = own[...].astype(F32) + other[...].astype(F32)

    def finish_kv(own, other):
        dkv_ref[...] = own[...].astype(F32) + other[...].astype(F32)

    def each(k, total):
        sum_ref[pl.ds(k * 32, 32)] = total

    fold = fold_steps(pc, down_ref, b0, b1, sb, b2, fs, fr, 0, CHUNKS, each)
    next(fold)
    for load in loads:
        load.wait()
    grads = scatter_steps(pc, part, buf, gs, gr, finish)
    next(grads)

    def poll(count):
        for _ in range(count):
            next(grads, None)
        next(fold, None)

    rows_iota = lax.broadcasted_iota(jnp.int32, (256, 512), 0)
    ones = jnp.ones((8, 128), BF)

    def tile(j, keys_values, limit=None):
        queries, upward = qt[j], gt[j]
        e = jnp.exp(dot_nt(keys_values, queries))
        if limit is not None:
            e = jnp.where(rows_iota < limit, e, 0.0)
        ds = (e * (dot_nt(keys_values, upward) - dl[j, 0:1])).astype(BF)
        dkv = dot_nn(ds, queries) + dot_nn(e.astype(BF), upward)
        return dot_tn(ds, keys_values), dkv

    for s in range(4):
        for j in range(2):
            sums = []
            for m2 in range(4):
                rows, cols = pl.ds(s * 128 + j * 64, 64), pl.ds(m2 * 128, 128)
                pair = q_ref[rows, cols].astype(F32)
                ratio = do_ref[rows, cols] * inv_ref[rows, cols]
                prod = ratio * o_ref[rows, cols]
                for odd in (False, True):
                    place = pl.ds(m2 * 128 + (64 if odd else 0), 64)
                    qt[j, place] = head_tile(pair, odd, False).astype(BF)
                    gt[j, place] = head_tile(ratio, odd, True).astype(BF)
                    sums.append(head_tile(prod, odd, False))
            whole = jnp.concatenate(sums, 0)
            big = whole.astype(BF)
            rest = (whole - big.astype(F32)).astype(BF)
            dl[j] = dot_nt(ones, big) + dot_nt(ones, rest)
        dqa[...] = jnp.zeros_like(dqa)

        def body(i, carry, s=s):
            which = pick_ref[0, s * 9 + i]
            dq1, dkv1 = tile(1, nat_ref[s, i])
            dq2, dkv2 = tile(which, nat_ref[s, pick_ref[1, s * 9 + i]], pick_ref[2, s * 9 + i])
            to_low = jnp.broadcast_to(which, dq2.shape) == 0
            dqa[0] += jnp.where(to_low, dq2, 0.0)
            dqa[1] += dq1 + jnp.where(to_low, 0.0, dq2)
            to_low = jnp.broadcast_to(which, dkv2.shape) == 0
            dnat[i] = (dkv1 + jnp.where(to_low, dkv2, 0.0)).reshape(4, 64, 128)
            dnat[15 - i] = jnp.where(to_low, 0.0, dkv2).reshape(4, 64, 128)
            return carry

        lax.fori_loop(0, 4, body, 0)
        poll(2)
        lax.fori_loop(4, 8, body, 0)
        kt = pick_ref[1, s * 9 + 8]
        dq3, dkv3 = tile(1, nat_ref[s, kt], pick_ref[2, s * 9 + 8])
        dqa[1] += dq3
        for t in range(8, 16):
            here = jnp.broadcast_to(kt, dkv3.shape) == t
            dnat[t] += jnp.where(here, dkv3, 0.0).reshape(4, 64, 128)
        for j in range(2):
            for m2 in range(4):
                even = dqa[j, pl.ds(m2 * 128, 64)]
                odd = dqa[j, pl.ds(m2 * 128 + 64, 64)]
                both = jnp.where(upper_lanes(even.shape), pltpu.roll(odd, 64, 1), even)
                dq_ref[pl.ds(s * 128 + j * 64, 64), pl.ds(m2 * 128, 128)] = both * 0.125

        def order(c, carry, s=s):
            for j in range(2):
                at = s * 64 + c * 2 + j
                pkv[c, s * 2 + j] = dnat[pair_ref[0, at], pair_ref[1, at]].astype(BF)
            return carry

        lax.fori_loop(0, 32, order, 0)
        poll(2)
    run_all(scatter_steps(pc, pkv, bkv, ks, kr, finish_kv), grads, fold)


def attend_back_call(pick, pairs, q, do, o, inv, nat, gp, gi, down):
    cols = gp.shape[2] + gi.shape[2]
    return pl.pallas_call(
        attend_back_kernel,
        out_shape=(sds((512, 512), F32), sds((8, 64, 128), F32), sds((64, cols), F32), sds((128, 2048), F32)),
        in_specs=[spec(SM), spec(SM)] + [spec(VM)] * 5 + [spec(HB)] * 2 + [spec(VM)],
        out_specs=(spec(VM),) * 4,
        scratch_shapes=[
            vm((32, 64, cols), BF), vm((31 * 64, cols), BF), vm((32, 8, 64, 128), BF), vm((31 * 8, 64, 128), BF),
            vm((2, 512, 128), BF), vm((2, 512, 128), BF), vm((2, 8, 512), F32), vm((16, 4, 64, 128), F32),
            vm((2, 512, 128), F32)] + [vm((128, 2048), BF) for _ in range(4)]
        + [dma(RS_SEMS), dma(RS_SEMS), dma(2), dma(RS_SEMS), dma(RS_SEMS), dma(3 * CHUNKS), dma(3 * CHUNKS)],
        compiler_params=params(4),
        name="attend_backward",
    )(pick, pairs, q, do, o, inv, nat, gp, gi, down)


def close_kernel(
    part_ref, g_ref, w_ref, v_ref, sum_ref, own_ref, gain_ref,
    b0, b1, sb, b2, part, buf, vb, gs, gr, gl, fs, fr, vs, vr, hs, hr,
):
    pc = Place()
    load = pltpu.make_async_copy(g_ref, part, gl)
    load.start()
    greet(pc)
    wire = Wire(vs, vr)

    def each(k, total):
        sum_ref[pl.ds(k * 32, 32)] = total

    def finish(own, other):
        total = own[...].astype(F32) + other[...].astype(F32)
        own_ref[...] = total
        first = jnp.sum(total * w_ref[...].astype(F32), -1, keepdims=True)
        vb[0] = jnp.where(lax.broadcasted_iota(jnp.int32, (64, 128), 1) == 0, first, v_ref[...])
        wire.send(0, vb.at[0], vb.at[1], pc.twin())
        wire.arrive(0, vb.at[1], pc.twin())
        vb[2] = vb[0] + vb[1]
        wire.send(1, vb.at[2], vb.at[3], pc.over())
        wire.arrive(1, vb.at[3], pc.over())
        vb[4] = vb[2] + vb[3]

    fold = fold_steps(pc, part_ref, b0, b1, sb, b2, fs, fr, 0, CHUNKS, each)
    next(fold)
    load.wait()
    grads = scatter_steps(pc, part, buf, gs, gr, finish)
    next(grads)
    next(fold)
    run_all(grads, fold)
    run_all(gather_steps(pc, vb.at[4], gain_ref, hs, hr, gl))
    wire.drain()


def close_call(part, g, w, v):
    return pl.pallas_call(
        close_kernel,
        out_shape=(sds((128, 2048), F32), sds(g.shape[1:], F32), sds((32, 64, 128), F32)),
        in_specs=[spec(VM), spec(HB), spec(VM), spec(VM)],
        out_specs=(spec(VM), spec(VM), spec(VM)),
        scratch_shapes=[vm((128, 2048), BF) for _ in range(4)]
        + [vm(g.shape, BF), vm((31 * g.shape[1], g.shape[2]), BF), vm((5, 64, 128), F32)]
        + [dma(RS_SEMS), dma(RS_SEMS), ONE, dma(3 * CHUNKS), dma(3 * CHUNKS), dma(2), dma(2), dma(AG_SEMS), dma(AG_SEMS)],
        compiler_params=params(5),
        name="close_sums",
    )(part, g, w, v)


def rope_tables(positions):
    half_width = HD // 2
    inverse = ROPE_BASE ** (-(jnp.arange(half_width, dtype=F32) * 2.0 / HD))
    angles = positions.astype(F32)[..., None] * inverse
    angles = jnp.concatenate([angles, angles], -1)
    return (jnp.cos(angles), jnp.sin(angles))


def rotate(vectors, cosine_table, sine_table):
    half_width = vectors.shape[-1] // 2
    turned = jnp.concatenate([-vectors[..., half_width:], vectors[..., :half_width]], -1)
    return vectors * cosine_table + turned * sine_table


def unrotate(gradient, cosine_table, sine_table):
    half_width = gradient.shape[-1] // 2
    scaled = gradient * sine_table
    turned = jnp.concatenate([scaled[..., half_width:], -scaled[..., :half_width]], -1)
    return gradient * cosine_table + turned


def adamw_step(master, first_state, second_state, gradient, rate_value):
    first_new = BETA_FIRST * first_state + (1.0 - BETA_FIRST) * gradient
    second_new = BETA_SECOND * second_state + (1.0 - BETA_SECOND) * gradient * gradient
    first_fix = 1.0 - BETA_FIRST**STEP
    second_fix = 1.0 - BETA_SECOND**STEP
    update = first_new / first_fix / (jnp.sqrt(second_new / second_fix) + ADAM_EPS)
    return (master - rate_value * (update + WEIGHT_DECAY * master), first_new, second_new)


def matmul(a, b, dims, out):
    return lax.dot_general(a, b, (dims, ((), ())), preferred_element_type=F32).astype(out)


def per_device(
    tokens, cotangent, block_pairs, offsets,
    qkv_master, qkv_first, qkv_second,
    proj_master, proj_first, proj_second,
    inner_master, inner_first, inner_second,
    down_master, down_first, down_second,
    gains, gain_first, gain_second,
):
    offsets = offsets.astype(jnp.int32)
    shift = offsets * 64
    g1, g2 = gains[:, 0][None], gains[:, 1][None]
    qkv_piece = qkv_master[:, 0].astype(BF)
    inner_piece = inner_master.reshape(64, 2816).astype(BF)
    mid_piece = jnp.concatenate([proj_master.astype(BF).T, inner_piece], 1)
    down_piece = down_master.astype(BF).T

    x = tokens[0].astype(F32)
    r1 = scale_of(x)
    normed = jnp.roll((x * r1 * g1).astype(BF), -shift[0], axis=1)
    tail = jnp.roll(cotangent[0], -shift[3], axis=1)
    a_all, qkv_full = open_call(normed, qkv_piece)
    a_all = a_all.reshape(512, D)
    qkv_full = qkv_full.reshape(D, 640)

    projected = matmul(a_all, qkv_full, ((1,), (0,)), F32)
    own_pairs = lax.dynamic_index_in_dim(block_pairs, lax.axis_index("ctx"), 1, keepdims=False)
    positions = (own_pairs[:, :, None] * BLK + jnp.arange(BLK, dtype=jnp.int32)).reshape(512)
    cosine, sine = rope_tables(positions)
    heads = projected[:, :576].reshape(512, 9, HD)
    turned = rotate(heads, cosine[:, None], sine[:, None]).astype(BF).reshape(512, 576)
    q = turned[:, :512] * jnp.asarray(0.125, BF)
    kv = jnp.concatenate([turned[:, 512:], projected[:, 576:].astype(BF)], 1)
    flat = block_pairs.reshape(4, 64)
    slots = jnp.arange(64, dtype=jnp.int32)
    blocks = jnp.arange(64, dtype=jnp.int32)
    slot = jnp.sum(jnp.where(flat[:, :, None] == blocks, slots[None, :, None], 0), 1)
    home = jnp.stack([slot // 2, slot % 2 + 2 * jnp.arange(4, dtype=jnp.int32)[:, None]]).reshape(2, 256)
    pairs = jnp.stack([flat // 4, flat % 4]).reshape(2, 256)
    low = own_pairs[:, :1]
    m = low // 4
    i = jnp.arange(9, dtype=jnp.int32)[None]
    is_low = (i <= m) & (i < 8)
    pick = jnp.stack(
        [
            jnp.where(is_low, 0, 1),
            jnp.where(is_low, i, jnp.where(i == 8, 15 - m, 15 - i)),
            jnp.where(i == 8, (63 - low - 4 * (15 - m) + 1) * 64, jnp.where(i == m, (low - 4 * m + 1) * 64, 256)),
        ]
    ).reshape(3, 36)
    o, inverse, nat, mid_full, tail_all = attend_call(pick, home, q, kv.reshape(8, 64, 128), mid_piece, tail)
    mid_full = mid_full.reshape(D, 3328)
    proj_full, inner_full = mid_full[:, :512], mid_full[:, 512:]
    tail_all = tail_all.reshape(512, D)

    ob = o.astype(BF)
    attended = matmul(ob, proj_full, ((1,), (1,)), BF).reshape(4, 128, D)
    middle, hb, down_full = middle_call(turn_table([offsets[1], 32 - offsets[2]]), attended, tokens[0], g2, down_piece)
    hb = hb.reshape(512, D)
    down_full = down_full.reshape(D, 1408)

    gate_up = matmul(hb, inner_full, ((1,), (0,)), F32)
    gate, up = gate_up[:, :1408], gate_up[:, 1408:]
    sg = jax.nn.sigmoid(gate)
    act = (gate * sg * up).astype(BF)
    dact = matmul(tail_all, down_full, ((1,), (0,)), F32)
    dgate = dact * up * sg * (1.0 + gate * (1.0 - sg))
    dup = dact * gate * sg
    du = jnp.concatenate([dgate, dup], 1).astype(BF)
    dh = matmul(du, inner_full, ((1,), (1,)), BF).reshape(4, 128, D)
    down_grad = matmul(tail_all, act, ((0,), (0,)), BF).reshape(32, 64, 1408)
    out_part = matmul(act, down_full, ((1,), (1,)), BF).reshape(4, 128, D)
    inner_grad = matmul(hb, du, ((0,), (0,)), BF).reshape(32, 64, 2816)
    dmid, ga, down_sum = back_call(turn_table([offsets[2], 32 - offsets[1]]), dh, middle, cotangent[0], g2, down_grad)
    ga = ga.reshape(512, D)

    do = matmul(ga, proj_full, ((1,), (0,)), F32)
    proj_grad = matmul(ga, ob, ((0,), (0,)), BF).reshape(32, 64, 512)
    dq, dkv, mid_sum, out_sum = attend_back_call(
        pick, pairs, q, do, o, inverse, nat, proj_grad, inner_grad, out_part
    )
    output = middle + jnp.roll(out_sum, shift[3], axis=1)

    dkv = dkv.reshape(512, 128)
    dk = jnp.concatenate([dq, dkv[:, :64]], 1).reshape(512, 9, HD)
    dk = unrotate(dk, cosine[:, None], sine[:, None]).reshape(512, 576)
    dp = jnp.concatenate([dk, dkv[:, 64:]], 1).astype(BF)
    da = matmul(dp, qkv_full, ((1,), (1,)), BF).reshape(4, 128, D)
    qkv_grad = matmul(a_all, dp, ((0,), (0,)), BF).reshape(32, 64, 640)
    proj_sum, inner_sum = mid_sum[:, :512].T, mid_sum[:, 512:]
    second = jnp.sum(inner_sum * inner_piece.astype(F32), -1, keepdims=True)
    da, qkv_sum, gain_sums = close_call(da, qkv_grad, qkv_piece, jnp.broadcast_to(second, (64, 128)))
    da = jnp.roll(da, shift[0], axis=1)
    weighted = da * g1
    input_grad = dmid + r1 * weighted - x * r1**3 * jnp.mean(weighted * x, -1, keepdims=True)
    gain_sums = gain_sums.reshape(D, 128)
    gain_grad = (
        jnp.stack([jnp.roll(gain_sums[:, 0], shift[0]), jnp.roll(gain_sums[:, 1], shift[2])], 1) / gains
    )

    rate_rows = 2.0 / math.sqrt(D)
    rate_proj = 1.0
    rate_down = 2.0 / math.sqrt(FF)
    qkv_out = adamw_step(qkv_master, qkv_first, qkv_second, qkv_sum[:, None], rate_rows)
    proj_out = adamw_step(proj_master, proj_first, proj_second, proj_sum, rate_proj)
    inner_out = adamw_step(inner_master, inner_first, inner_second, inner_sum.reshape(64, 2, 1408), rate_rows)
    down_out = adamw_step(down_master, down_first, down_second, down_sum.T, rate_down)
    gain_out = adamw_step(gains, gain_first, gain_second, gain_grad, GAIN_RATE)
    return (output[None], input_grad[None], *qkv_out, *proj_out, *inner_out, *down_out, *gain_out)


def solution(mesh):
    rows, every = P("wsh", "ctx", None), P()
    qkv, inner, cols = P("ctx", "wsh", None), P("ctx", None, "wsh"), P("wsh", "ctx")
    return jax.shard_map(
        per_device,
        mesh=mesh,
        in_specs=(rows, rows, every, every) + (qkv,) * 3 + (cols,) * 3 + (inner,) * 3 + (cols,) * 3 + (every,) * 3,
        out_specs=(rows, rows) + (qkv,) * 3 + (cols,) * 3 + (inner,) * 3 + (cols,) * 3 + (every,) * 3,
        check_vma=False,
    )
```

```python
import math

import jax
import jax.numpy as jnp
from jax import lax
from jax.experimental import pallas as pl
from jax.experimental.pallas import tpu as pltpu
from jax.sharding import PartitionSpec as P
MESH = pl.DeviceIdType.MESH
F32, BF = jnp.float32, jnp.bfloat16
VM, HB, SM = pltpu.VMEM, pl.ANY, pltpu.SMEM

D = 2048
HD = 64
FF = 5632
BLK = 64
STEP = 7
NORM_EPS = 1e-05
ROPE_BASE = 10000.0
BETA_FIRST = 0.5
BETA_SECOND = 0.5
ADAM_EPS = 1e-08
WEIGHT_DECAY = 0.1
GAIN_RATE = 0.4

AG_SEMS = 81
RS_SEMS = 81


class Place:
    def __init__(self):
        c = lax.axis_index("ctx")
        w = lax.axis_index("wsh")
        self.c, self.w = c, w
        self.yl, self.yh, self.co = c // 16, w // 2, w % 2
        x, z = (c // 4) % 4, c % 4
        self.y16 = [self.yl * 16, 16 - self.yl * 16]
        self.x4 = {k: ((x + k + 4) % 4) * 4 for k in (-2, -1, 0, 1, 2)}
        self.z1 = {k: (z + k + 4) % 4 for k in (-2, -1, 0, 1, 2)}
        self.far = (1 - self.yh) * 2 + self.co
        self.near_twin = self.yh * 2 + 1 - self.co
        self.far_twin = (1 - self.yh) * 2 + 1 - self.co

    def step(self, axis, k):
        if axis == "x":
            return (self.y16[0] + self.x4[k] + self.z1[0], self.w)
        return (self.y16[0] + self.x4[0] + self.z1[k], self.w)

    def mate(self):
        return (self.y16[1] + self.x4[0] + self.z1[0], self.w)

    def over(self):
        return (self.c, self.far)

    def twin(self):
        return (self.c, self.near_twin)

    def piece(self, half, v, dp, dq):
        if half == 0:
            return self.y16[v] + self.x4[dp] + self.z1[dq]
        return self.y16[v] + self.x4[dq] + self.z1[dp]


def ctx_peers(place):
    return [place.step("x", 1), place.step("x", -1), place.step("z", 1), place.step("z", -1), place.mate()]


def greet(place):
    bar = pltpu.get_barrier_semaphore()
    peers = ctx_peers(place) + [place.over(), place.twin()]
    for peer in peers:
        pl.semaphore_signal(bar, inc=1, device_id=peer, device_id_type=MESH)
    pl.semaphore_wait(bar, len(peers))


class Wire:
    def __init__(self, ssem, rsem):
        self.ssem, self.rsem, self.sent = ssem, rsem, []

    def send(self, k, src, dst, to):
        cp = pltpu.make_async_remote_copy(src, dst, self.ssem.at[k], self.rsem.at[k], device_id=to, device_id_type=MESH)
        cp.start()
        self.sent.append(cp)

    def arrive(self, k, view, frm):
        pltpu.make_async_remote_copy(view, view, self.ssem.at[k], self.rsem.at[k], device_id=frm, device_id_type=MESH).wait_recv()

    def drain(self):
        for cp in self.sent:
            cp.wait_send()
        self.sent = []


AXES = (("x", "z"), ("z", "x"))
GROUPS = (0, -1, 1, 2)


def gather_steps(pc, src, dst, ssem, rsem, lsem, late=False):
    wire = Wire(ssem, rsem)
    R = src.shape[0]
    H, S = R // 2, R // 4

    def part(v, h, dp, dq, lo=0, n=None):
        return dst.at[pc.piece(h, v, dp, dq), pl.ds(h * H + lo, H if n is None else n)]

    def key(v, h, k):
        return (v * 2 + h) * 20 + k

    local = pltpu.make_async_copy(src, dst.at[pc.c], lsem)
    local.start()
    both = (0,) if late else (0, 1)

    def cross(h, gi, d):
        if late:
            k = 40 + (h * 4 + gi) * 4 + (0, 2, 1, 3)[d + 1]
            view = part(0, h, GROUPS[gi], d)
            if gi == 0 and d == 0:
                wire.send(k, src.at[pl.ds(h * H, H)], view, pc.mate())
            else:
                wire.send(k, view, view, pc.mate())

    if not late:
        wire.send(80, src, dst.at[pc.c], pc.mate())

    def first(v, h):
        A, B = AXES[h]
        view = src.at[pl.ds(h * H, H)] if v == 0 else part(v, h, 0, 0)
        there = part(v, h, 0, 0)
        wire.send(key(v, h, 0), view, there, pc.step(A, 1))
        wire.send(key(v, h, 1), view, there, pc.step(A, -1))
        wire.send(key(v, h, 4), view, there, pc.step(B, 1))
        wire.send(key(v, h, 5), view, there, pc.step(B, -1))

    def along(v, h, gi):
        A, B = AXES[h]
        view = part(v, h, GROUPS[gi], 0)
        wire.send(key(v, h, 4 + 4 * gi), view, view, pc.step(B, 1))
        wire.send(key(v, h, 5 + 4 * gi), view, view, pc.step(B, -1))

    def spread1(v, h):
        A, B = AXES[h]
        wire.arrive(key(v, h, 0), part(v, h, -1, 0), pc.step(A, -1))
        s = part(v, h, -1, 0, 0, S)
        wire.send(key(v, h, 2), s, s, pc.step(A, 1))
        along(v, h, 1)
        wire.arrive(key(v, h, 1), part(v, h, 1, 0), pc.step(A, 1))
        s = part(v, h, 1, 0, S, S)
        wire.send(key(v, h, 3), s, s, pc.step(A, -1))
        along(v, h, 2)

    def spread2(v, h):
        A, B = AXES[h]
        wire.arrive(key(v, h, 2), part(v, h, 2, 0, 0, S), pc.step(A, -1))
        wire.arrive(key(v, h, 3), part(v, h, 2, 0, S, S), pc.step(A, 1))
        along(v, h, 3)

    def pass_on(v, h, gi):
        A, B = AXES[h]
        g = GROUPS[gi]
        k = 4 + 4 * gi
        wire.arrive(key(v, h, k), part(v, h, g, -1), pc.step(B, -1))
        s = part(v, h, g, -1, 0, S)
        wire.send(key(v, h, k + 2), s, s, pc.step(B, 1))
        wire.arrive(key(v, h, k + 1), part(v, h, g, 1), pc.step(B, 1))
        s = part(v, h, g, 1, S, S)
        wire.send(key(v, h, k + 3), s, s, pc.step(B, -1))

    for h in (0, 1):
        first(0, h)
        cross(h, 0, 0)
    yield
    if not late:
        wire.arrive(80, dst.at[pc.piece(0, 1, 0, 0)], pc.mate())
        for h in (0, 1):
            first(1, h)
        yield
    for v in both:
        for h in (0, 1):
            spread1(v, h)
            cross(h, 1, 0)
            cross(h, 2, 0)
        yield
    for v in both:
        for h in (0, 1):
            spread2(v, h)
            cross(h, 3, 0)
        yield
    for gi in range(4):
        for v in both:
            for h in (0, 1):
                pass_on(v, h, gi)
                cross(h, gi, -1)
                cross(h, gi, 1)
            yield
    for gi in range(4):
        for v in both:
            for h in (0, 1):
                A, B = AXES[h]
                k = 4 + 4 * gi
                wire.arrive(key(v, h, k + 2), part(v, h, GROUPS[gi], 2, 0, S), pc.step(B, -1))
                wire.arrive(key(v, h, k + 3), part(v, h, GROUPS[gi], 2, S, S), pc.step(B, 1))
                cross(h, gi, 2)
        yield
    if late:
        for gi in range(4):
            for h in (0, 1):
                for d in (-1, 0, 1, 2):
                    k = 40 + (h * 4 + gi) * 4 + (0, 2, 1, 3)[d + 1]
                    wire.arrive(k, part(1, h, GROUPS[gi], d), pc.mate())
            yield
    wire.drain()
    local.wait()


def scatter_steps(pc, part, buf, ssem, rsem, finish):
    wire = Wire(ssem, rsem)
    R = part.shape[1]
    H, S = R // 2, R // 4

    def key(v, h, k):
        return (v * 2 + h) * 20 + k

    def box(v, h, gi, which):
        base = ((v * 2 + h) * 5 + gi) * (R + H)
        off, n = ((0, S), (S, S), (2 * S, H), (2 * S + H, H))[which]
        return buf.at[pl.ds(base + off, n)]

    def mine(v, h, dp, dq, lo=0, n=None):
        return part.at[pc.piece(h, v, dp, dq), pl.ds(h * H + lo, H if n is None else n)]

    def add(to, *more):
        total = to[...].astype(F32)
        for m in more:
            total = total + m[...].astype(F32)
        to[...] = total.astype(BF)

    def where(stage, gi, d):
        return (GROUPS[gi], d) if stage == 1 else (d, 0)

    def ring_axis(stage, h):
        return AXES[h][1] if stage == 1 else AXES[h][0]

    def raw(v, h, gi, stage):
        X = ring_axis(stage, h)
        k = 4 * gi
        wire.send(key(v, h, k), mine(v, h, *where(stage, gi, -2), 0, S), box(v, h, gi, 0), pc.step(X, -1))
        wire.send(key(v, h, k + 1), mine(v, h, *where(stage, gi, 2), S, S), box(v, h, gi, 1), pc.step(X, 1))

    def mid(v, h, gi, stage):
        X = ring_axis(stage, h)
        k = 4 * gi
        wire.arrive(key(v, h, k), box(v, h, gi, 0), pc.step(X, 1))
        add(mine(v, h, *where(stage, gi, -1), 0, S), box(v, h, gi, 0))
        wire.send(key(v, h, k + 2), mine(v, h, *where(stage, gi, -1)), box(v, h, gi, 2), pc.step(X, -1))
        wire.arrive(key(v, h, k + 1), box(v, h, gi, 1), pc.step(X, -1))
        add(mine(v, h, *where(stage, gi, 1), S, S), box(v, h, gi, 1))
        wire.send(key(v, h, k + 3), mine(v, h, *where(stage, gi, 1)), box(v, h, gi, 3), pc.step(X, 1))

    def end(v, h, gi, stage):
        X = ring_axis(stage, h)
        k = 4 * gi
        wire.arrive(key(v, h, k + 2), box(v, h, gi, 2), pc.step(X, 1))
        wire.arrive(key(v, h, k + 3), box(v, h, gi, 3), pc.step(X, -1))
        add(mine(v, h, *where(stage, gi, 0)), box(v, h, gi, 2), box(v, h, gi, 3))

    order = (3, 1, 2, 0)
    for gi in order:
        for v in (1, 0):
            for h in (0, 1):
                raw(v, h, gi, 1)
    yield
    for gi in order:
        for v in (1, 0):
            for h in (0, 1):
                mid(v, h, gi, 1)
            yield
    for v in (1, 0):
        for gi in order:
            for h in (0, 1):
                end(v, h, gi, 1)
            if gi == 3:
                for h in (0, 1):
                    raw(v, h, 4, 2)
            yield
        if v == 1:
            for h in (0, 1):
                mid(1, h, 4, 2)
            yield
    for h in (0, 1):
        end(1, h, 4, 2)
    theirs = part.at[pc.piece(0, 1, 0, 0)]
    tail = buf.at[pl.ds(30 * R, R)]
    wire.send(80, theirs, tail, pc.mate())
    yield
    for h in (0, 1):
        mid(0, h, 4, 2)
    yield
    for h in (0, 1):
        end(0, h, 4, 2)
    yield
    wire.arrive(80, tail, pc.mate())
    finish(part.at[pc.c], tail)
    wire.drain()


def in_turn(*gens, lead=3):
    live, waiting = [gens[0]], list(gens[1:])
    count = 0
    while live:
        for g in list(live):
            try:
                next(g)
                yield
            except StopIteration:
                live.remove(g)
        count += 1
        if waiting and (count % lead == 0 or not live):
            live.append(waiting.pop(0))


def run_all(*gens):
    live = list(gens)
    while live:
        for g in list(live):
            try:
                next(g)
            except StopIteration:
                live.remove(g)


class Fold:
    def __init__(self, pc, part, boxes, ssem, rsem, chunks):
        self.wire = Wire(ssem, rsem)
        self.pc, self.part, self.chunks = pc, part, chunks
        self.b0, self.b1, self.sb, self.b2 = boxes
        n = part.shape[1] // chunks
        self.rows = [pl.ds(k * n, n) for k in range(chunks)]

    def far_twin(self):
        for k, r in enumerate(self.rows):
            self.wire.send(k, self.part.at[self.pc.far_twin, r], self.b0.at[r], self.pc.twin())

    def near_twin(self):
        for k, r in enumerate(self.rows):
            self.wire.send(self.chunks + k, self.part.at[self.pc.near_twin, r], self.b1.at[r], self.pc.twin())

    def far(self):
        for k, r in enumerate(self.rows):
            self.wire.arrive(k, self.b0.at[r], self.pc.twin())
            self.sb[r] = (self.part[self.pc.far, r].astype(F32) + self.b0[r].astype(F32)).astype(BF)
            self.wire.send(2 * self.chunks + k, self.sb.at[r], self.b2.at[r], self.pc.over())

    def total(self, k):
        r = self.rows[k]
        self.wire.arrive(self.chunks + k, self.b1.at[r], self.pc.twin())
        near = self.part[self.pc.w, r].astype(F32) + self.b1[r].astype(F32)
        self.wire.arrive(2 * self.chunks + k, self.b2.at[r], self.pc.over())
        return near + self.b2[r].astype(F32)

    def steps(self, each):
        self.far_twin()
        self.near_twin()
        yield
        self.far()
        yield
        for k in range(self.chunks):
            each(k, self.total(k))
            yield
        self.wire.drain()


class Share:
    def __init__(self, pc, dst, ssem, rsem, base, chunks):
        self.wire = Wire(ssem, rsem)
        self.pc, self.dst, self.base, self.chunks = pc, dst, base, chunks
        self.n = dst.shape[1] // chunks

    def at(self, w, k):
        return self.dst.at[w, pl.ds(k * self.n, self.n)]

    def send(self, k):
        pc = self.pc
        self.wire.send(self.base + k, self.at(pc.w, k), self.at(pc.w, k), pc.over())
        self.wire.send(self.base + self.chunks + k, self.at(pc.w, k), self.at(pc.w, k), pc.twin())

    def finish_steps(self):
        pc, n = self.pc, self.chunks
        over = (1 - pc.yh) * 2 + pc.co
        for k in range(n):
            self.wire.arrive(self.base + k, self.at(over, k), pc.over())
            self.wire.send(self.base + 2 * n + k, self.at(over, k), self.at(over, k), pc.twin())
            yield
        for k in range(n):
            self.wire.arrive(self.base + n + k, self.at(pc.yh * 2 + 1 - pc.co, k), pc.twin())
        for k in range(n):
            self.wire.arrive(self.base + 2 * n + k, self.at((1 - pc.yh) * 2 + 1 - pc.co, k), pc.twin())
        self.wire.drain()


def turn(value, table, row, buf):
    count = value.shape[1] // 128
    swapped = [pltpu.roll(value[:, m * 128 : (m + 1) * 128], 64, 1) for m in range(count)]
    low = lax.broadcasted_iota(jnp.int32, swapped[0].shape, 1) < 64
    for m in range(count):
        buf[0, m] = value[:, m * 128 : (m + 1) * 128]
        buf[1, m] = jnp.where(low, swapped[m], swapped[(m + 1) % count])
    odd = table[row, count]
    return jnp.concatenate([buf[odd, table[row, m]] for m in range(count)], axis=1)


def dma(n):
    return pltpu.SemaphoreType.DMA((n,))


def params(cid):
    return pltpu.CompilerParams(collective_id=cid, has_side_effects=True, vmem_limit_bytes=62 << 20)


def vm(shape, dtype):
    return pltpu.VMEM(shape, dtype)


def sds(shape, dtype):
    return jax.ShapeDtypeStruct(shape, dtype)


def spec(space):
    return pl.BlockSpec(memory_space=space)


CHUNKS = 4
ONE = pltpu.SemaphoreType.DMA(())


def upper_lanes(shape):
    return lax.broadcasted_iota(jnp.int32, shape, 1) >= 64


def head_tile(pair, odd, upper):
    moved = pair if odd == upper else pltpu.roll(pair, 64, 1)
    lanes = upper_lanes(pair.shape)
    return jnp.where(lanes if upper else jnp.logical_not(lanes), moved, 0.0)


def dot_nt(a, b):
    return lax.dot_general(a, b, (((1,), (1,)), ((), ())), preferred_element_type=F32)


def dot_nn(a, b):
    return lax.dot_general(a, b, (((1,), (0,)), ((), ())), preferred_element_type=F32)


def dot_tn(a, b):
    return lax.dot_general(a, b, (((0,), (0,)), ((), ())), preferred_element_type=F32)


def table_kernel(pair_ref, off_ref, at_ref, pick_ref, home_ref, out_ref, turn_ref):
    def slot(c, carry):
        for s in range(4):
            for j in range(2):
                b = pair_ref[s, c * 2 + j]
                home_ref[0, s * 64 + b] = c
                home_ref[1, s * 64 + b] = j + 2 * s
                out_ref[0, s * 64 + c * 2 + j] = b >> 2
                out_ref[1, s * 64 + c * 2 + j] = b & 3
        return carry

    lax.fori_loop(0, 32, slot, 0)
    at = at_ref[0]
    for s in range(4):
        low = pair_ref[s, 2 * at]
        m = low >> 2
        for i in range(8):
            pick_ref[0, s * 9 + i] = jnp.where(i <= m, 0, 1)
            pick_ref[1, s * 9 + i] = jnp.where(i <= m, i, 15 - i)
            pick_ref[2, s * 9 + i] = jnp.where(i == m, (low - 4 * m + 1) * 64, 256)
        pick_ref[0, s * 9 + 8] = 1
        pick_ref[1, s * 9 + 8] = 15 - m
        pick_ref[2, s * 9 + 8] = (4 * m - low + 4) * 64
    for row, (which, sign) in enumerate(((0, -1), (3, -1), (1, 1), (2, -1), (2, 1), (1, -1), (0, 1))):
        pieces = (off_ref[which] * sign + 32) & 31
        for n in range(16):
            turn_ref[row, n] = (n + 32 - ((pieces + 1) >> 1)) & 15
        turn_ref[row, 16] = pieces & 1


def table_call(pairs, offsets, place):
    return pl.pallas_call(
        table_kernel,
        out_shape=tuple(sds(shape, jnp.int32) for shape in ((3, 36), (2, 256), (2, 256), (7, 17))),
        in_specs=[spec(SM)] * 3,
        out_specs=(spec(SM),) * 4,
        name="tables",
    )(pairs, offsets, place)


def scale_of(v):
    return lax.rsqrt(jnp.mean(v * v, -1, keepdims=True) + NORM_EPS)


def swap_lanes(v):
    parts = []
    for m in range(v.shape[1] // 128):
        part = v[:, m * 128 : (m + 1) * 128]
        first = (lax.broadcasted_iota(jnp.int32, part.shape, 1) % 64) < 32
        parts.append(jnp.where(first, pltpu.roll(part, 96, 1), pltpu.roll(part, 32, 1)))
    return parts[0] if len(parts) == 1 else jnp.concatenate(parts, 1)


def forward_kernel(
    pick_ref, home_ref, turn_ref, x_ref, t_ref, g_ref, cos_ref, sin_ref, wq_ref, wp_ref, wd_ref, wg_ref, wu_ref,
    a_ref, q_ref, o_ref, inv_ref, nat_ref, tail_ref, wqf, wpf, wdf, wgf, wuf, mid_ref, hb_ref,
    kv, kvg, qt, acc, ob, part, b0, b1, sb, b2, tb,
    qs, qr, ql, ks, kr, kl, ps, pr, pll, ds, dr, dl, gs, gr, gl, us, ur, ul, ss, sr, ts, tr, hs, hr, fs, fr,
):
    pc = Place()
    greet(pc)
    joined = gather_steps(pc, wq_ref, wqf, qs, qr, ql)
    keys = gather_steps(pc, kv, kvg, ks, kr, kl)
    proj = gather_steps(pc, wp_ref, wpf, ps, pr, pll)
    big = in_turn(
        gather_steps(pc, wd_ref, wdf, ds, dr, dl, late=True),
        gather_steps(pc, wg_ref, wgf, gs, gr, gl),
        gather_steps(pc, wu_ref, wuf, us, ur, ul),
    )
    next(joined)
    rows_share = Share(pc, a_ref, ss, sr, 0, CHUNKS)
    for k in range(CHUNKS):
        rows = pl.ds(k * 32, 32)
        x = x_ref[rows].astype(F32)
        a_ref[pc.w, rows] = turn(x * scale_of(x) * g_ref[0:1], turn_ref, 0, tb).astype(BF)
        rows_share.send(k)
    next(joined)
    for k in range(CHUNKS):
        rows = pl.ds(k * 32, 32)
        tail_ref[pc.w, rows] = turn(t_ref[rows].astype(F32), turn_ref, 1, tb).astype(BF)
    next(big)
    run_all(joined, rows_share.finish_steps())
    next(big)
    next(proj)
    a = a_ref[...].reshape(512, D)
    cosine = cos_ref[...].reshape(512, 256)
    sine = sin_ref[...].reshape(512, 256)
    last = lax.dot_general(
        a, wqf[:, :, pl.ds(512, 128)].reshape(D, 128), (((1,), (0,)), ((), ())), preferred_element_type=F32
    )
    kv[...] = (last * cosine[:, 128:] + swap_lanes(last) * sine[:, 128:]).astype(BF).reshape(8, 64, 128)
    next(keys)
    next(proj)
    tail_share = Share(pc, tail_ref, ts, tr, 0, CHUNKS)
    for k in range(CHUNKS):
        tail_share.send(k)
    tail = tail_share.finish_steps()
    for n in range(2):
        heads = lax.dot_general(
            a, wqf[:, :, pl.ds(n * 256, 256)].reshape(D, 256), (((1,), (0,)), ((), ())), preferred_element_type=F32
        )
        turned = swap_lanes(heads)
        for m in range(2):
            cols = slice(m * 128, (m + 1) * 128)
            out = (heads[:, cols] * cosine[:, :128] + turned[:, cols] * sine[:, :128]).astype(BF).astype(F32) * 0.125
            q_ref[:, :, :, pl.ds(n * 256 + m * 128, 128)] = out.astype(BF).reshape(4, 2, 64, 128)
    run_all(keys)

    def poll(count):
        for _ in range(count):
            next(proj, None)
            next(big, None)
        next(tail, None)

    lanes = lax.broadcasted_iota(jnp.int32, (512, 256), 1)
    wide = lax.broadcasted_iota(jnp.int32, (256, 128), 1) < 64

    def tile(queries, keys_values, limit=None):
        e = jnp.exp(dot_nt(queries, keys_values))
        if limit is not None:
            e = jnp.where(lanes < limit, e, 0.0)
        ones_values = jnp.where(wide, jnp.ones_like(keys_values), keys_values)
        return dot_nn(e.astype(BF), ones_values)

    def attend(s):
        for j in range(2):
            for m in range(4):
                pair = q_ref[s, j, :, pl.ds(m * 128, 128)].astype(F32)
                qt[j, pl.ds(m * 128, 64)] = head_tile(pair, False, False).astype(BF)
                qt[j, pl.ds(m * 128 + 64, 64)] = head_tile(pair, True, False).astype(BF)

        def order(t, carry):
            for r in range(4):
                at = s * 64 + t * 4 + r
                nat_ref[s, t, pl.ds(r * 64, 64)] = kvg[home_ref[0, at], home_ref[1, at]]
            return carry

        lax.fori_loop(0, 16, order, 0)
        acc[...] = jnp.zeros_like(acc)

        def body(i, carry):
            which = pick_ref[0, s * 9 + i]
            high_part = tile(qt[1], nat_ref[s, i])
            picked = tile(qt[which], nat_ref[s, pick_ref[1, s * 9 + i]], pick_ref[2, s * 9 + i])
            to_low = jnp.broadcast_to(which, picked.shape) == 0
            acc[0] += jnp.where(to_low, picked, 0.0)
            acc[1] += high_part + jnp.where(to_low, 0.0, picked)
            return carry

        for n in range(4):
            lax.fori_loop(2 * n, 2 * n + 2, body, 0)
            poll(2)
        acc[1] += tile(qt[1], nat_ref[s, pick_ref[1, s * 9 + 8]], pick_ref[2, s * 9 + 8])
        for j in range(2):
            for m2 in range(4):
                even = acc[j, pl.ds(m2 * 128, 64)]
                odd = acc[j, pl.ds(m2 * 128 + 64, 64)]
                up = upper_lanes(even.shape)
                bottom = jnp.where(up, pltpu.roll(odd, 64, 1), even)
                top = jnp.where(up, odd, pltpu.roll(even, 64, 1))
                inverse = 1.0 / bottom
                cols = pl.ds(m2 * 128, 128)
                inv_ref[s, j, :, cols] = inverse
                o_ref[s, j, :, cols] = top * inverse
                ob[pl.ds(j * 64, 64), cols] = (top * inverse).astype(BF)
        poll(2)

    def project(s):
        for n in range(8):
            columns = wpf[pl.ds(n * 4, 4)].reshape(256, 512)
            part[s, :, pl.ds(n * 256, 256)] = dot_nt(ob[...], columns).astype(BF)

    fold = Fold(pc, part, (b0, b1, sb, b2), fs, fr, CHUNKS)
    attend(pc.far_twin)
    run_all(proj)
    project(pc.far_twin)
    fold.far_twin()
    attend(pc.far)
    project(pc.far)
    fold.far()
    attend(pc.near_twin)
    project(pc.near_twin)
    fold.near_twin()
    attend(pc.w)
    project(pc.w)
    run_all(tail)
    norm_share = Share(pc, hb_ref, hs, hr, 0, CHUNKS)
    for k in range(CHUNKS):
        rows = pl.ds(k * 32, 32)
        mid = x_ref[rows].astype(F32) + turn(fold.total(k), turn_ref, 2, tb)
        mid_ref[rows] = mid
        hb_ref[pc.w, rows] = turn(mid * scale_of(mid) * g_ref[1:2], turn_ref, 3, tb).astype(BF)
        norm_share.send(k)
        next(big, None)
    fold.wire.drain()
    run_all(big, norm_share.finish_steps())


def forward_call(pick, home, turns, x, t, g, cosine, sine, wq, wp, wd, wg, wu):
    ag = [dma(AG_SEMS), dma(AG_SEMS), ONE]
    return pl.pallas_call(
        forward_kernel,
        out_shape=(
            sds((4, 128, D), BF), sds((4, 2, 64, 512), BF), sds((4, 2, 64, 512), F32), sds((4, 2, 64, 512), F32),
            sds((4, 16, 256, 128), BF), sds((4, 128, D), BF), sds((32,) + wq.shape, BF), sds((32,) + wp.shape, BF),
            sds((32,) + wd.shape, BF), sds((32,) + wg.shape, BF), sds((32,) + wu.shape, BF),
            sds((128, D), F32), sds((4, 128, D), BF),
        ),
        in_specs=[spec(SM)] * 3 + [spec(VM)] * 5 + [spec(HB)] * 5,
        out_specs=(spec(VM),) * 8 + (spec(HB),) * 3 + (spec(VM),) * 2,
        scratch_shapes=[
            vm((8, 64, 128), BF), vm((32, 8, 64, 128), BF), vm((2, 512, 128), BF), vm((2, 512, 128), F32),
            vm((128, 512), BF), vm((4, 128, D), BF),
        ] + fold_scratch() + ag * 6 + [dma(3 * CHUNKS)] * 8,
        compiler_params=params(1),
        name="forward_rows",
    )(pick, home, turns, x, t, g, cosine, sine, wq, wp, wd, wg, wu)


def fold_scratch():
    return [vm((128, 2048), BF) for _ in range(4)] + [vm((2, 16, 32, 128), F32)]


def outer(dst, cols, lhs, rhs):
    for n in range(8):
        block = lhs[:, :, pl.ds(n * 256, 256)].reshape(512, 256)
        dst[pl.ds(n * 4, 4), :, cols] = dot_tn(block, rhs).astype(BF).reshape(4, 64, rhs.shape[1])


def backward_kernel(
    pick_ref, pair_ref, turn_ref, g_ref, dh_ref, tail_in, act_ref, hb_in, dg_in, du_in, mid_in, cot_ref, x_ref, cos_in, sin_in,
    q_in, o_in, inv_in, nat_in, wp_in, wq_in, a_in, out_in, pq_ref, pg_ref, pu_ref,
    grad_ref, out_ref, sq_ref, sp_ref, sg_ref, su_ref, sd_ref, gain_ref,
    xpart, xbuf, ypart, ybuf, rows, tail, hb, dg, du, ga, mid, cosine, sine, q, o, inv, wp, wq, nat0, nat1,
    dmid, dp, dkv, dnat, dqa, qt, gt, dl, dor, b0, b1, sb, b2, tb, vb,
    ds, dr, gs, gr, us, ur, ps, pr, ks, kr, qs, qr, hs, hr, fs, fr, es, er, cs, cr, ss, sr, vs, vr, ls, ns, free,
):
    pc = Place()
    fetches = {}

    def fetch(name, src, dst, k):
        fetches[name] = pltpu.make_async_copy(src, dst, ls.at[k])
        fetches[name].start()

    def have(*names):
        for name in names:
            fetches.pop(name).wait()

    fetch("rows", dh_ref, rows, 0)
    fetch("tail", tail_in, tail, 1)
    fetch("mid", mid_in, mid, 2)
    fetch("hb", hb_in, hb, 3)
    fetch("dg", dg_in, dg, 4)
    fetch("du", du_in, du, 5)
    fetch("wp", wp_in, wp, 6)
    fetch("q", q_in, q, 7)
    fetch("o", o_in, o, 8)
    fetch("inv", inv_in, inv, 9)
    fetch("cos", cos_in, cosine, 10)
    fetch("sin", sin_in, sine, 11)
    fetch("wq", wq_in, wq, 12)
    order = (pc.w, pc.near_twin, pc.far, pc.far_twin)
    slots = (nat0, nat1)
    tiles = [pltpu.make_async_copy(nat_in.at[s], slots[n % 2], ns.at[n]) for n, s in enumerate(order)]
    tiles[0].start()
    tiles[1].start()
    greet(pc)

    def tell(k, wsh):
        peers = [pc.over(), pc.twin()] if wsh else ctx_peers(pc)
        for peer in peers:
            pl.semaphore_signal(free.at[k], inc=1, device_id=peer, device_id_type=MESH)

    def hear(k, wsh):
        pl.semaphore_wait(free.at[k], 2 if wsh else 5)

    def total(own, other):
        return own[...].astype(F32) + other[...].astype(F32)

    def to(ref):
        def finish(own, other):
            ref[...] = total(own, other)

        return finish

    def gain_part(ref, piece):
        return jnp.sum(ref[...] * piece[...].astype(F32), -1, keepdims=True)

    boxes = (b0, b1, sb, b2)
    wide = slice(0, 1408)
    have("rows")
    fold = Fold(pc, rows, boxes, fs, fr, CHUNKS)
    fold.far_twin()
    fold.near_twin()
    have("tail")
    outer(xpart, wide, tail, act_ref[...])
    down = scatter_steps(pc, xpart, xbuf, ds, dr, to(sd_ref))
    next(down)
    fold.far()
    have("hb", "dg", "du")
    outer(ypart, wide, hb, dg[...])
    gate = scatter_steps(pc, ypart.at[:, :, pl.ds(0, 1408)], ybuf.at[:, pl.ds(0, 1408)], gs, gr, to(sg_ref))
    next(gate)
    fetch("out", out_in, tail, 13)
    state = {"ga": False, "y": False, "x": False}

    def lane_x():
        yield from down
        tell(0, False)
        outer(xpart, wide, hb, du[...])
        fetch("a", a_in, hb, 14)
        hear(0, False)
        yield
        yield from scatter_steps(pc, xpart, xbuf, us, ur, to(su_ref))
        tell(1, False)
        state["x"] = True

    def lane_y():
        yield from gate
        tell(2, False)
        assert state["ga"]
        outer(ypart, pl.ds(1024, 512), ga, o[...].reshape(512, 512).astype(BF))
        hear(2, False)
        state["y"] = True
        yield
        yield from scatter_steps(
            pc, ypart.at[:, :, pl.ds(1024, 512)], ybuf.at[:, pl.ds(1024, 512)], ps, pr, to(sp_ref)
        )

    xs, ys = lane_x(), lane_y()
    share = Share(pc, ga, ss, sr, 0, CHUNKS)
    have("mid")
    for k in range(CHUNKS):
        r = pl.ds(k * 32, 32)
        m = mid[r]
        weighted = turn(fold.total(k), turn_ref, 4, tb) * g_ref[1:2]
        scale = scale_of(m)
        mean = jnp.mean(weighted * m, -1, keepdims=True)
        dm = cot_ref[r].astype(F32) + scale * weighted - m * (scale * scale * scale) * mean
        dmid[r] = dm
        ga[pc.w, r] = turn(dm, turn_ref, 5, tb).astype(BF)
        share.send(k)
    fold.wire.drain()
    tell(3, True)
    for _ in share.finish_steps():
        next(xs)
        next(ys)
    state["ga"] = True
    have("out", "wp", "q", "o", "inv", "cos", "sin")
    hear(3, True)
    out_fold = Fold(pc, tail, boxes, es, er, CHUNKS)

    def put_out(k, value):
        out_ref[pl.ds(k * 32, 32)] = value

    out_steps = out_fold.steps(put_out)

    def poll(count):
        for _ in range(count):
            next(xs, None)
            next(ys, None)
        next(out_steps, None)

    rows_iota = lax.broadcasted_iota(jnp.int32, (256, 512), 0)
    ones = jnp.ones((8, 128), BF)

    def tile(j, keys_values, limit=None):
        queries, upward = qt[j], gt[j]
        e = jnp.exp(dot_nt(keys_values, queries))
        if limit is not None:
            e = jnp.where(rows_iota < limit, e, 0.0)
        dscore = (e * (dot_nt(keys_values, upward) - dl[j, 0:1])).astype(BF)
        return dot_tn(dscore, keys_values), dot_nn(dscore, queries) + dot_nn(e.astype(BF), upward)

    def attend(n):
        s, kv = order[n], slots[n % 2]
        dor[...] = dot_nn(ga[s], wp[...].reshape(D, 512)).reshape(2, 64, 512)
        for j in range(2):
            sums = []
            for m2 in range(4):
                cols = pl.ds(m2 * 128, 128)
                pair = q[s, j, :, cols].astype(F32)
                ratio = dor[j, :, cols] * inv[s, j, :, cols]
                prod = ratio * o[s, j, :, cols]
                for odd in (False, True):
                    place = pl.ds(m2 * 128 + (64 if odd else 0), 64)
                    qt[j, place] = head_tile(pair, odd, False).astype(BF)
                    gt[j, place] = head_tile(ratio, odd, True).astype(BF)
                    sums.append(head_tile(prod, odd, False))
            whole = jnp.concatenate(sums, 0)
            big = whole.astype(BF)
            rest = (whole - big.astype(F32)).astype(BF)
            dl[j] = dot_nt(ones, big) + dot_nt(ones, rest)
        dqa[...] = jnp.zeros_like(dqa)
        tiles[n].wait()

        def body(i, carry):
            which = pick_ref[0, s * 9 + i]
            dq1, dkv1 = tile(1, kv[i])
            dq2, dkv2 = tile(which, kv[pick_ref[1, s * 9 + i]], pick_ref[2, s * 9 + i])
            to_low = jnp.broadcast_to(which, dq2.shape) == 0
            dqa[0] += jnp.where(to_low, dq2, 0.0)
            dqa[1] += dq1 + jnp.where(to_low, 0.0, dq2)
            to_low = jnp.broadcast_to(which, dkv2.shape) == 0
            dnat[i] = (dkv1 + jnp.where(to_low, dkv2, 0.0)).reshape(4, 64, 128)
            dnat[15 - i] = jnp.where(to_low, 0.0, dkv2).reshape(4, 64, 128)
            return carry

        for part in range(4):
            lax.fori_loop(2 * part, 2 * part + 2, body, 0)
            poll(2)
        kt = pick_ref[1, s * 9 + 8]
        dq3, dkv3 = tile(1, kv[kt], pick_ref[2, s * 9 + 8])
        dqa[1] += dq3
        for t in range(8, 16):
            here = jnp.broadcast_to(kt, dkv3.shape) == t
            dnat[t] += jnp.where(here, dkv3, 0.0).reshape(4, 64, 128)
        if n + 2 < 4:
            tiles[n + 2].start()
        for j in range(2):
            for m2 in range(4):
                even = dqa[j, pl.ds(m2 * 128, 64)]
                odd = dqa[j, pl.ds(m2 * 128 + 64, 64)]
                both = jnp.where(upper_lanes(even.shape), pltpu.roll(odd, 64, 1), even) * 0.125
                turned = both * cosine[s, j, :, :128] - swap_lanes(both) * sine[s, j, :, :128]
                dp[s, j, :, pl.ds(m2 * 128, 128)] = turned.astype(BF)
        while not state["y"]:
            next(xs, None)
            next(ys)

        def place_block(c, carry):
            for j in range(2):
                at = s * 64 + c * 2 + j
                block = dnat[pair_ref[0, at], pair_ref[1, at]].astype(BF)
                ypart[c, :, pl.ds(pl.multiple_of((s * 2 + j) * 128, 128), 128)] = block
            return carry

        lax.fori_loop(0, 32, place_block, 0)

    for n in range(4):
        attend(n)
    for _ in out_steps:
        pass
    tell(4, True)
    keys = scatter_steps(pc, ypart.at[:, :, pl.ds(0, 1024)], ybuf.at[:, pl.ds(0, 1024)], ks, kr, to(dkv))
    for _ in keys:
        next(xs, None)
    for s in range(4):
        for j in range(2):
            both = dkv[:, pl.ds((s * 2 + j) * 128, 128)]
            turned = both * cosine[s, j, :, 128:] - swap_lanes(both) * sine[s, j, :, 128:]
            dp[s, j, :, pl.ds(512, 128)] = turned.astype(BF)
    have("wq")

    def back(s):
        for n in range(8):
            columns = wq[pl.ds(n * 4, 4)].reshape(256, 640)
            rows[s, :, pl.ds(n * 256, 256)] = dot_nt(dp[s].reshape(128, 640), columns).astype(BF)

    hear(4, True)
    last = Fold(pc, rows, boxes, cs, cr, CHUNKS)
    back(pc.far_twin)
    last.far_twin()
    back(pc.near_twin)
    last.near_twin()
    back(pc.far)
    last.far()
    back(pc.w)
    for _ in xs:
        next(ys, None)
    have("a")
    outer(xpart, pl.ds(0, 640), hb, dp[...].reshape(512, 640))
    hear(1, False)
    joined = scatter_steps(pc, xpart.at[:, :, pl.ds(0, 640)], xbuf.at[:, pl.ds(0, 640)], qs, qr, to(sq_ref))
    next(joined)
    next(joined)
    for k in range(CHUNKS):
        r = pl.ds(k * 32, 32)
        x = x_ref[r].astype(F32)
        weighted = turn(last.total(k), turn_ref, 6, tb) * g_ref[0:1]
        scale = scale_of(x)
        mean = jnp.mean(weighted * x, -1, keepdims=True)
        grad_ref[r] = dmid[r] + scale * weighted - x * (scale * scale * scale) * mean
        next(joined)
    last.wire.drain()
    run_all(joined, ys)
    wire = Wire(vs, vr)
    first = gain_part(sq_ref, pq_ref)
    second = gain_part(sg_ref, pg_ref) + gain_part(su_ref, pu_ref)
    vb[0] = jnp.where(lax.broadcasted_iota(jnp.int32, (64, 128), 1) == 0, first, second)
    wire.send(0, vb.at[0], vb.at[1], pc.twin())
    wire.arrive(0, vb.at[1], pc.twin())
    vb[2] = vb[0] + vb[1]
    wire.send(1, vb.at[2], vb.at[3], pc.over())
    wire.arrive(1, vb.at[3], pc.over())
    vb[4] = vb[2] + vb[3]
    run_all(gather_steps(pc, vb.at[4], gain_ref, hs, hr, ls.at[15]))
    wire.drain()


def backward_call(*args):
    rs = [dma(RS_SEMS)] * 2
    small = [dma(3 * CHUNKS)] * 2
    return pl.pallas_call(
        backward_kernel,
        out_shape=(
            sds((128, D), F32), sds((128, D), F32), sds((64, 640), F32), sds((64, 512), F32),
            sds((64, 1408), F32), sds((64, 1408), F32), sds((64, 1408), F32), sds((32, 64, 128), F32),
        ),
        in_specs=[spec(SM)] * 3 + [spec(VM)] + [spec(HB)] * 2 + [spec(VM)] + [spec(HB)] * 4 + [spec(VM)] * 2
        + [spec(HB)] * 10 + [spec(VM)] * 3,
        out_specs=(spec(VM),) * 8,
        scratch_shapes=[
            vm((32, 64, 1408), BF), vm((31 * 64, 1408), BF), vm((32, 64, 1536), BF), vm((31 * 64, 1536), BF),
            vm((4, 128, D), BF), vm((4, 128, D), BF), vm((4, 128, D), BF), vm((512, 1408), BF), vm((512, 1408), BF),
            vm((4, 128, D), BF), vm((128, D), F32), vm((4, 2, 64, 256), F32), vm((4, 2, 64, 256), F32),
            vm((4, 2, 64, 512), BF), vm((4, 2, 64, 512), F32), vm((4, 2, 64, 512), F32), vm((32, 64, 512), BF),
            vm((32, 64, 640), BF), vm((16, 256, 128), BF), vm((16, 256, 128), BF),
            vm((128, D), F32), vm((4, 2, 64, 640), BF), vm((64, 1024), F32), vm((16, 4, 64, 128), F32),
            vm((2, 512, 128), F32), vm((2, 512, 128), BF), vm((2, 512, 128), BF), vm((2, 8, 512), F32), vm((2, 64, 512), F32),
        ] + fold_scratch() + [vm((5, 64, 128), F32)]
        + rs * 6 + [dma(AG_SEMS)] * 2 + small * 4 + [dma(2)] * 2 + [dma(16), dma(4), pltpu.SemaphoreType.REGULAR((5,))],
        compiler_params=params(2),
        name="backward_rows",
    )(*args)


def rope_tables(positions):
    half_width = HD // 2
    inverse = ROPE_BASE ** (-(jnp.arange(half_width, dtype=F32) * 2.0 / HD))
    angles = positions.astype(F32)[..., None] * inverse
    cosine, sine = jnp.cos(angles), jnp.sin(angles)
    signed = jnp.concatenate([-sine, sine], -1)
    cosine = jnp.concatenate([cosine, cosine], -1)
    cosine = jnp.concatenate([cosine] * 3 + [jnp.ones_like(cosine)], -1)
    return (cosine, jnp.concatenate([signed] * 3 + [jnp.zeros_like(signed)], -1))


def adamw_step(master, first_state, second_state, gradient, rate_value):
    first_new = BETA_FIRST * first_state + (1.0 - BETA_FIRST) * gradient
    second_new = BETA_SECOND * second_state + (1.0 - BETA_SECOND) * gradient * gradient
    first_fix = 1.0 - BETA_FIRST**STEP
    second_fix = 1.0 - BETA_SECOND**STEP
    update = first_new / first_fix / (jnp.sqrt(second_new / second_fix) + ADAM_EPS)
    return (master - rate_value * (update + WEIGHT_DECAY * master), first_new, second_new)


def matmul(a, b, dims, out):
    return lax.dot_general(a, b, (dims, ((), ())), preferred_element_type=F32).astype(out)


def per_device(
    tokens, cotangent, block_pairs, offsets,
    qkv_master, qkv_first, qkv_second,
    proj_master, proj_first, proj_second,
    inner_master, inner_first, inner_second,
    down_master, down_first, down_second,
    gains, gain_first, gain_second,
):
    offsets = offsets.astype(jnp.int32)
    shift = offsets * 64
    g1, g2 = gains[:, 0][None], gains[:, 1][None]
    qkv_piece = qkv_master[:, 0].astype(BF)
    gate_piece, up_piece = inner_master[:, 0].astype(BF), inner_master[:, 1].astype(BF)
    down_piece = down_master.astype(BF).T
    proj_piece = proj_master.astype(BF).T
    place = lax.axis_index("ctx").astype(jnp.int32)
    pick, home, pairs, turns = table_call(block_pairs.reshape(4, 64).astype(jnp.int32), offsets, place[None])
    own_pairs = lax.dynamic_index_in_dim(block_pairs, place, 1, keepdims=False)
    positions = (own_pairs[:, :, None] * BLK + jnp.arange(BLK, dtype=jnp.int32)).reshape(4, 2, 64)
    cosine, sine = rope_tables(positions)

    (a_all, q, o, inverse, nat, tail_all, qkv_full, proj_full, down_full, gate_full, up_full, middle, hb) = forward_call(
        pick, home, turns, tokens[0], cotangent[0], jnp.concatenate([g1, g2], 0), cosine, sine,
        qkv_piece, proj_piece, down_piece, gate_piece, up_piece,
    )
    a_all, hb, tail_all = a_all.reshape(512, D), hb.reshape(512, D), tail_all.reshape(512, D)
    qkv_full, proj_full = qkv_full.reshape(D, 640), proj_full.reshape(D, 512)
    down_full, gate_full, up_full = (w.reshape(D, 1408) for w in (down_full, gate_full, up_full))
    gate = matmul(hb, gate_full, ((1,), (0,)), F32)
    up = matmul(hb, up_full, ((1,), (0,)), F32)
    sg = jax.nn.sigmoid(gate)
    act = (gate * sg * up).astype(BF)
    dact = matmul(tail_all, down_full, ((1,), (0,)), F32)
    dgate = (dact * up * sg * (1.0 + gate * (1.0 - sg))).astype(BF)
    dup = (dact * gate * sg).astype(BF)
    dh = matmul(dgate, gate_full, ((1,), (1,)), F32) + matmul(dup, up_full, ((1,), (1,)), F32)
    dh = dh.astype(BF).reshape(4, 128, D)
    out_part = matmul(act, down_full, ((1,), (1,)), BF).reshape(4, 128, D)
    input_grad, out_sum, qkv_sum, proj_sum, gate_sum, up_sum, down_sum, gain_sums = backward_call(
        pick, pairs, turns, jnp.concatenate([g1, g2], 0), dh, tail_all.reshape(4, 128, D), act, hb.reshape(4, 128, D),
        dgate, dup, middle, cotangent[0], tokens[0], cosine, sine, q, o, inverse, nat, proj_full.reshape(32, 64, 512),
        qkv_full.reshape(32, 64, 640), a_all.reshape(4, 128, D), out_part, qkv_piece, gate_piece, up_piece,
    )
    output = middle + jnp.roll(out_sum, shift[3], axis=1)
    gain_sums = gain_sums.reshape(D, 128)
    gain_grad = (
        jnp.stack([jnp.roll(gain_sums[:, 0], shift[0]), jnp.roll(gain_sums[:, 1], shift[2])], 1) / gains
    )

    rate_rows = 2.0 / math.sqrt(D)
    rate_proj = 1.0
    rate_down = 2.0 / math.sqrt(FF)
    qkv_out = adamw_step(qkv_master, qkv_first, qkv_second, qkv_sum[:, None], rate_rows)
    proj_out = adamw_step(proj_master, proj_first, proj_second, proj_sum.T, rate_proj)
    inner_out = adamw_step(inner_master, inner_first, inner_second, jnp.stack([gate_sum, up_sum], 1), rate_rows)
    down_out = adamw_step(down_master, down_first, down_second, down_sum.T, rate_down)
    gain_out = adamw_step(gains, gain_first, gain_second, gain_grad, GAIN_RATE)
    return (output[None], input_grad[None], *qkv_out, *proj_out, *inner_out, *down_out, *gain_out)


def solution(mesh):
    rows, every = P("wsh", "ctx", None), P()
    qkv, inner, cols = P("ctx", "wsh", None), P("ctx", None, "wsh"), P("wsh", "ctx")
    return jax.shard_map(
        per_device,
        mesh=mesh,
        in_specs=(rows, rows, every, every) + (qkv,) * 3 + (cols,) * 3 + (inner,) * 3 + (cols,) * 3 + (every,) * 3,
        out_specs=(rows, rows) + (qkv,) * 3 + (cols,) * 3 + (inner,) * 3 + (cols,) * 3 + (every,) * 3,
        check_vma=False,
    )
```

```python
import math

import jax
import jax.numpy as jnp
from jax import lax
from jax.experimental import pallas as pl
from jax.experimental.pallas import tpu as pltpu
from jax.sharding import PartitionSpec as P
MESH = pl.DeviceIdType.MESH
F32, BF = jnp.float32, jnp.bfloat16
VM, HB, SM = pltpu.VMEM, pl.ANY, pltpu.SMEM

D = 2048
HD = 64
FF = 5632
BLK = 64
STEP = 7
NORM_EPS = 1e-05
ROPE_BASE = 10000.0
BETA_FIRST = 0.5
BETA_SECOND = 0.5
ADAM_EPS = 1e-08
WEIGHT_DECAY = 0.1
GAIN_RATE = 0.4

AG_SEMS = 81
RS_SEMS = 81


class Place:
    def __init__(self):
        c = lax.axis_index("ctx")
        w = lax.axis_index("wsh")
        self.c, self.w = c, w
        self.yl, self.yh, self.co = c // 16, w // 2, w % 2
        x, z = (c // 4) % 4, c % 4
        self.y16 = [self.yl * 16, 16 - self.yl * 16]
        self.x4 = {k: ((x + k + 4) % 4) * 4 for k in (-2, -1, 0, 1, 2)}
        self.z1 = {k: (z + k + 4) % 4 for k in (-2, -1, 0, 1, 2)}
        self.far = (1 - self.yh) * 2 + self.co
        self.near_twin = self.yh * 2 + 1 - self.co
        self.far_twin = (1 - self.yh) * 2 + 1 - self.co

    def step(self, axis, k):
        if axis == "x":
            return (self.y16[0] + self.x4[k] + self.z1[0], self.w)
        return (self.y16[0] + self.x4[0] + self.z1[k], self.w)

    def mate(self):
        return (self.y16[1] + self.x4[0] + self.z1[0], self.w)

    def over(self):
        return (self.c, self.far)

    def twin(self):
        return (self.c, self.near_twin)

    def piece(self, half, v, dp, dq):
        if half == 0:
            return self.y16[v] + self.x4[dp] + self.z1[dq]
        return self.y16[v] + self.x4[dq] + self.z1[dp]


def ctx_peers(place):
    return [place.step("x", 1), place.step("x", -1), place.step("z", 1), place.step("z", -1), place.mate()]


def greet(place):
    bar = pltpu.get_barrier_semaphore()
    peers = ctx_peers(place) + [place.over(), place.twin(), place.step("x", 2), place.step("z", 2)]
    for peer in peers:
        pl.semaphore_signal(bar, inc=1, device_id=peer, device_id_type=MESH)
    pl.semaphore_wait(bar, len(peers))


class Wire:
    def __init__(self, ssem, rsem):
        self.ssem, self.rsem, self.sent = ssem, rsem, []

    def send(self, k, src, dst, to):
        cp = pltpu.make_async_remote_copy(src, dst, self.ssem.at[k], self.rsem.at[k], device_id=to, device_id_type=MESH)
        cp.start()
        self.sent.append(cp)

    def arrive(self, k, view, frm):
        pltpu.make_async_remote_copy(view, view, self.ssem.at[k], self.rsem.at[k], device_id=frm, device_id_type=MESH).wait_recv()

    def drain(self):
        for cp in self.sent:
            cp.wait_send()
        self.sent = []


AXES = (("x", "z"), ("z", "x"))
GROUPS = (0, -1, 1, 2)


def gather_steps(pc, src, dst, ssem, rsem, lsem, late=False):
    wire = Wire(ssem, rsem)
    R = src.shape[0]
    H, S = R // 2, R // 4

    def part(v, h, dp, dq, lo=0, n=None):
        return dst.at[pc.piece(h, v, dp, dq), pl.ds(h * H + lo, H if n is None else n)]

    def key(v, h, k):
        return (v * 2 + h) * 20 + k

    local = pltpu.make_async_copy(src, dst.at[pc.c], lsem)
    local.start()
    both = (0,) if late else (0, 1)

    def cross(h, gi, d):
        if late:
            k = 40 + (h * 4 + gi) * 4 + (0, 2, 1, 3)[d + 1]
            view = part(0, h, GROUPS[gi], d)
            if gi == 0 and d == 0:
                wire.send(k, src.at[pl.ds(h * H, H)], view, pc.mate())
            else:
                wire.send(k, view, view, pc.mate())

    if not late:
        wire.send(80, src, dst.at[pc.c], pc.mate())

    def first(v, h):
        A, B = AXES[h]
        view = src.at[pl.ds(h * H, H)] if v == 0 else part(v, h, 0, 0)
        there = part(v, h, 0, 0)
        wire.send(key(v, h, 0), view, there, pc.step(A, 1))
        wire.send(key(v, h, 1), view, there, pc.step(A, -1))
        wire.send(key(v, h, 4), view, there, pc.step(B, 1))
        wire.send(key(v, h, 5), view, there, pc.step(B, -1))

    def along(v, h, gi):
        A, B = AXES[h]
        view = part(v, h, GROUPS[gi], 0)
        wire.send(key(v, h, 4 + 4 * gi), view, view, pc.step(B, 1))
        wire.send(key(v, h, 5 + 4 * gi), view, view, pc.step(B, -1))

    def spread1(v, h):
        A, B = AXES[h]
        wire.arrive(key(v, h, 0), part(v, h, -1, 0), pc.step(A, -1))
        s = part(v, h, -1, 0, 0, S)
        wire.send(key(v, h, 2), s, s, pc.step(A, 1))
        along(v, h, 1)
        wire.arrive(key(v, h, 1), part(v, h, 1, 0), pc.step(A, 1))
        s = part(v, h, 1, 0, S, S)
        wire.send(key(v, h, 3), s, s, pc.step(A, -1))
        along(v, h, 2)

    def spread2(v, h):
        A, B = AXES[h]
        wire.arrive(key(v, h, 2), part(v, h, 2, 0, 0, S), pc.step(A, -1))
        wire.arrive(key(v, h, 3), part(v, h, 2, 0, S, S), pc.step(A, 1))
        along(v, h, 3)

    def pass_on(v, h, gi):
        A, B = AXES[h]
        g = GROUPS[gi]
        k = 4 + 4 * gi
        wire.arrive(key(v, h, k), part(v, h, g, -1), pc.step(B, -1))
        s = part(v, h, g, -1, 0, S)
        wire.send(key(v, h, k + 2), s, s, pc.step(B, 1))
        wire.arrive(key(v, h, k + 1), part(v, h, g, 1), pc.step(B, 1))
        s = part(v, h, g, 1, S, S)
        wire.send(key(v, h, k + 3), s, s, pc.step(B, -1))

    for h in (0, 1):
        first(0, h)
        cross(h, 0, 0)
    yield
    if not late:
        wire.arrive(80, dst.at[pc.piece(0, 1, 0, 0)], pc.mate())
        for h in (0, 1):
            first(1, h)
        yield
    for v in both:
        for h in (0, 1):
            spread1(v, h)
            cross(h, 1, 0)
            cross(h, 2, 0)
        yield
    for v in both:
        for h in (0, 1):
            spread2(v, h)
            cross(h, 3, 0)
        yield
    for gi in range(4):
        for v in both:
            for h in (0, 1):
                pass_on(v, h, gi)
                cross(h, gi, -1)
                cross(h, gi, 1)
            yield
    for gi in range(4):
        for v in both:
            for h in (0, 1):
                A, B = AXES[h]
                k = 4 + 4 * gi
                wire.arrive(key(v, h, k + 2), part(v, h, GROUPS[gi], 2, 0, S), pc.step(B, -1))
                wire.arrive(key(v, h, k + 3), part(v, h, GROUPS[gi], 2, S, S), pc.step(B, 1))
                cross(h, gi, 2)
        yield
    if late:
        for gi in range(4):
            for h in (0, 1):
                for d in (-1, 0, 1, 2):
                    k = 40 + (h * 4 + gi) * 4 + (0, 2, 1, 3)[d + 1]
                    wire.arrive(k, part(1, h, GROUPS[gi], d), pc.mate())
            yield
    wire.drain()
    local.wait()


def scatter_steps(pc, part, buf, ssem, rsem, finish):
    wire = Wire(ssem, rsem)
    R = part.shape[1]
    H, S = R // 2, R // 4

    def key(v, h, k):
        return (v * 2 + h) * 20 + k

    def box(v, h, gi, which):
        base = ((v * 2 + h) * 5 + gi) * (R + H)
        off, n = ((0, S), (S, S), (2 * S, H), (2 * S + H, H))[which]
        return buf.at[pl.ds(base + off, n)]

    def mine(v, h, dp, dq, lo=0, n=None):
        return part.at[pc.piece(h, v, dp, dq), pl.ds(h * H + lo, H if n is None else n)]

    def add(to, *more):
        total = to[...].astype(F32)
        for m in more:
            total = total + m[...].astype(F32)
        to[...] = total.astype(BF)

    def where(stage, gi, d):
        return (GROUPS[gi], d) if stage == 1 else (d, 0)

    def ring_axis(stage, h):
        return AXES[h][1] if stage == 1 else AXES[h][0]

    def raw(v, h, gi, stage):
        X = ring_axis(stage, h)
        k = 4 * gi
        wire.send(key(v, h, k), mine(v, h, *where(stage, gi, -2), 0, S), box(v, h, gi, 0), pc.step(X, -1))
        wire.send(key(v, h, k + 1), mine(v, h, *where(stage, gi, 2), S, S), box(v, h, gi, 1), pc.step(X, 1))

    def mid(v, h, gi, stage):
        X = ring_axis(stage, h)
        k = 4 * gi
        wire.arrive(key(v, h, k), box(v, h, gi, 0), pc.step(X, 1))
        add(mine(v, h, *where(stage, gi, -1), 0, S), box(v, h, gi, 0))
        wire.send(key(v, h, k + 2), mine(v, h, *where(stage, gi, -1)), box(v, h, gi, 2), pc.step(X, -1))
        wire.arrive(key(v, h, k + 1), box(v, h, gi, 1), pc.step(X, -1))
        add(mine(v, h, *where(stage, gi, 1), S, S), box(v, h, gi, 1))
        wire.send(key(v, h, k + 3), mine(v, h, *where(stage, gi, 1)), box(v, h, gi, 3), pc.step(X, 1))

    def end(v, h, gi, stage):
        X = ring_axis(stage, h)
        k = 4 * gi
        wire.arrive(key(v, h, k + 2), box(v, h, gi, 2), pc.step(X, 1))
        wire.arrive(key(v, h, k + 3), box(v, h, gi, 3), pc.step(X, -1))
        add(mine(v, h, *where(stage, gi, 0)), box(v, h, gi, 2), box(v, h, gi, 3))

    order = (3, 1, 2, 0)
    for gi in order:
        for v in (1, 0):
            for h in (0, 1):
                raw(v, h, gi, 1)
    yield
    for gi in order:
        for v in (1, 0):
            for h in (0, 1):
                mid(v, h, gi, 1)
            yield
    for v in (1, 0):
        for gi in order:
            for h in (0, 1):
                end(v, h, gi, 1)
            if gi == 3:
                for h in (0, 1):
                    raw(v, h, 4, 2)
            yield
        if v == 1:
            for h in (0, 1):
                mid(1, h, 4, 2)
            yield
    for h in (0, 1):
        end(1, h, 4, 2)
    theirs = part.at[pc.piece(0, 1, 0, 0)]
    tail = buf.at[pl.ds(30 * R, R)]
    wire.send(80, theirs, tail, pc.mate())
    yield
    for h in (0, 1):
        mid(0, h, 4, 2)
    yield
    for h in (0, 1):
        end(0, h, 4, 2)
    yield
    wire.arrive(80, tail, pc.mate())
    finish(part.at[pc.c], tail)
    wire.drain()


def in_turn(*gens, lead=3):
    live, waiting = [gens[0]], list(gens[1:])
    count = 0
    while live:
        for g in list(live):
            try:
                next(g)
                yield
            except StopIteration:
                live.remove(g)
        count += 1
        if waiting and (count % lead == 0 or not live):
            live.append(waiting.pop(0))


def run_all(*gens):
    live = list(gens)
    while live:
        for g in list(live):
            try:
                next(g)
            except StopIteration:
                live.remove(g)


class Fold:
    def __init__(self, pc, part, boxes, ssem, rsem, chunks):
        self.wire = Wire(ssem, rsem)
        self.pc, self.part, self.chunks = pc, part, chunks
        self.b0, self.b1, self.sb, self.b2 = boxes
        n = part.shape[1] // chunks
        self.rows = [pl.ds(k * n, n) for k in range(chunks)]

    def far_twin(self):
        for k, r in enumerate(self.rows):
            self.wire.send(k, self.part.at[self.pc.far_twin, r], self.b0.at[r], self.pc.twin())

    def near_twin(self):
        for k, r in enumerate(self.rows):
            self.wire.send(self.chunks + k, self.part.at[self.pc.near_twin, r], self.b1.at[r], self.pc.twin())

    def far(self):
        for k, r in enumerate(self.rows):
            self.wire.arrive(k, self.b0.at[r], self.pc.twin())
            self.sb[r] = (self.part[self.pc.far, r].astype(F32) + self.b0[r].astype(F32)).astype(BF)
            self.wire.send(2 * self.chunks + k, self.sb.at[r], self.b2.at[r], self.pc.over())

    def total(self, k):
        r = self.rows[k]
        self.wire.arrive(self.chunks + k, self.b1.at[r], self.pc.twin())
        near = self.part[self.pc.w, r].astype(F32) + self.b1[r].astype(F32)
        self.wire.arrive(2 * self.chunks + k, self.b2.at[r], self.pc.over())
        return near + self.b2[r].astype(F32)

    def steps(self, each):
        self.far_twin()
        self.near_twin()
        yield
        self.far()
        yield
        for k in range(self.chunks):
            each(k, self.total(k))
            yield
        self.wire.drain()


class Share:
    def __init__(self, pc, dst, ssem, rsem, base, chunks):
        self.wire = Wire(ssem, rsem)
        self.pc, self.dst, self.base, self.chunks = pc, dst, base, chunks
        self.n = dst.shape[1] // chunks

    def at(self, w, k):
        return self.dst.at[w, pl.ds(k * self.n, self.n)]

    def send(self, k):
        pc = self.pc
        self.wire.send(self.base + k, self.at(pc.w, k), self.at(pc.w, k), pc.over())
        self.wire.send(self.base + self.chunks + k, self.at(pc.w, k), self.at(pc.w, k), pc.twin())

    def relay(self, k):
        far = self.at(self.pc.far, k)
        self.wire.arrive(self.base + k, far, self.pc.over())
        self.wire.send(self.base + 2 * self.chunks + k, far, far, self.pc.twin())

    def arrive_twin(self):
        for k in range(self.chunks):
            self.wire.arrive(self.base + self.chunks + k, self.at(self.pc.near_twin, k), self.pc.twin())

    def arrive_last(self):
        for k in range(self.chunks):
            self.wire.arrive(self.base + 2 * self.chunks + k, self.at(self.pc.far_twin, k), self.pc.twin())
        self.wire.drain()

    def finish_steps(self):
        for k in range(self.chunks):
            self.relay(k)
            yield
        self.arrive_twin()
        self.arrive_last()


def turn(value, table, row, buf):
    count = value.shape[1] // 128
    swapped = [pltpu.roll(value[:, m * 128 : (m + 1) * 128], 64, 1) for m in range(count)]
    low = lax.broadcasted_iota(jnp.int32, swapped[0].shape, 1) < 64
    for m in range(count):
        buf[0, m] = value[:, m * 128 : (m + 1) * 128]
        buf[1, m] = jnp.where(low, swapped[m], swapped[(m + 1) % count])
    odd = table[row, count]
    return jnp.concatenate([buf[odd, table[row, m]] for m in range(count)], axis=1)


def dma(n):
    return pltpu.SemaphoreType.DMA((n,))


def params(cid):
    return pltpu.CompilerParams(collective_id=cid, has_side_effects=True, vmem_limit_bytes=62 << 20)


def vm(shape, dtype):
    return pltpu.VMEM(shape, dtype)


def sds(shape, dtype):
    return jax.ShapeDtypeStruct(shape, dtype)


def spec(space):
    return pl.BlockSpec(memory_space=space)


CHUNKS = 4
ONE = pltpu.SemaphoreType.DMA(())


def upper_lanes(shape):
    return lax.broadcasted_iota(jnp.int32, shape, 1) >= 64


def head_tile(pair, odd, upper):
    moved = pair if odd == upper else pltpu.roll(pair, 64, 1)
    lanes = upper_lanes(pair.shape)
    return jnp.where(lanes if upper else jnp.logical_not(lanes), moved, 0.0)


def dot_nt(a, b):
    return lax.dot_general(a, b, (((1,), (1,)), ((), ())), preferred_element_type=F32)


def dot_nn(a, b):
    return lax.dot_general(a, b, (((1,), (0,)), ((), ())), preferred_element_type=F32)


def dot_tn(a, b):
    return lax.dot_general(a, b, (((0,), (0,)), ((), ())), preferred_element_type=F32)


def table_kernel(pair_ref, off_ref, at_ref, pick_ref, home_ref, out_ref, turn_ref):
    def slot(c, carry):
        for s in range(4):
            for j in range(2):
                b = pair_ref[s, c * 2 + j]
                home_ref[0, s * 64 + b] = c
                home_ref[1, s * 64 + b] = j
                out_ref[0, s * 64 + c * 2 + j] = b >> 2
                out_ref[1, s * 64 + c * 2 + j] = b & 3
        return carry

    lax.fori_loop(0, 32, slot, 0)
    at = at_ref[0]
    for s in range(4):
        low = pair_ref[s, 2 * at]
        m = low >> 2
        for i in range(8):
            pick_ref[0, s * 9 + i] = jnp.where(i <= m, 0, 1)
            pick_ref[1, s * 9 + i] = jnp.where(i <= m, i, 15 - i)
            pick_ref[2, s * 9 + i] = jnp.where(i == m, (low - 4 * m + 1) * 64, 256)
        pick_ref[0, s * 9 + 8] = 1
        pick_ref[1, s * 9 + 8] = 15 - m
        pick_ref[2, s * 9 + 8] = (4 * m - low + 4) * 64
    for row, (which, sign) in enumerate(((0, -1), (3, -1), (1, 1), (2, -1), (2, 1), (1, -1), (0, 1), (3, 1))):
        pieces = (off_ref[which] * sign + 32) & 31
        for n in range(16):
            turn_ref[row, n] = (n + 32 - ((pieces + 1) >> 1)) & 15
        turn_ref[row, 16] = pieces & 1


def table_call(pairs, offsets, place):
    return pl.pallas_call(
        table_kernel,
        out_shape=tuple(sds(shape, jnp.int32) for shape in ((3, 36), (2, 256), (2, 256), (8, 17))),
        in_specs=[spec(SM)] * 3,
        out_specs=(spec(SM),) * 4,
        name="tables",
    )(pairs, offsets, place)


def scale_of(v):
    return lax.rsqrt(jnp.mean(v * v, -1, keepdims=True) + NORM_EPS)


def swap_lanes(v):
    parts = []
    for m in range(v.shape[1] // 128):
        part = v[:, m * 128 : (m + 1) * 128]
        first = (lax.broadcasted_iota(jnp.int32, part.shape, 1) % 64) < 32
        parts.append(jnp.where(first, pltpu.roll(part, 96, 1), pltpu.roll(part, 32, 1)))
    return parts[0] if len(parts) == 1 else jnp.concatenate(parts, 1)


def key_only(cosine, sine):
    up = upper_lanes(cosine.shape)
    return jnp.where(up, 1.0, cosine), jnp.where(up, 0.0, sine)


def forward_kernel(
    pick_ref, home_ref, turn_ref, x_ref, t_ref, g_ref, cos_ref, sin_ref, wq_ref, wp_ref, wd_ref, wg_ref, wu_ref,
    a_out, q_out, o_out, inv_out, nat_out, tail_out, wq_out, wp_out, mid_ref, hb_out, act_ref, dg_ref, du_ref, dh_out, out_out,
    a_ref, q_ref, o_ref, inv_ref, nat_ref, tail_ref, wqf, wpf, wdf, wgf, wuf, hb_ref, gate, dact,
    kv, kva, kvb, kvga, kvgb, qt, acc, ob, part, b0, b1, sb, b2, tb,
    qs, qr, ql, ws, wr, wl, ks, kr, kl, js, jr, jl, ps, pr, pll, ds, dr, dl, gs, gr, gl, us, ur, ul, ss, sr, ts, tr, hs, hr, fs, fr, os,
):
    pc = Place()
    greet(pc)
    puts = []

    def put(src, dst):
        puts.append(pltpu.make_async_copy(src, dst, os.at[len(puts)]))
        puts[-1].start()

    done = {"down": False, "gate": False}

    def flagged(name, steps):
        yield from steps
        done[name] = True

    pair_cols, head_cols = pl.ds(512, 128), pl.ds(0, 512)
    joined = gather_steps(pc, wq_ref.at[:, pair_cols], wqf.at[:, :, pair_cols], qs, qr, ql)
    heads_in = gather_steps(pc, wq_ref.at[:, head_cols], wqf.at[:, :, head_cols], ws, wr, wl)
    order = (pc.far_twin, pc.far, pc.near_twin, pc.w)
    keys = [gather_steps(pc, kva, kvga, ks, kr, kl), gather_steps(pc, kvb, kvgb, js, jr, jl)]
    proj = gather_steps(pc, wp_ref, wpf, ps, pr, pll)
    big = in_turn(
        flagged("down", gather_steps(pc, wd_ref, wdf, ds, dr, dl, late=True)),
        flagged("gate", gather_steps(pc, wg_ref, wgf, gs, gr, gl)),
        gather_steps(pc, wu_ref, wuf, us, ur, ul),
    )
    next(joined)
    rows_share = Share(pc, a_ref, ss, sr, 0, CHUNKS)
    for k in range(CHUNKS):
        rows = pl.ds(k * 32, 32)
        x = x_ref[rows].astype(F32)
        a_ref[pc.w, rows] = turn(x * scale_of(x) * g_ref[0:1], turn_ref, 0, tb).astype(BF)
        rows_share.send(k)
    next(joined)
    for k in range(CHUNKS):
        rows = pl.ds(k * 32, 32)
        tail_ref[pc.w, rows] = turn(t_ref[rows].astype(F32), turn_ref, 1, tb).astype(BF)
    next(big)
    next(heads_in)
    run_all(joined, rows_share.finish_steps())
    next(big)
    next(proj)
    put(a_ref, a_out)
    a = a_ref[...].reshape(512, D)
    cosine = cos_ref[...].reshape(512, 128)
    sine = sin_ref[...].reshape(512, 128)
    last = dot_nn(a, wqf[:, :, pl.ds(512, 128)].reshape(D, 128))
    key_cosine, key_sine = key_only(cosine, sine)
    kv[...] = (last * key_cosine + swap_lanes(last) * key_sine).astype(BF).reshape(4, 2, 64, 128)
    for n, s in enumerate(order):
        (kva, kvb)[n // 2][pl.ds(n % 2 * 2, 2)] = kv[s]
    next(keys[0])
    next(heads_in)
    next(keys[0])
    next(keys[1])
    next(proj)
    tail_share = Share(pc, tail_ref, ts, tr, 0, CHUNKS)
    for k in range(CHUNKS):
        tail_share.send(k)
    tail = tail_share.finish_steps()
    run_all(heads_in, keys[0])
    put(wqf, wq_out)
    for n in range(2):
        next(keys[1])
        heads = dot_nn(a, wqf[:, :, pl.ds(n * 256, 256)].reshape(D, 256))
        turned = swap_lanes(heads)
        for m in range(2):
            cols = slice(m * 128, (m + 1) * 128)
            out = (heads[:, cols] * cosine + turned[:, cols] * sine).astype(BF).astype(F32) * 0.125
            q_ref[:, :, :, pl.ds(n * 256 + m * 128, 128)] = out.astype(BF).reshape(4, 2, 64, 128)
    put(q_ref, q_out)

    def poll(count):
        for _ in range(count):
            next(proj, None)
            next(big, None)
        next(tail, None)

    lanes = lax.broadcasted_iota(jnp.int32, (512, 256), 1)
    wide = lax.broadcasted_iota(jnp.int32, (256, 128), 1) < 64

    def tile(queries, keys_values, limit=None):
        e = jnp.exp(dot_nt(queries, keys_values))
        if limit is not None:
            e = jnp.where(lanes < limit, e, 0.0)
        ones_values = jnp.where(wide, jnp.ones_like(keys_values), keys_values)
        return dot_nn(e.astype(BF), ones_values)

    def attend(n):
        s, gathered, slot = order[n], (kvga, kvgb)[n // 2], n % 2 * 2
        if n == 2:
            run_all(keys[1])
        for j in range(2):
            for m in range(4):
                pair = q_ref[s, j, :, pl.ds(m * 128, 128)].astype(F32)
                qt[j, pl.ds(m * 128, 64)] = head_tile(pair, False, False).astype(BF)
                qt[j, pl.ds(m * 128 + 64, 64)] = head_tile(pair, True, False).astype(BF)

        def settle(t, carry):
            for r in range(4):
                at = s * 64 + t * 4 + r
                nat_ref[s, t, pl.ds(r * 64, 64)] = gathered[home_ref[0, at], slot + home_ref[1, at]]
            return carry

        lax.fori_loop(0, 16, settle, 0)
        acc[...] = jnp.zeros_like(acc)

        def body(i, carry):
            which = pick_ref[0, s * 9 + i]
            high_part = tile(qt[1], nat_ref[s, i])
            picked = tile(qt[which], nat_ref[s, pick_ref[1, s * 9 + i]], pick_ref[2, s * 9 + i])
            to_low = jnp.broadcast_to(which, picked.shape) == 0
            acc[0] += jnp.where(to_low, picked, 0.0)
            acc[1] += high_part + jnp.where(to_low, 0.0, picked)
            return carry

        for part in range(4):
            lax.fori_loop(2 * part, 2 * part + 2, body, 0)
            if n < 2:
                next(keys[1], None)
                next(keys[1], None)
            poll(2)
        acc[1] += tile(qt[1], nat_ref[s, pick_ref[1, s * 9 + 8]], pick_ref[2, s * 9 + 8])
        for j in range(2):
            for m2 in range(4):
                even = acc[j, pl.ds(m2 * 128, 64)]
                odd = acc[j, pl.ds(m2 * 128 + 64, 64)]
                up = upper_lanes(even.shape)
                bottom = jnp.where(up, pltpu.roll(odd, 64, 1), even)
                top = jnp.where(up, odd, pltpu.roll(even, 64, 1))
                inverse = 1.0 / bottom
                cols = pl.ds(m2 * 128, 128)
                inv_ref[s, j, :, cols] = inverse
                o_ref[s, j, :, cols] = top * inverse
                ob[pl.ds(j * 64, 64), cols] = (top * inverse).astype(BF)
        poll(2)

    def project(s):
        for n in range(8):
            columns = wpf[pl.ds(n * 4, 4)].reshape(256, 512)
            part[s, :, pl.ds(n * 256, 256)] = dot_nt(ob[...], columns).astype(BF)

    fold = Fold(pc, part, (b0, b1, sb, b2), fs, fr, CHUNKS)
    attend(0)
    run_all(proj)
    put(wpf, wp_out)
    project(pc.far_twin)
    fold.far_twin()
    attend(1)
    project(pc.far)
    fold.far()
    attend(2)
    project(pc.near_twin)
    fold.near_twin()
    attend(3)
    project(pc.w)
    run_all(tail)
    tail_put = pltpu.make_async_copy(tail_ref, tail_out, os.at[11])
    tail_put.start()
    put(o_ref, o_out)
    put(inv_ref, inv_out)
    put(nat_ref, nat_out)
    norm_share = Share(pc, hb_ref, hs, hr, 0, CHUNKS)
    for k in range(CHUNKS):
        rows = pl.ds(k * 32, 32)
        mid = x_ref[rows].astype(F32) + turn(fold.total(k), turn_ref, 2, tb)
        mid_ref[rows] = mid
        hb_ref[pc.w, rows] = turn(mid * scale_of(mid) * g_ref[1:2], turn_ref, 3, tb).astype(BF)
        norm_share.send(k)
        next(big, None)
    fold.wire.drain()
    while not done["down"]:
        next(big)
    columns = ((0, 512), (512, 512), (1024, 384))

    def times(rows, weights, lo, n):
        return dot_nn(rows[...].reshape(512, D), weights[:, :, pl.ds(lo, n)].reshape(D, n))

    for lo, n in columns:
        dact[:, pl.ds(lo, n)] = times(tail_ref, wdf, lo, n)
        next(big, None)
    for _ in norm_share.finish_steps():
        next(big, None)
    put(hb_ref, hb_out)
    while not done["gate"]:
        next(big)
    for lo, n in columns:
        gate[:, pl.ds(lo, n)] = times(hb_ref, wgf, lo, n)
        next(big, None)
    run_all(big)
    for lo, n in columns:
        cols = pl.ds(lo, n)
        up = times(hb_ref, wuf, lo, n)
        g, d = gate[:, cols], dact[:, cols]
        sg = 1.0 / (1.0 + jnp.exp(-g))
        act_ref[:, cols] = (g * sg * up).astype(BF)
        dg_ref[:, cols] = (d * up * sg * (1.0 + g * (1.0 - sg))).astype(BF)
        du_ref[:, cols] = (d * g * sg).astype(BF)
    for n in range(8):
        pieces, cols = pl.ds(n * 4, 4), pl.ds(n * 256, 256)
        dh = dot_nt(dg_ref[...], wgf[pieces].reshape(256, 1408)) + dot_nt(du_ref[...], wuf[pieces].reshape(256, 1408))
        part[:, :, cols] = dh.astype(BF).reshape(4, 128, 256)
    put(part, dh_out)
    tail_put.wait()
    for n in range(8):
        pieces, cols = pl.ds(n * 4, 4), pl.ds(n * 256, 256)
        tail_ref[:, :, cols] = dot_nt(act_ref[...], wdf[pieces].reshape(256, 1408)).astype(BF).reshape(4, 128, 256)
    put(tail_ref, out_out)
    for copy in puts:
        copy.wait()


def forward_call(pick, home, turns, x, t, g, cosine, sine, wq, wp, wd, wg, wu):
    ag = [dma(AG_SEMS), dma(AG_SEMS), ONE]
    return pl.pallas_call(
        forward_kernel,
        out_shape=(
            sds((4, 128, D), BF), sds((4, 2, 64, 512), BF), sds((4, 2, 64, 512), F32), sds((4, 2, 64, 512), F32),
            sds((4, 16, 256, 128), BF), sds((4, 128, D), BF), sds((32,) + wq.shape, BF), sds((32,) + wp.shape, BF),
            sds((128, D), F32), sds((4, 128, D), BF), sds((512, 1408), BF), sds((512, 1408), BF), sds((512, 1408), BF),
            sds((4, 128, D), BF), sds((4, 128, D), BF),
        ),
        in_specs=[spec(SM)] * 3 + [spec(VM)] * 5 + [spec(HB)] * 5,
        out_specs=(spec(HB),) * 8 + (spec(VM), spec(HB)) + (spec(VM),) * 3 + (spec(HB),) * 2,
        scratch_shapes=[
            vm((4, 128, D), BF), vm((4, 2, 64, 512), BF), vm((4, 2, 64, 512), F32), vm((4, 2, 64, 512), F32),
            vm((4, 16, 256, 128), BF), vm((4, 128, D), BF), vm((32,) + wq.shape, BF), vm((32,) + wp.shape, BF),
            vm((32,) + wd.shape, BF), vm((32,) + wg.shape, BF), vm((32,) + wu.shape, BF),
            vm((4, 128, D), BF), vm((512, 1408), F32), vm((512, 1408), F32),
            vm((4, 2, 64, 128), BF), vm((4, 64, 128), BF), vm((4, 64, 128), BF), vm((32, 4, 64, 128), BF), vm((32, 4, 64, 128), BF),
            vm((2, 512, 128), BF), vm((2, 512, 128), F32),
            vm((128, 512), BF), vm((4, 128, D), BF),
        ] + fold_scratch() + ag * 8 + [dma(3 * CHUNKS)] * 8 + [dma(12)],
        compiler_params=params(1),
        name="forward_rows",
    )(pick, home, turns, x, t, g, cosine, sine, wq, wp, wd, wg, wu)


def fold_scratch():
    return [vm((128, 2048), BF) for _ in range(4)] + [vm((2, 16, 32, 128), F32)]


def outer(dst, cols, lhs, rhs):
    for n in range(8):
        block = lhs[:, :, pl.ds(n * 256, 256)].reshape(512, 256)
        dst[pl.ds(n * 4, 4), :, cols] = dot_tn(block, rhs).astype(BF).reshape(4, 64, rhs.shape[1])


def backward_kernel(
    pick_ref, pair_ref, turn_ref, g_ref, dh_ref, tail_in, act_ref, hb_in, dg_in, du_in, mid_in, cot_ref, x_ref, cos_in, sin_in,
    q_in, o_in, inv_in, nat_in, wp_in, wq_in, a_in, out_in, pq_ref, pg_ref, pu_ref,
    grad_ref, out_ref, sq_ref, sp_ref, si_ref, sd_ref, gain_ref,
    xpart, xbuf, ypart, ybuf, rows, tail, hb, dg, du, ga, mid, cosine, sine, q, o, inv, wp, wq, nat0, nat1,
    dmid, dp, dkv, dnat, dqa, qt, gt, dl, dor, b0, b1, sb, b2, tb, vb,
    ds, dr, gs, gr, us, ur, ps, pr, ks, kr, js, jr, qs, qr, ns2, nr2, fs, fr, es, er, cs, cr, ss, sr, vs, vr, ls, ns, free,
):
    pc = Place()
    fetches = {}

    def fetch(name, src, dst, k):
        fetches[name] = pltpu.make_async_copy(src, dst, ls.at[k])
        fetches[name].start()

    def have(*names):
        for name in names:
            fetches.pop(name).wait()

    fetch("rows", dh_ref, rows, 0)
    fetch("tail", tail_in, tail, 1)
    fetch("mid", mid_in, mid, 2)
    fetch("hb", hb_in, hb, 3)
    fetch("dg", dg_in, dg, 4)
    fetch("du", du_in, du, 5)
    fetch("wp", wp_in, wp, 6)
    fetch("q", q_in, q, 7)
    fetch("o", o_in, o, 8)
    fetch("inv", inv_in, inv, 9)
    fetch("cos", cos_in, cosine, 10)
    fetch("sin", sin_in, sine, 11)
    fetch("wq", wq_in, wq, 12)
    order = (pc.w, pc.near_twin, pc.far, pc.far_twin)
    slots = (nat0, nat1)
    tiles = [pltpu.make_async_copy(nat_in.at[s], slots[n % 2], ns.at[n]) for n, s in enumerate(order)]
    tiles[0].start()
    tiles[1].start()
    greet(pc)

    def tell(k, wsh):
        peers = [pc.over(), pc.twin()] if wsh else ctx_peers(pc)
        for peer in peers:
            pl.semaphore_signal(free.at[k], inc=1, device_id=peer, device_id_type=MESH)

    def hear(k, wsh):
        pl.semaphore_wait(free.at[k], 2 if wsh else 5)

    def total(own, other):
        return own[...].astype(F32) + other[...].astype(F32)

    def to(ref):
        def finish(own, other):
            ref[...] = total(own, other)

        return finish

    gains = {}

    def to_part(name, ref, n, cols, piece):
        def finish(own, other):
            value = total(own, other)
            ref[:, n, cols] = value
            gains[name] = jnp.sum(value * piece[:, cols].astype(F32), -1, keepdims=True)

        return finish

    boxes = (b0, b1, sb, b2)
    wide = slice(0, 1408)

    def y_sum(lo, n, ssem, rsem, finish):
        cols = pl.ds(lo, n)
        return scatter_steps(pc, ypart.at[:, :, cols], ybuf.at[:, cols], ssem, rsem, finish)

    have("rows")
    fold = Fold(pc, rows, boxes, fs, fr, CHUNKS)
    fold.far_twin()
    fold.near_twin()
    have("hb", "dg")
    outer(ypart, wide, hb, dg[...])
    gate = y_sum(0, 1408, gs, gr, to_part("gate", si_ref, 0, pl.ds(0, 1408), pg_ref))
    next(gate)
    fold.far()
    have("tail", "du")
    outer(xpart, wide, tail, act_ref[...])
    down = scatter_steps(pc, xpart, xbuf, ds, dr, to(sd_ref))
    next(down)
    next(gate)
    fetch("out", out_in, tail, 13)
    state = {"y": False, "a": False}

    def lane_x():
        yield from down
        tell(0, False)
        outer(xpart, wide, hb, du[...])
        fetch("a", a_in, hb, 14)
        state["a"] = True
        hear(0, False)
        yield
        yield from scatter_steps(pc, xpart, xbuf, us, ur, to_part("up", si_ref, 1, pl.ds(0, 1408), pu_ref))

    def lane_y():
        yield from gate
        tell(2, False)
        hear(2, False)
        state["y"] = True

    xs, ys = lane_x(), lane_y()
    share = Share(pc, ga, ss, sr, 0, CHUNKS)
    have("mid")
    for k in range(CHUNKS):
        r = pl.ds(k * 32, 32)
        m = mid[r]
        weighted = turn(fold.total(k), turn_ref, 4, tb) * g_ref[1:2]
        scale = scale_of(m)
        mean = jnp.mean(weighted * m, -1, keepdims=True)
        dm = cot_ref[r].astype(F32) + scale * weighted - m * (scale * scale * scale) * mean
        dmid[r] = dm
        ga[pc.w, r] = turn(dm, turn_ref, 5, tb).astype(BF)
        share.send(k)
        next(ys, None)
    fold.wire.drain()
    tell(3, True)
    have("out", "wp", "q", "o", "inv", "cos", "sin")
    out_fold = Fold(pc, tail, boxes, es, er, CHUNKS)

    def put_out(k, value):
        r = pl.ds(k * 32, 32)
        out_ref[r] = mid[r] + turn(value, turn_ref, 7, tb)

    out_steps = out_fold.steps(put_out)

    def poll(n, part):
        if n == 0:
            next(ys, None)
            next(ys, None)
            next(xs, None)
        elif n == 1:
            share.relay(part)
            next(xs, None)
            next(xs, None)
        else:
            next(lanes["keys"], None)
            next(xs, None)
            if part % 2:
                next(lanes.get("proj"), None) if n == 3 else next(xs, None)

    rows_iota = lax.broadcasted_iota(jnp.int32, (256, 512), 0)
    ones = jnp.ones((8, 128), BF)

    def tile(j, keys_values, limit=None):
        queries, upward = qt[j], gt[j]
        e = jnp.exp(dot_nt(keys_values, queries))
        if limit is not None:
            e = jnp.where(rows_iota < limit, e, 0.0)
        dscore = (e * (dot_nt(keys_values, upward) - dl[j, 0:1])).astype(BF)
        return dot_tn(dscore, keys_values), dot_nn(dscore, queries) + dot_nn(e.astype(BF), upward)

    lanes = {}

    def attend(n):
        s, kv = order[n], slots[n % 2]
        if n == 1:
            share.arrive_twin()
        if n == 3:
            share.arrive_last()
            outer(ypart, pl.ds(1024, 512), ga, o[...].reshape(512, 512).astype(BF))
            lanes["proj"] = y_sum(1024, 512, ps, pr, to(sp_ref))
            next(lanes["proj"])
        dor[...] = dot_nn(ga[s], wp[...].reshape(D, 512)).reshape(2, 64, 512)
        for j in range(2):
            sums = []
            for m2 in range(4):
                cols = pl.ds(m2 * 128, 128)
                pair = q[s, j, :, cols].astype(F32)
                ratio = dor[j, :, cols] * inv[s, j, :, cols]
                prod = ratio * o[s, j, :, cols]
                for odd in (False, True):
                    place = pl.ds(m2 * 128 + (64 if odd else 0), 64)
                    qt[j, place] = head_tile(pair, odd, False).astype(BF)
                    gt[j, place] = head_tile(ratio, odd, True).astype(BF)
                    sums.append(head_tile(prod, odd, False))
            whole = jnp.concatenate(sums, 0)
            big = whole.astype(BF)
            rest = (whole - big.astype(F32)).astype(BF)
            dl[j] = dot_nt(ones, big) + dot_nt(ones, rest)
        dqa[...] = jnp.zeros_like(dqa)
        tiles[n].wait()

        def body(i, carry):
            which = pick_ref[0, s * 9 + i]
            dq1, dkv1 = tile(1, kv[i])
            dq2, dkv2 = tile(which, kv[pick_ref[1, s * 9 + i]], pick_ref[2, s * 9 + i])
            to_low = jnp.broadcast_to(which, dq2.shape) == 0
            dqa[0] += jnp.where(to_low, dq2, 0.0)
            dqa[1] += dq1 + jnp.where(to_low, 0.0, dq2)
            to_low = jnp.broadcast_to(which, dkv2.shape) == 0
            dnat[i] = (dkv1 + jnp.where(to_low, dkv2, 0.0)).reshape(4, 64, 128)
            dnat[15 - i] = jnp.where(to_low, 0.0, dkv2).reshape(4, 64, 128)
            return carry

        for part in range(4):
            lax.fori_loop(2 * part, 2 * part + 2, body, 0)
            poll(n, part)
        kt = pick_ref[1, s * 9 + 8]
        dq3, dkv3 = tile(1, kv[kt], pick_ref[2, s * 9 + 8])
        dqa[1] += dq3
        for t in range(8, 16):
            here = jnp.broadcast_to(kt, dkv3.shape) == t
            dnat[t] += jnp.where(here, dkv3, 0.0).reshape(4, 64, 128)
        if n + 2 < 4:
            tiles[n + 2].start()
        for j in range(2):
            for m2 in range(4):
                even = dqa[j, pl.ds(m2 * 128, 64)]
                odd = dqa[j, pl.ds(m2 * 128 + 64, 64)]
                both = jnp.where(upper_lanes(even.shape), pltpu.roll(odd, 64, 1), even) * 0.125
                turned = both * cosine[s, j] - swap_lanes(both) * sine[s, j]
                dp[s, j, :, pl.ds(m2 * 128, 128)] = turned.astype(BF)
        while not state["y"]:
            next(ys, None)

        def place_block(c, carry):
            for j in range(2):
                at = s * 64 + c * 2 + j
                block = dnat[pair_ref[0, at], pair_ref[1, at]].astype(BF)
                ypart[c, :, pl.ds((n * 2 + j) * 128, 128)] = block
            return carry

        lax.fori_loop(0, 32, place_block, 0)

    attend(0)
    attend(1)
    lanes["keys"] = y_sum(0, 512, ks, kr, to(dkv.at[:, pl.ds(0, 512)]))
    next(lanes["keys"])
    attend(2)
    attend(3)
    keys = y_sum(512, 512, js, jr, to(dkv.at[:, pl.ds(512, 512)]))
    next(keys)
    hear(3, True)
    next(out_steps)
    for _ in lanes["keys"]:
        next(keys, None)
    tell(6, False)
    while not state["a"]:
        next(xs)
    have("a")
    outer(ypart, pl.ds(0, 512), hb, dp[:, :, :, pl.ds(0, 512)].reshape(512, 512))
    hear(6, False)

    heads = y_sum(0, 512, qs, qr, to_part("heads", sq_ref, 0, pl.ds(0, 512), pq_ref))
    next(heads)
    next(out_steps)
    count = 0
    for _ in keys:
        count += 1
        next(lanes["proj"], None)
        if count % 2:
            next(xs, None)
        else:
            next(heads, None)
        if count % 4 == 0:
            next(out_steps, None)
    for _ in out_steps:
        next(xs, None)
    tell(4, True)
    for n, s in enumerate(order):
        for j in range(2):
            both = dkv[:, pl.ds((n * 2 + j) * 128, 128)]
            key_cosine, key_sine = key_only(cosine[s, j], sine[s, j])
            turned = both * key_cosine - swap_lanes(both) * key_sine
            dp[s, j, :, pl.ds(512, 128)] = turned.astype(BF)
    have("wq")

    def back(s):
        for n in range(8):
            columns = wq[pl.ds(n * 4, 4)].reshape(256, 640)
            rows[s, :, pl.ds(n * 256, 256)] = dot_nt(dp[s].reshape(128, 640), columns).astype(BF)

    hear(4, True)
    last = Fold(pc, rows, boxes, cs, cr, CHUNKS)
    back(pc.far_twin)
    last.far_twin()
    back(pc.near_twin)
    last.near_twin()
    back(pc.far)
    last.far()
    for _ in lanes["proj"]:
        next(xs, None)
    tell(5, False)
    outer(ypart, pl.ds(1024, 128), hb, dp[:, :, :, pl.ds(512, 128)].reshape(512, 128))
    hear(5, False)
    pair_sum = y_sum(1024, 128, ns2, nr2, to_part("pair", sq_ref, 0, pl.ds(512, 128), pq_ref))
    next(pair_sum)
    back(pc.w)
    for k in range(CHUNKS):
        next(pair_sum)
        r = pl.ds(k * 32, 32)
        x = x_ref[r].astype(F32)
        weighted = turn(last.total(k), turn_ref, 6, tb) * g_ref[0:1]
        scale = scale_of(x)
        mean = jnp.mean(weighted * x, -1, keepdims=True)
        grad_ref[r] = dmid[r] + scale * weighted - x * (scale * scale * scale) * mean
    last.wire.drain()
    run_all(pair_sum, heads, xs)
    first = gains["heads"] + gains["pair"]
    second = gains["gate"] + gains["up"]
    line = lax.broadcasted_iota(jnp.int32, (64, 128), 0)
    lane = lax.broadcasted_iota(jnp.int32, (64, 128), 1)
    both = jnp.where(lane == line, first, 0.0) + jnp.where(lane == line + 64, second, 0.0)
    vb[0] = jnp.broadcast_to(jnp.sum(both, 0, keepdims=True), (8, 128))
    wire = Wire(vs, vr)
    wire.send(0, vb.at[0], vb.at[1], pc.twin())
    wire.arrive(0, vb.at[1], pc.twin())
    vb[2] = vb[0] + vb[1]
    wire.send(1, vb.at[2], vb.at[3], pc.over())
    wire.arrive(1, vb.at[3], pc.over())
    gain_ref[pc.c] = vb[2] + vb[3]

    def gain_at(v, dx, dz):
        return gain_ref.at[pc.piece(0, v, dx, dz)]

    steps = (1, -1, 2)
    wire.send(2, gain_at(0, 0, 0), gain_at(0, 0, 0), pc.mate())
    wire.arrive(2, gain_at(1, 0, 0), pc.mate())
    for v in (0, 1):
        for i, d in enumerate(steps):
            wire.send(3 + v * 3 + i, gain_at(v, 0, 0), gain_at(v, 0, 0), pc.step("x", d))
    for v in (0, 1):
        for i, d in enumerate(steps):
            wire.arrive(3 + v * 3 + i, gain_at(v, -d if d < 2 else 2, 0), pc.step("x", -d if d < 2 else 2))
    for v in (0, 1):
        for m, dx in enumerate((0, 1, -1, 2)):
            for i, d in enumerate(steps):
                wire.send(9 + (v * 4 + m) * 3 + i, gain_at(v, dx, 0), gain_at(v, dx, 0), pc.step("z", d))
    for v in (0, 1):
        for m, dx in enumerate((0, 1, -1, 2)):
            for i, d in enumerate(steps):
                there = -d if d < 2 else 2
                wire.arrive(9 + (v * 4 + m) * 3 + i, gain_at(v, dx, there), pc.step("z", there))
    wire.drain()


def backward_call(*args):
    rs = [dma(RS_SEMS)] * 2
    small = [dma(3 * CHUNKS)] * 2
    return pl.pallas_call(
        backward_kernel,
        out_shape=(
            sds((128, D), F32), sds((128, D), F32), sds((64, 1, 640), F32), sds((64, 512), F32),
            sds((64, 2, 1408), F32), sds((64, 1408), F32), sds((32, 8, 128), F32),
        ),
        in_specs=[spec(SM)] * 3 + [spec(VM)] + [spec(HB)] * 2 + [spec(VM)] + [spec(HB)] * 4 + [spec(VM)] * 2
        + [spec(HB)] * 10 + [spec(VM)] * 3,
        out_specs=(spec(VM),) * 7,
        scratch_shapes=[
            vm((32, 64, 1408), BF), vm((31 * 64, 1408), BF), vm((32, 64, 1536), BF), vm((31 * 64, 1536), BF),
            vm((4, 128, D), BF), vm((4, 128, D), BF), vm((4, 128, D), BF), vm((512, 1408), BF), vm((512, 1408), BF),
            vm((4, 128, D), BF), vm((128, D), F32), vm((4, 2, 64, 128), F32), vm((4, 2, 64, 128), F32),
            vm((4, 2, 64, 512), BF), vm((4, 2, 64, 512), F32), vm((4, 2, 64, 512), F32), vm((32, 64, 512), BF),
            vm((32, 64, 640), BF), vm((16, 256, 128), BF), vm((16, 256, 128), BF),
            vm((128, D), F32), vm((4, 2, 64, 640), BF), vm((64, 1024), F32), vm((16, 4, 64, 128), F32),
            vm((2, 512, 128), F32), vm((2, 512, 128), BF), vm((2, 512, 128), BF), vm((2, 8, 512), F32), vm((2, 64, 512), F32),
        ] + fold_scratch() + [vm((4, 8, 128), F32)]
        + rs * 8 + small * 4 + [dma(33)] * 2 + [dma(16), dma(4), pltpu.SemaphoreType.REGULAR((7,))],
        compiler_params=params(2),
        name="backward_rows",
    )(*args)


def rope_tables(positions):
    half_width = HD // 2
    inverse = ROPE_BASE ** (-(jnp.arange(half_width, dtype=F32) * 2.0 / HD))
    angles = positions.astype(F32)[..., None] * inverse
    cosine, sine = jnp.cos(angles), jnp.sin(angles)
    signed = jnp.concatenate([-sine, sine], -1)
    return (jnp.concatenate([cosine] * 4, -1), jnp.concatenate([signed] * 2, -1))


def adamw_step(master, first_state, second_state, gradient, rate_value):
    first_new = BETA_FIRST * first_state + (1.0 - BETA_FIRST) * gradient
    second_new = BETA_SECOND * second_state + (1.0 - BETA_SECOND) * gradient * gradient
    first_fix = 1.0 - BETA_FIRST**STEP
    second_fix = 1.0 - BETA_SECOND**STEP
    update = first_new / first_fix / (jnp.sqrt(second_new / second_fix) + ADAM_EPS)
    return (master - rate_value * (update + WEIGHT_DECAY * master), first_new, second_new)


def per_device(
    tokens, cotangent, block_pairs, offsets,
    qkv_master, qkv_first, qkv_second,
    proj_master, proj_first, proj_second,
    inner_master, inner_first, inner_second,
    down_master, down_first, down_second,
    gains, gain_first, gain_second,
):
    offsets = offsets.astype(jnp.int32)
    shift = offsets * 64
    g1, g2 = gains[:, 0][None], gains[:, 1][None]
    qkv_piece = qkv_master[:, 0].astype(BF)
    gate_piece, up_piece = inner_master[:, 0].astype(BF), inner_master[:, 1].astype(BF)
    down_piece = down_master.astype(BF).T
    proj_piece = proj_master.astype(BF).T
    place = lax.axis_index("ctx").astype(jnp.int32)
    pick, home, pairs, turns = table_call(block_pairs.reshape(4, 64).astype(jnp.int32), offsets, place[None])
    own_pairs = lax.dynamic_index_in_dim(block_pairs, place, 1, keepdims=False)
    positions = (own_pairs[:, :, None] * BLK + jnp.arange(BLK, dtype=jnp.int32)).reshape(4, 2, 64)
    cosine, sine = rope_tables(positions)

    (a_all, q, o, inverse, nat, tail_all, qkv_full, proj_full, middle, hb, act, dgate, dup, dh, out_part) = forward_call(
        pick, home, turns, tokens[0], cotangent[0], jnp.concatenate([g1, g2], 0), cosine, sine,
        qkv_piece, proj_piece, down_piece, gate_piece, up_piece,
    )
    input_grad, output, qkv_sum, proj_sum, inner_sum, down_sum, gain_sums = backward_call(
        pick, pairs, turns, jnp.concatenate([g1, g2], 0), dh, tail_all, act, hb,
        dgate, dup, middle, cotangent[0], tokens[0], cosine, sine, q, o, inverse, nat, proj_full, qkv_full, a_all, out_part, qkv_piece, gate_piece, up_piece,
    )
    gain_sums = gain_sums[:, 0]
    gain_grad = (
        jnp.stack([jnp.roll(gain_sums[:, :64].reshape(D), shift[0]), jnp.roll(gain_sums[:, 64:].reshape(D), shift[2])], 1) / gains
    )

    rate_rows = 2.0 / math.sqrt(D)
    rate_proj = 1.0
    rate_down = 2.0 / math.sqrt(FF)
    qkv_out = adamw_step(qkv_master, qkv_first, qkv_second, qkv_sum, rate_rows)
    proj_out = adamw_step(proj_master, proj_first, proj_second, proj_sum.T, rate_proj)
    inner_out = adamw_step(inner_master, inner_first, inner_second, inner_sum, rate_rows)
    down_out = adamw_step(down_master, down_first, down_second, down_sum.T, rate_down)
    gain_out = adamw_step(gains, gain_first, gain_second, gain_grad, GAIN_RATE)
    return (output[None], input_grad[None], *qkv_out, *proj_out, *inner_out, *down_out, *gain_out)


def solution(mesh):
    rows, every = P("wsh", "ctx", None), P()
    qkv, inner, cols = P("ctx", "wsh", None), P("ctx", None, "wsh"), P("wsh", "ctx")
    return jax.shard_map(
        per_device,
        mesh=mesh,
        in_specs=(rows, rows, every, every) + (qkv,) * 3 + (cols,) * 3 + (inner,) * 3 + (cols,) * 3 + (every,) * 3,
        out_specs=(rows, rows) + (qkv,) * 3 + (cols,) * 3 + (inner,) * 3 + (cols,) * 3 + (every,) * 3,
        check_vma=False,
    )
```

```python
import math

import jax
import jax.numpy as jnp
from jax import lax
from jax.experimental import pallas as pl
from jax.experimental.pallas import tpu as pltpu
from jax.sharding import PartitionSpec as P
MESH = pl.DeviceIdType.MESH
F32, BF = jnp.float32, jnp.bfloat16
VM, HB, SM = pltpu.VMEM, pl.ANY, pltpu.SMEM

D = 2048
HD = 64
FF = 5632
BLK = 64
STEP = 7
NORM_EPS = 1e-05
ROPE_BASE = 10000.0
BETA_FIRST = 0.5
BETA_SECOND = 0.5
ADAM_EPS = 1e-08
WEIGHT_DECAY = 0.1
GAIN_RATE = 0.4

AG_SEMS = 81
RS_SEMS = 81


class Place:
    def __init__(self):
        c = lax.axis_index("ctx")
        w = lax.axis_index("wsh")
        self.c, self.w = c, w
        self.yl, self.yh, self.co = c // 16, w // 2, w % 2
        x, z = (c // 4) % 4, c % 4
        self.y16 = [self.yl * 16, 16 - self.yl * 16]
        self.x4 = {k: ((x + k + 4) % 4) * 4 for k in (-2, -1, 0, 1, 2)}
        self.z1 = {k: (z + k + 4) % 4 for k in (-2, -1, 0, 1, 2)}
        self.far = (1 - self.yh) * 2 + self.co
        self.near_twin = self.yh * 2 + 1 - self.co
        self.far_twin = (1 - self.yh) * 2 + 1 - self.co

    def step(self, axis, k):
        if axis == "x":
            return (self.y16[0] + self.x4[k] + self.z1[0], self.w)
        return (self.y16[0] + self.x4[0] + self.z1[k], self.w)

    def mate(self):
        return (self.y16[1] + self.x4[0] + self.z1[0], self.w)

    def over(self):
        return (self.c, self.far)

    def twin(self):
        return (self.c, self.near_twin)

    def piece(self, half, v, dp, dq):
        if half == 0:
            return self.y16[v] + self.x4[dp] + self.z1[dq]
        return self.y16[v] + self.x4[dq] + self.z1[dp]


def ctx_peers(place):
    return [place.step("x", 1), place.step("x", -1), place.step("z", 1), place.step("z", -1), place.mate()]


def greet(place):
    bar = pltpu.get_barrier_semaphore()
    peers = ctx_peers(place) + [place.over(), place.twin(), place.step("x", 2), place.step("z", 2)]
    for peer in peers:
        pl.semaphore_signal(bar, inc=1, device_id=peer, device_id_type=MESH)
    pl.semaphore_wait(bar, len(peers))


class Wire:
    def __init__(self, ssem, rsem):
        self.ssem, self.rsem, self.sent = ssem, rsem, []

    def send(self, k, src, dst, to):
        cp = pltpu.make_async_remote_copy(src, dst, self.ssem.at[k], self.rsem.at[k], device_id=to, device_id_type=MESH)
        cp.start()
        self.sent.append(cp)

    def arrive(self, k, view, frm):
        pltpu.make_async_remote_copy(view, view, self.ssem.at[k], self.rsem.at[k], device_id=frm, device_id_type=MESH).wait_recv()

    def drain(self):
        for cp in self.sent:
            cp.wait_send()
        self.sent = []


AXES = (("x", "z"), ("z", "x"))
GROUPS = (0, -1, 1, 2)


def gather_steps(pc, src, dst, ssem, rsem, lsem, late=False):
    wire = Wire(ssem, rsem)
    R = src.shape[0]
    H, S = R // 2, R // 4

    def part(v, h, dp, dq, lo=0, n=None):
        return dst.at[pc.piece(h, v, dp, dq), pl.ds(h * H + lo, H if n is None else n)]

    def key(v, h, k):
        return (v * 2 + h) * 20 + k

    local = pltpu.make_async_copy(src, dst.at[pc.c], lsem)
    local.start()
    both = (0,) if late else (0, 1)

    def cross(h, gi, d):
        if late:
            k = 40 + (h * 4 + gi) * 4 + (0, 2, 1, 3)[d + 1]
            view = part(0, h, GROUPS[gi], d)
            if gi == 0 and d == 0:
                wire.send(k, src.at[pl.ds(h * H, H)], view, pc.mate())
            else:
                wire.send(k, view, view, pc.mate())

    if not late:
        wire.send(80, src, dst.at[pc.c], pc.mate())

    def first(v, h):
        A, B = AXES[h]
        view = src.at[pl.ds(h * H, H)] if v == 0 else part(v, h, 0, 0)
        there = part(v, h, 0, 0)
        wire.send(key(v, h, 0), view, there, pc.step(A, 1))
        wire.send(key(v, h, 1), view, there, pc.step(A, -1))
        wire.send(key(v, h, 4), view, there, pc.step(B, 1))
        wire.send(key(v, h, 5), view, there, pc.step(B, -1))

    def along(v, h, gi):
        A, B = AXES[h]
        view = part(v, h, GROUPS[gi], 0)
        wire.send(key(v, h, 4 + 4 * gi), view, view, pc.step(B, 1))
        wire.send(key(v, h, 5 + 4 * gi), view, view, pc.step(B, -1))

    def spread1(v, h):
        A, B = AXES[h]
        wire.arrive(key(v, h, 0), part(v, h, -1, 0), pc.step(A, -1))
        s = part(v, h, -1, 0, 0, S)
        wire.send(key(v, h, 2), s, s, pc.step(A, 1))
        along(v, h, 1)
        wire.arrive(key(v, h, 1), part(v, h, 1, 0), pc.step(A, 1))
        s = part(v, h, 1, 0, S, S)
        wire.send(key(v, h, 3), s, s, pc.step(A, -1))
        along(v, h, 2)

    def spread2(v, h):
        A, B = AXES[h]
        wire.arrive(key(v, h, 2), part(v, h, 2, 0, 0, S), pc.step(A, -1))
        wire.arrive(key(v, h, 3), part(v, h, 2, 0, S, S), pc.step(A, 1))
        along(v, h, 3)

    def pass_on(v, h, gi):
        A, B = AXES[h]
        g = GROUPS[gi]
        k = 4 + 4 * gi
        wire.arrive(key(v, h, k), part(v, h, g, -1), pc.step(B, -1))
        s = part(v, h, g, -1, 0, S)
        wire.send(key(v, h, k + 2), s, s, pc.step(B, 1))
        wire.arrive(key(v, h, k + 1), part(v, h, g, 1), pc.step(B, 1))
        s = part(v, h, g, 1, S, S)
        wire.send(key(v, h, k + 3), s, s, pc.step(B, -1))

    for h in (0, 1):
        first(0, h)
        cross(h, 0, 0)
    yield
    if not late:
        wire.arrive(80, dst.at[pc.piece(0, 1, 0, 0)], pc.mate())
        for h in (0, 1):
            first(1, h)
        yield
    for v in both:
        for h in (0, 1):
            spread1(v, h)
            cross(h, 1, 0)
            cross(h, 2, 0)
        yield
    for v in both:
        for h in (0, 1):
            spread2(v, h)
            cross(h, 3, 0)
        yield
    for gi in range(4):
        for v in both:
            for h in (0, 1):
                pass_on(v, h, gi)
                cross(h, gi, -1)
                cross(h, gi, 1)
            yield
    for gi in range(4):
        for v in both:
            for h in (0, 1):
                A, B = AXES[h]
                k = 4 + 4 * gi
                wire.arrive(key(v, h, k + 2), part(v, h, GROUPS[gi], 2, 0, S), pc.step(B, -1))
                wire.arrive(key(v, h, k + 3), part(v, h, GROUPS[gi], 2, S, S), pc.step(B, 1))
                cross(h, gi, 2)
        yield
    if late:
        for gi in range(4):
            for h in (0, 1):
                for d in (-1, 0, 1, 2):
                    k = 40 + (h * 4 + gi) * 4 + (0, 2, 1, 3)[d + 1]
                    wire.arrive(k, part(1, h, GROUPS[gi], d), pc.mate())
            yield
    wire.drain()
    local.wait()


def scatter_steps(pc, part, buf, ssem, rsem, finish):
    wire = Wire(ssem, rsem)
    R = part.shape[1]
    H, S = R // 2, R // 4

    def key(v, h, k):
        return (v * 2 + h) * 20 + k

    def box(v, h, gi, which):
        base = ((v * 2 + h) * 5 + gi) * (R + H)
        off, n = ((0, S), (S, S), (2 * S, H), (2 * S + H, H))[which]
        return buf.at[pl.ds(base + off, n)]

    def mine(v, h, dp, dq, lo=0, n=None):
        return part.at[pc.piece(h, v, dp, dq), pl.ds(h * H + lo, H if n is None else n)]

    def add(to, *more):
        total = to[...].astype(F32)
        for m in more:
            total = total + m[...].astype(F32)
        to[...] = total.astype(BF)

    def where(stage, gi, d):
        return (GROUPS[gi], d) if stage == 1 else (d, 0)

    def ring_axis(stage, h):
        return AXES[h][1] if stage == 1 else AXES[h][0]

    def raw(v, h, gi, stage):
        X = ring_axis(stage, h)
        k = 4 * gi
        wire.send(key(v, h, k), mine(v, h, *where(stage, gi, -2), 0, S), box(v, h, gi, 0), pc.step(X, -1))
        wire.send(key(v, h, k + 1), mine(v, h, *where(stage, gi, 2), S, S), box(v, h, gi, 1), pc.step(X, 1))

    def mid(v, h, gi, stage):
        X = ring_axis(stage, h)
        k = 4 * gi
        wire.arrive(key(v, h, k), box(v, h, gi, 0), pc.step(X, 1))
        add(mine(v, h, *where(stage, gi, -1), 0, S), box(v, h, gi, 0))
        wire.send(key(v, h, k + 2), mine(v, h, *where(stage, gi, -1)), box(v, h, gi, 2), pc.step(X, -1))
        wire.arrive(key(v, h, k + 1), box(v, h, gi, 1), pc.step(X, -1))
        add(mine(v, h, *where(stage, gi, 1), S, S), box(v, h, gi, 1))
        wire.send(key(v, h, k + 3), mine(v, h, *where(stage, gi, 1)), box(v, h, gi, 3), pc.step(X, 1))

    def end(v, h, gi, stage):
        X = ring_axis(stage, h)
        k = 4 * gi
        wire.arrive(key(v, h, k + 2), box(v, h, gi, 2), pc.step(X, 1))
        wire.arrive(key(v, h, k + 3), box(v, h, gi, 3), pc.step(X, -1))
        add(mine(v, h, *where(stage, gi, 0)), box(v, h, gi, 2), box(v, h, gi, 3))

    order = (3, 1, 2, 0)
    for gi in order:
        for v in (1, 0):
            for h in (0, 1):
                raw(v, h, gi, 1)
    yield
    for gi in order:
        for v in (1, 0):
            for h in (0, 1):
                mid(v, h, gi, 1)
            yield
    for v in (1, 0):
        for gi in order:
            for h in (0, 1):
                end(v, h, gi, 1)
            if gi == 3:
                for h in (0, 1):
                    raw(v, h, 4, 2)
            yield
        if v == 1:
            for h in (0, 1):
                mid(1, h, 4, 2)
            yield
    for h in (0, 1):
        end(1, h, 4, 2)
    theirs = part.at[pc.piece(0, 1, 0, 0)]
    tail = buf.at[pl.ds(30 * R, R)]
    wire.send(80, theirs, tail, pc.mate())
    yield
    for h in (0, 1):
        mid(0, h, 4, 2)
    yield
    for h in (0, 1):
        end(0, h, 4, 2)
    yield
    wire.arrive(80, tail, pc.mate())
    finish(part.at[pc.c], tail)
    wire.drain()


def in_turn(*gens, lead=3):
    live, waiting = [gens[0]], list(gens[1:])
    count = 0
    while live:
        for g in list(live):
            try:
                next(g)
                yield
            except StopIteration:
                live.remove(g)
        count += 1
        if waiting and (count % lead == 0 or not live):
            live.append(waiting.pop(0))


def run_all(*gens):
    live = list(gens)
    while live:
        for g in list(live):
            try:
                next(g)
            except StopIteration:
                live.remove(g)


class Fold:
    def __init__(self, pc, part, boxes, ssem, rsem, chunks):
        self.wire = Wire(ssem, rsem)
        self.pc, self.part, self.chunks = pc, part, chunks
        self.b0, self.b1, self.sb, self.b2 = boxes
        n = part.shape[1] // chunks
        self.rows = [pl.ds(k * n, n) for k in range(chunks)]

    def far_twin(self):
        for k, r in enumerate(self.rows):
            self.wire.send(k, self.part.at[self.pc.far_twin, r], self.b0.at[r], self.pc.twin())

    def near_twin(self):
        for k, r in enumerate(self.rows):
            self.wire.send(self.chunks + k, self.part.at[self.pc.near_twin, r], self.b1.at[r], self.pc.twin())

    def far(self):
        for k, r in enumerate(self.rows):
            self.wire.arrive(k, self.b0.at[r], self.pc.twin())
            self.sb[r] = (self.part[self.pc.far, r].astype(F32) + self.b0[r].astype(F32)).astype(BF)
            self.wire.send(2 * self.chunks + k, self.sb.at[r], self.b2.at[r], self.pc.over())

    def total(self, k):
        r = self.rows[k]
        self.wire.arrive(self.chunks + k, self.b1.at[r], self.pc.twin())
        near = self.part[self.pc.w, r].astype(F32) + self.b1[r].astype(F32)
        self.wire.arrive(2 * self.chunks + k, self.b2.at[r], self.pc.over())
        return near + self.b2[r].astype(F32)

    def steps(self, each):
        self.far_twin()
        self.near_twin()
        yield
        self.far()
        yield
        for k in range(self.chunks):
            each(k, self.total(k))
            yield
        self.wire.drain()


class Share:
    def __init__(self, pc, dst, ssem, rsem, base, chunks):
        self.wire = Wire(ssem, rsem)
        self.pc, self.dst, self.base, self.chunks = pc, dst, base, chunks
        self.n = dst.shape[1] // chunks

    def at(self, w, k):
        return self.dst.at[w, pl.ds(k * self.n, self.n)]

    def send(self, k):
        pc = self.pc
        self.wire.send(self.base + k, self.at(pc.w, k), self.at(pc.w, k), pc.over())
        self.wire.send(self.base + self.chunks + k, self.at(pc.w, k), self.at(pc.w, k), pc.twin())

    def relay(self, k):
        far = self.at(self.pc.far, k)
        self.wire.arrive(self.base + k, far, self.pc.over())
        self.wire.send(self.base + 2 * self.chunks + k, far, far, self.pc.twin())

    def arrive_twin(self):
        for k in range(self.chunks):
            self.wire.arrive(self.base + self.chunks + k, self.at(self.pc.near_twin, k), self.pc.twin())

    def arrive_last(self):
        for k in range(self.chunks):
            self.wire.arrive(self.base + 2 * self.chunks + k, self.at(self.pc.far_twin, k), self.pc.twin())
        self.wire.drain()

    def finish_steps(self):
        for k in range(self.chunks):
            self.relay(k)
            yield
        self.arrive_twin()
        self.arrive_last()


def turn(value, table, row, buf):
    count = value.shape[1] // 128
    swapped = [pltpu.roll(value[:, m * 128 : (m + 1) * 128], 64, 1) for m in range(count)]
    low = lax.broadcasted_iota(jnp.int32, swapped[0].shape, 1) < 64
    for m in range(count):
        buf[0, m] = value[:, m * 128 : (m + 1) * 128]
        buf[1, m] = jnp.where(low, swapped[m], swapped[(m + 1) % count])
    odd = table[row, count]
    return jnp.concatenate([buf[odd, table[row, m]] for m in range(count)], axis=1)


def dma(n):
    return pltpu.SemaphoreType.DMA((n,))


def params(cid):
    return pltpu.CompilerParams(collective_id=cid, has_side_effects=True, vmem_limit_bytes=62 << 20)


def vm(shape, dtype):
    return pltpu.VMEM(shape, dtype)


def sds(shape, dtype):
    return jax.ShapeDtypeStruct(shape, dtype)


def spec(space):
    return pl.BlockSpec(memory_space=space)


CHUNKS = 4
ONE = pltpu.SemaphoreType.DMA(())


def upper_lanes(shape):
    return lax.broadcasted_iota(jnp.int32, shape, 1) >= 64


def head_tile(pair, odd, upper):
    moved = pair if odd == upper else pltpu.roll(pair, 64, 1)
    lanes = upper_lanes(pair.shape)
    return jnp.where(lanes if upper else jnp.logical_not(lanes), moved, 0.0)


def dot_nt(a, b):
    return lax.dot_general(a, b, (((1,), (1,)), ((), ())), preferred_element_type=F32)


def dot_nn(a, b):
    return lax.dot_general(a, b, (((1,), (0,)), ((), ())), preferred_element_type=F32)


def dot_tn(a, b):
    return lax.dot_general(a, b, (((0,), (0,)), ((), ())), preferred_element_type=F32)


def table_kernel(pair_ref, off_ref, at_ref, pick_ref, home_ref, out_ref, turn_ref):
    def slot(c, carry):
        for s in range(4):
            for j in range(2):
                b = pair_ref[s, c * 2 + j]
                home_ref[0, s * 64 + b] = c
                home_ref[1, s * 64 + b] = j
                out_ref[0, s * 64 + c * 2 + j] = b >> 2
                out_ref[1, s * 64 + c * 2 + j] = b & 3
        return carry

    lax.fori_loop(0, 32, slot, 0)
    at = at_ref[0]
    for s in range(4):
        low = pair_ref[s, 2 * at]
        m = low >> 2
        for i in range(8):
            pick_ref[0, s * 9 + i] = jnp.where(i <= m, 0, 1)
            pick_ref[1, s * 9 + i] = jnp.where(i <= m, i, 15 - i)
            pick_ref[2, s * 9 + i] = jnp.where(i == m, (low - 4 * m + 1) * 64, 256)
        pick_ref[0, s * 9 + 8] = 1
        pick_ref[1, s * 9 + 8] = 15 - m
        pick_ref[2, s * 9 + 8] = (4 * m - low + 4) * 64
    for row, (which, sign) in enumerate(((0, -1), (3, -1), (1, 1), (2, -1), (2, 1), (1, -1), (0, 1), (3, 1))):
        pieces = (off_ref[which] * sign + 32) & 31
        for n in range(16):
            turn_ref[row, n] = (n + 32 - ((pieces + 1) >> 1)) & 15
        turn_ref[row, 16] = pieces & 1


def table_call(pairs, offsets, place):
    return pl.pallas_call(
        table_kernel,
        out_shape=tuple(sds(shape, jnp.int32) for shape in ((3, 36), (2, 256), (2, 256), (8, 17))),
        in_specs=[spec(SM)] * 3,
        out_specs=(spec(SM),) * 4,
        name="tables",
    )(pairs, offsets, place)


def scale_of(v):
    return lax.rsqrt(jnp.mean(v * v, -1, keepdims=True) + NORM_EPS)


def swap_lanes(v):
    parts = []
    for m in range(v.shape[1] // 128):
        part = v[:, m * 128 : (m + 1) * 128]
        first = (lax.broadcasted_iota(jnp.int32, part.shape, 1) % 64) < 32
        parts.append(jnp.where(first, pltpu.roll(part, 96, 1), pltpu.roll(part, 32, 1)))
    return parts[0] if len(parts) == 1 else jnp.concatenate(parts, 1)


def key_only(cosine, sine):
    up = upper_lanes(cosine.shape)
    return jnp.where(up, 1.0, cosine), jnp.where(up, 0.0, sine)


def forward_kernel(
    pick_ref, home_ref, turn_ref, x_ref, t_ref, g_ref, cos_ref, sin_ref, wq_ref, wp_ref, wd_ref, wg_ref, wu_ref,
    a_out, q_out, o_out, inv_out, nat_out, tail_out, wq_out, wp_out, mid_ref, hb_out, act_ref, dg_ref, du_ref, dh_out, out_out,
    a_ref, q_ref, o_ref, inv_ref, nat_ref, tail_ref, wqf, wpf, wdf, wgf, wuf, hb_ref, gate, dact,
    kv, kva, kvb, kvga, kvgb, qt, acc, ob, part, b0, b1, sb, b2, tb,
    qs, qr, ql, ws, wr, wl, ks, kr, kl, js, jr, jl, ps, pr, pll, ds, dr, dl, gs, gr, gl, us, ur, ul, ss, sr, ts, tr, hs, hr, fs, fr, os,
):
    pc = Place()
    greet(pc)
    puts = []

    def put(src, dst):
        puts.append(pltpu.make_async_copy(src, dst, os.at[len(puts)]))
        puts[-1].start()

    done = {"down": False, "gate": False}

    def flagged(name, steps):
        yield from steps
        done[name] = True

    pair_cols, head_cols = pl.ds(512, 128), pl.ds(0, 512)
    joined = gather_steps(pc, wq_ref.at[:, pair_cols], wqf.at[:, :, pair_cols], qs, qr, ql)
    heads_in = gather_steps(pc, wq_ref.at[:, head_cols], wqf.at[:, :, head_cols], ws, wr, wl)
    order = (pc.far_twin, pc.far, pc.near_twin, pc.w)
    keys = [gather_steps(pc, kva, kvga, ks, kr, kl), gather_steps(pc, kvb, kvgb, js, jr, jl)]
    proj = gather_steps(pc, wp_ref, wpf, ps, pr, pll)
    big = in_turn(
        flagged("down", gather_steps(pc, wd_ref, wdf, ds, dr, dl, late=True)),
        flagged("gate", gather_steps(pc, wg_ref, wgf, gs, gr, gl)),
        gather_steps(pc, wu_ref, wuf, us, ur, ul),
    )
    next(joined)
    rows_share = Share(pc, a_ref, ss, sr, 0, CHUNKS)
    for k in range(CHUNKS):
        rows = pl.ds(k * 32, 32)
        x = x_ref[rows].astype(F32)
        a_ref[pc.w, rows] = turn(x * scale_of(x) * g_ref[0:1], turn_ref, 0, tb).astype(BF)
        rows_share.send(k)
    next(joined)
    for k in range(CHUNKS):
        rows = pl.ds(k * 32, 32)
        tail_ref[pc.w, rows] = turn(t_ref[rows].astype(F32), turn_ref, 1, tb).astype(BF)
    next(big)
    next(heads_in)
    run_all(joined, rows_share.finish_steps())
    next(big)
    next(proj)
    put(a_ref, a_out)
    a = a_ref[...].reshape(512, D)
    cosine = cos_ref[...].reshape(512, 128)
    sine = sin_ref[...].reshape(512, 128)
    last = dot_nn(a, wqf[:, :, pl.ds(512, 128)].reshape(D, 128))
    key_cosine, key_sine = key_only(cosine, sine)
    kv[...] = (last * key_cosine + swap_lanes(last) * key_sine).astype(BF).reshape(4, 2, 64, 128)
    for n, s in enumerate(order):
        (kva, kvb)[n // 2][pl.ds(n % 2 * 2, 2)] = kv[s]
    next(keys[0])
    next(heads_in)
    next(keys[0])
    next(keys[1])
    next(proj)
    tail_share = Share(pc, tail_ref, ts, tr, 0, CHUNKS)
    for k in range(CHUNKS):
        tail_share.send(k)
    tail = tail_share.finish_steps()
    run_all(heads_in, keys[0])
    put(wqf, wq_out)
    for n in range(2):
        next(keys[1])
        heads = dot_nn(a, wqf[:, :, pl.ds(n * 256, 256)].reshape(D, 256))
        turned = swap_lanes(heads)
        for m in range(2):
            cols = slice(m * 128, (m + 1) * 128)
            out = (heads[:, cols] * cosine + turned[:, cols] * sine).astype(BF).astype(F32) * 0.125
            q_ref[:, :, :, pl.ds(n * 256 + m * 128, 128)] = out.astype(BF).reshape(4, 2, 64, 128)
    put(q_ref, q_out)

    def poll(count):
        for _ in range(count):
            next(proj, None)
            next(big, None)
        next(tail, None)

    lanes = lax.broadcasted_iota(jnp.int32, (512, 256), 1)
    wide = lax.broadcasted_iota(jnp.int32, (256, 128), 1) < 64

    def tile(queries, keys_values, limit=None):
        e = jnp.exp(dot_nt(queries, keys_values))
        if limit is not None:
            e = jnp.where(lanes < limit, e, 0.0)
        ones_values = jnp.where(wide, jnp.ones_like(keys_values), keys_values)
        return dot_nn(e.astype(BF), ones_values)

    def attend(n):
        s, gathered, slot = order[n], (kvga, kvgb)[n // 2], n % 2 * 2
        if n == 2:
            run_all(keys[1])
        for j in range(2):
            for m in range(4):
                pair = q_ref[s, j, :, pl.ds(m * 128, 128)].astype(F32)
                qt[j, pl.ds(m * 128, 64)] = head_tile(pair, False, False).astype(BF)
                qt[j, pl.ds(m * 128 + 64, 64)] = head_tile(pair, True, False).astype(BF)

        def settle(t, carry):
            for r in range(4):
                at = s * 64 + t * 4 + r
                nat_ref[s, t, pl.ds(r * 64, 64)] = gathered[home_ref[0, at], slot + home_ref[1, at]]
            return carry

        lax.fori_loop(0, 16, settle, 0)
        acc[...] = jnp.zeros_like(acc)

        def body(i, carry):
            which = pick_ref[0, s * 9 + i]
            high_part = tile(qt[1], nat_ref[s, i])
            picked = tile(qt[which], nat_ref[s, pick_ref[1, s * 9 + i]], pick_ref[2, s * 9 + i])
            to_low = jnp.broadcast_to(which, picked.shape) == 0
            acc[0] += jnp.where(to_low, picked, 0.0)
            acc[1] += high_part + jnp.where(to_low, 0.0, picked)
            return carry

        for part in range(4):
            lax.fori_loop(2 * part, 2 * part + 2, body, 0)
            if n < 2:
                next(keys[1], None)
                next(keys[1], None)
            poll(2)
        acc[1] += tile(qt[1], nat_ref[s, pick_ref[1, s * 9 + 8]], pick_ref[2, s * 9 + 8])
        for j in range(2):
            for m2 in range(4):
                even = acc[j, pl.ds(m2 * 128, 64)]
                odd = acc[j, pl.ds(m2 * 128 + 64, 64)]
                up = upper_lanes(even.shape)
                bottom = jnp.where(up, pltpu.roll(odd, 64, 1), even)
                top = jnp.where(up, odd, pltpu.roll(even, 64, 1))
                inverse = 1.0 / bottom
                cols = pl.ds(m2 * 128, 128)
                inv_ref[s, j, :, cols] = inverse
                o_ref[s, j, :, cols] = top * inverse
                ob[pl.ds(j * 64, 64), cols] = (top * inverse).astype(BF)
        poll(2)

    def project(s):
        for n in range(8):
            columns = wpf[pl.ds(n * 4, 4)].reshape(256, 512)
            part[s, :, pl.ds(n * 256, 256)] = dot_nt(ob[...], columns).astype(BF)

    fold = Fold(pc, part, (b0, b1, sb, b2), fs, fr, CHUNKS)
    attend(0)
    run_all(proj)
    put(wpf, wp_out)
    project(pc.far_twin)
    fold.far_twin()
    attend(1)
    project(pc.far)
    fold.far()
    attend(2)
    project(pc.near_twin)
    fold.near_twin()
    attend(3)
    project(pc.w)
    run_all(tail)
    tail_put = pltpu.make_async_copy(tail_ref, tail_out, os.at[11])
    tail_put.start()
    put(o_ref, o_out)
    put(inv_ref, inv_out)
    put(nat_ref, nat_out)
    norm_share = Share(pc, hb_ref, hs, hr, 0, CHUNKS)
    for k in range(CHUNKS):
        rows = pl.ds(k * 32, 32)
        mid = x_ref[rows].astype(F32) + turn(fold.total(k), turn_ref, 2, tb)
        mid_ref[rows] = mid
        hb_ref[pc.w, rows] = turn(mid * scale_of(mid) * g_ref[1:2], turn_ref, 3, tb).astype(BF)
        norm_share.send(k)
        next(big, None)
    fold.wire.drain()
    while not done["down"]:
        next(big)
    columns = ((0, 512), (512, 512), (1024, 384))

    def times(rows, weights, lo, n):
        return dot_nn(rows[...].reshape(512, D), weights[:, :, pl.ds(lo, n)].reshape(D, n))

    for lo, n in columns:
        dact[:, pl.ds(lo, n)] = times(tail_ref, wdf, lo, n)
        next(big, None)
    for _ in norm_share.finish_steps():
        next(big, None)
    put(hb_ref, hb_out)
    while not done["gate"]:
        next(big)
    for lo, n in columns:
        gate[:, pl.ds(lo, n)] = times(hb_ref, wgf, lo, n)
        next(big, None)
    run_all(big)
    for lo, n in columns:
        cols = pl.ds(lo, n)
        up = times(hb_ref, wuf, lo, n)
        g, d = gate[:, cols], dact[:, cols]
        sg = 1.0 / (1.0 + jnp.exp(-g))
        act_ref[:, cols] = (g * sg * up).astype(BF)
        dg_ref[:, cols] = (d * up * sg * (1.0 + g * (1.0 - sg))).astype(BF)
        du_ref[:, cols] = (d * g * sg).astype(BF)
    for n in range(8):
        pieces, cols = pl.ds(n * 4, 4), pl.ds(n * 256, 256)
        dh = dot_nt(dg_ref[...], wgf[pieces].reshape(256, 1408)) + dot_nt(du_ref[...], wuf[pieces].reshape(256, 1408))
        part[:, :, cols] = dh.astype(BF).reshape(4, 128, 256)
    put(part, dh_out)
    tail_put.wait()
    for n in range(8):
        pieces, cols = pl.ds(n * 4, 4), pl.ds(n * 256, 256)
        tail_ref[:, :, cols] = dot_nt(act_ref[...], wdf[pieces].reshape(256, 1408)).astype(BF).reshape(4, 128, 256)
    put(tail_ref, out_out)
    for copy in puts:
        copy.wait()


def forward_call(pick, home, turns, x, t, g, cosine, sine, wq, wp, wd, wg, wu):
    ag = [dma(AG_SEMS), dma(AG_SEMS), ONE]
    return pl.pallas_call(
        forward_kernel,
        out_shape=(
            sds((4, 128, D), BF), sds((4, 2, 64, 512), BF), sds((4, 2, 64, 512), F32), sds((4, 2, 64, 512), F32),
            sds((4, 16, 256, 128), BF), sds((4, 128, D), BF), sds((32,) + wq.shape, BF), sds((32,) + wp.shape, BF),
            sds((128, D), F32), sds((4, 128, D), BF), sds((512, 1408), BF), sds((512, 1408), BF), sds((512, 1408), BF),
            sds((4, 128, D), BF), sds((4, 128, D), BF),
        ),
        in_specs=[spec(SM)] * 3 + [spec(VM)] * 5 + [spec(HB)] * 5,
        out_specs=(spec(HB),) * 8 + (spec(VM), spec(HB)) + (spec(VM),) * 3 + (spec(HB),) * 2,
        scratch_shapes=[
            vm((4, 128, D), BF), vm((4, 2, 64, 512), BF), vm((4, 2, 64, 512), F32), vm((4, 2, 64, 512), F32),
            vm((4, 16, 256, 128), BF), vm((4, 128, D), BF), vm((32,) + wq.shape, BF), vm((32,) + wp.shape, BF),
            vm((32,) + wd.shape, BF), vm((32,) + wg.shape, BF), vm((32,) + wu.shape, BF),
            vm((4, 128, D), BF), vm((512, 1408), F32), vm((512, 1408), F32),
            vm((4, 2, 64, 128), BF), vm((4, 64, 128), BF), vm((4, 64, 128), BF), vm((32, 4, 64, 128), BF), vm((32, 4, 64, 128), BF),
            vm((2, 512, 128), BF), vm((2, 512, 128), F32),
            vm((128, 512), BF), vm((4, 128, D), BF),
        ] + fold_scratch() + ag * 8 + [dma(3 * CHUNKS)] * 8 + [dma(12)],
        compiler_params=params(1),
        name="forward_rows",
    )(pick, home, turns, x, t, g, cosine, sine, wq, wp, wd, wg, wu)


def fold_scratch():
    return [vm((128, 2048), BF) for _ in range(4)] + [vm((2, 16, 32, 128), F32)]


def outer(dst, cols, lhs, rhs):
    for n in range(8):
        block = lhs[:, :, pl.ds(n * 256, 256)].reshape(512, 256)
        dst[pl.ds(n * 4, 4), :, cols] = dot_tn(block, rhs).astype(BF).reshape(4, 64, rhs.shape[1])


def backward_kernel(
    pick_ref, pair_ref, turn_ref, g_ref, dh_ref, tail_in, act_ref, hb_in, dg_in, du_in, mid_in, cot_ref, x_ref, cos_in, sin_in,
    q_in, o_in, inv_in, nat_in, wp_in, wq_in, a_in, out_in, pq_ref, pg_ref, pu_ref,
    grad_ref, out_ref, sq_ref, sp_ref, si_ref, sd_ref, gain_ref,
    xpart, xbuf, ypart, ybuf, rows, tail, hb, dg, du, ga, mid, cosine, sine, q, o, inv, wp, wq, nat0, nat1,
    dmid, dp, dkv, dnat, dqa, qt, gt, dl, dor, b0, b1, sb, b2, tb, vb,
    ds, dr, gs, gr, us, ur, ps, pr, ks, kr, js, jr, qs, qr, ns2, nr2, fs, fr, es, er, cs, cr, ss, sr, vs, vr, ls, ns, free,
):
    pc = Place()
    fetches = {}

    def fetch(name, src, dst, k):
        fetches[name] = pltpu.make_async_copy(src, dst, ls.at[k])
        fetches[name].start()

    def have(*names):
        for name in names:
            fetches.pop(name).wait()

    fetch("rows", dh_ref, rows, 0)
    fetch("tail", tail_in, tail, 1)
    fetch("mid", mid_in, mid, 2)
    fetch("hb", hb_in, hb, 3)
    fetch("dg", dg_in, dg, 4)
    fetch("du", du_in, du, 5)
    fetch("wp", wp_in, wp, 6)
    fetch("q", q_in, q, 7)
    fetch("o", o_in, o, 8)
    fetch("inv", inv_in, inv, 9)
    fetch("cos", cos_in, cosine, 10)
    fetch("sin", sin_in, sine, 11)
    fetch("wq", wq_in, wq, 12)
    order = (pc.w, pc.near_twin, pc.far, pc.far_twin)
    slots = (nat0, nat1)
    tiles = [pltpu.make_async_copy(nat_in.at[s], slots[n % 2], ns.at[n]) for n, s in enumerate(order)]
    tiles[0].start()
    tiles[1].start()
    greet(pc)

    def tell(k, wsh):
        peers = [pc.over(), pc.twin()] if wsh else ctx_peers(pc)
        for peer in peers:
            pl.semaphore_signal(free.at[k], inc=1, device_id=peer, device_id_type=MESH)

    def hear(k, wsh):
        pl.semaphore_wait(free.at[k], 2 if wsh else 5)

    def total(own, other):
        return own[...].astype(F32) + other[...].astype(F32)

    def to(ref):
        def finish(own, other):
            ref[...] = total(own, other)

        return finish

    gains = {}

    def to_part(name, ref, n, cols, piece):
        def finish(own, other):
            value = total(own, other)
            ref[:, n, cols] = value
            gains[name] = jnp.sum(value * piece[:, cols].astype(F32), -1, keepdims=True)

        return finish

    boxes = (b0, b1, sb, b2)
    wide = slice(0, 1408)

    def y_sum(lo, n, ssem, rsem, finish):
        cols = pl.ds(lo, n)
        return scatter_steps(pc, ypart.at[:, :, cols], ybuf.at[:, cols], ssem, rsem, finish)

    have("rows")
    fold = Fold(pc, rows, boxes, fs, fr, CHUNKS)
    fold.far_twin()
    fold.near_twin()
    have("hb", "dg")
    outer(ypart, wide, hb, dg[...])
    gate = y_sum(0, 1408, gs, gr, to_part("gate", si_ref, 0, pl.ds(0, 1408), pg_ref))
    next(gate)
    fold.far()
    have("tail", "du")
    outer(xpart, wide, tail, act_ref[...])
    down = scatter_steps(pc, xpart, xbuf, ds, dr, to(sd_ref))
    next(down)
    next(gate)
    fetch("out", out_in, tail, 13)
    state = {"y": False, "a": False}

    def lane_x():
        yield from down
        tell(0, False)
        outer(xpart, wide, hb, du[...])
        fetch("a", a_in, hb, 14)
        state["a"] = True
        hear(0, False)
        yield
        yield from scatter_steps(pc, xpart, xbuf, us, ur, to_part("up", si_ref, 1, pl.ds(0, 1408), pu_ref))

    def lane_y():
        yield from gate
        tell(2, False)
        hear(2, False)
        state["y"] = True

    xs, ys = lane_x(), lane_y()
    share = Share(pc, ga, ss, sr, 0, CHUNKS)
    have("mid")
    for k in range(CHUNKS):
        r = pl.ds(k * 32, 32)
        m = mid[r]
        weighted = turn(fold.total(k), turn_ref, 4, tb) * g_ref[1:2]
        scale = scale_of(m)
        mean = jnp.mean(weighted * m, -1, keepdims=True)
        dm = cot_ref[r].astype(F32) + scale * weighted - m * (scale * scale * scale) * mean
        dmid[r] = dm
        ga[pc.w, r] = turn(dm, turn_ref, 5, tb).astype(BF)
        share.send(k)
        next(ys, None)
    fold.wire.drain()
    tell(3, True)
    have("out", "wp", "q", "o", "inv", "cos", "sin")
    out_fold = Fold(pc, tail, boxes, es, er, CHUNKS)

    def put_out(k, value):
        r = pl.ds(k * 32, 32)
        out_ref[r] = mid[r] + turn(value, turn_ref, 7, tb)

    out_steps = out_fold.steps(put_out)

    def poll(n, part):
        if n == 0:
            next(ys, None)
            next(ys, None)
            next(xs, None)
        elif n == 1:
            share.relay(part)
            next(xs, None)
        else:
            next(lanes["keys"], None)
            next(xs, None)
            if part % 2:
                next(lanes.get("proj"), None) if n == 3 else next(xs, None)

    rows_iota = lax.broadcasted_iota(jnp.int32, (256, 512), 0)
    ones = jnp.ones((8, 128), BF)

    def tile(j, keys_values, limit=None):
        queries, upward = qt[j], gt[j]
        e = jnp.exp(dot_nt(keys_values, queries))
        if limit is not None:
            e = jnp.where(rows_iota < limit, e, 0.0)
        dscore = (e * (dot_nt(keys_values, upward) - dl[j, 0:1])).astype(BF)
        return dot_tn(dscore, keys_values), dot_nn(dscore, queries) + dot_nn(e.astype(BF), upward)

    lanes = {}

    def attend(n):
        s, kv = order[n], slots[n % 2]
        if n == 1:
            share.arrive_twin()
        if n == 3:
            share.arrive_last()
            outer(ypart, pl.ds(1024, 512), ga, o[...].reshape(512, 512).astype(BF))
            lanes["proj"] = y_sum(1024, 512, ps, pr, to(sp_ref))
            next(lanes["proj"])
        dor[...] = dot_nn(ga[s], wp[...].reshape(D, 512)).reshape(2, 64, 512)
        for j in range(2):
            sums = []
            for m2 in range(4):
                cols = pl.ds(m2 * 128, 128)
                pair = q[s, j, :, cols].astype(F32)
                ratio = dor[j, :, cols] * inv[s, j, :, cols]
                prod = ratio * o[s, j, :, cols]
                for odd in (False, True):
                    place = pl.ds(m2 * 128 + (64 if odd else 0), 64)
                    qt[j, place] = head_tile(pair, odd, False).astype(BF)
                    gt[j, place] = head_tile(ratio, odd, True).astype(BF)
                    sums.append(head_tile(prod, odd, False))
            whole = jnp.concatenate(sums, 0)
            big = whole.astype(BF)
            rest = (whole - big.astype(F32)).astype(BF)
            dl[j] = dot_nt(ones, big) + dot_nt(ones, rest)
        dqa[...] = jnp.zeros_like(dqa)
        tiles[n].wait()

        def body(i, carry):
            which = pick_ref[0, s * 9 + i]
            dq1, dkv1 = tile(1, kv[i])
            dq2, dkv2 = tile(which, kv[pick_ref[1, s * 9 + i]], pick_ref[2, s * 9 + i])
            to_low = jnp.broadcast_to(which, dq2.shape) == 0
            dqa[0] += jnp.where(to_low, dq2, 0.0)
            dqa[1] += dq1 + jnp.where(to_low, 0.0, dq2)
            to_low = jnp.broadcast_to(which, dkv2.shape) == 0
            dnat[i] = (dkv1 + jnp.where(to_low, dkv2, 0.0)).reshape(4, 64, 128)
            dnat[15 - i] = jnp.where(to_low, 0.0, dkv2).reshape(4, 64, 128)
            return carry

        for part in range(4):
            lax.fori_loop(2 * part, 2 * part + 2, body, 0)
            poll(n, part)
        kt = pick_ref[1, s * 9 + 8]
        dq3, dkv3 = tile(1, kv[kt], pick_ref[2, s * 9 + 8])
        dqa[1] += dq3
        for t in range(8, 16):
            here = jnp.broadcast_to(kt, dkv3.shape) == t
            dnat[t] += jnp.where(here, dkv3, 0.0).reshape(4, 64, 128)
        if n + 2 < 4:
            tiles[n + 2].start()
        for j in range(2):
            for m2 in range(4):
                even = dqa[j, pl.ds(m2 * 128, 64)]
                odd = dqa[j, pl.ds(m2 * 128 + 64, 64)]
                both = jnp.where(upper_lanes(even.shape), pltpu.roll(odd, 64, 1), even) * 0.125
                turned = both * cosine[s, j] - swap_lanes(both) * sine[s, j]
                dp[s, j, :, pl.ds(m2 * 128, 128)] = turned.astype(BF)
        while not state["y"]:
            next(ys, None)

        def place_block(c, carry):
            for j in range(2):
                at = s * 64 + c * 2 + j
                block = dnat[pair_ref[0, at], pair_ref[1, at]].astype(BF)
                ypart[c, :, pl.ds((n * 2 + j) * 128, 128)] = block
            return carry

        lax.fori_loop(0, 32, place_block, 0)

    attend(0)
    attend(1)
    lanes["keys"] = y_sum(0, 512, ks, kr, to(dkv.at[:, pl.ds(0, 512)]))
    next(lanes["keys"])
    attend(2)
    attend(3)
    keys = y_sum(512, 512, js, jr, to(dkv.at[:, pl.ds(512, 512)]))
    next(keys)
    hear(3, True)
    next(out_steps)
    for _ in lanes["keys"]:
        next(keys, None)
    tell(6, False)
    while not state["a"]:
        next(xs)
    have("a")
    outer(ypart, pl.ds(0, 512), hb, dp[:, :, :, pl.ds(0, 512)].reshape(512, 512))
    hear(6, False)

    heads = y_sum(0, 512, qs, qr, to_part("heads", sq_ref, 0, pl.ds(0, 512), pq_ref))
    next(heads)
    next(out_steps)
    count = 0
    for _ in keys:
        count += 1
        next(lanes["proj"], None)
        if count % 2:
            next(xs, None)
        else:
            next(heads, None)
        if count % 4 == 0:
            next(out_steps, None)
    for _ in out_steps:
        next(xs, None)
    tell(4, True)
    for n, s in enumerate(order):
        for j in range(2):
            both = dkv[:, pl.ds((n * 2 + j) * 128, 128)]
            key_cosine, key_sine = key_only(cosine[s, j], sine[s, j])
            turned = both * key_cosine - swap_lanes(both) * key_sine
            dp[s, j, :, pl.ds(512, 128)] = turned.astype(BF)
    have("wq")

    def back(s):
        for n in range(8):
            columns = wq[pl.ds(n * 4, 4)].reshape(256, 640)
            rows[s, :, pl.ds(n * 256, 256)] = dot_nt(dp[s].reshape(128, 640), columns).astype(BF)

    hear(4, True)
    last = Fold(pc, rows, boxes, cs, cr, CHUNKS)
    back(pc.far_twin)
    last.far_twin()
    back(pc.near_twin)
    last.near_twin()
    back(pc.far)
    last.far()
    for _ in lanes["proj"]:
        next(xs, None)
    tell(5, False)
    outer(ypart, pl.ds(1024, 128), hb, dp[:, :, :, pl.ds(512, 128)].reshape(512, 128))
    hear(5, False)
    pair_sum = y_sum(1024, 128, ns2, nr2, to_part("pair", sq_ref, 0, pl.ds(512, 128), pq_ref))
    next(pair_sum)
    back(pc.w)
    for k in range(CHUNKS):
        next(pair_sum)
        r = pl.ds(k * 32, 32)
        x = x_ref[r].astype(F32)
        weighted = turn(last.total(k), turn_ref, 6, tb) * g_ref[0:1]
        scale = scale_of(x)
        mean = jnp.mean(weighted * x, -1, keepdims=True)
        grad_ref[r] = dmid[r] + scale * weighted - x * (scale * scale * scale) * mean
    last.wire.drain()
    run_all(pair_sum, heads, xs)
    first = gains["heads"] + gains["pair"]
    second = gains["gate"] + gains["up"]
    line = lax.broadcasted_iota(jnp.int32, (64, 128), 0)
    lane = lax.broadcasted_iota(jnp.int32, (64, 128), 1)
    both = jnp.where(lane == line, first, 0.0) + jnp.where(lane == line + 64, second, 0.0)
    vb[0] = jnp.broadcast_to(jnp.sum(both, 0, keepdims=True), (8, 128))
    wire = Wire(vs, vr)
    wire.send(0, vb.at[0], vb.at[1], pc.twin())
    wire.arrive(0, vb.at[1], pc.twin())
    vb[2] = vb[0] + vb[1]
    wire.send(1, vb.at[2], vb.at[3], pc.over())
    wire.arrive(1, vb.at[3], pc.over())
    gain_ref[pc.c] = vb[2] + vb[3]

    def gain_at(v, dx, dz):
        return gain_ref.at[pc.piece(0, v, dx, dz)]

    steps = (1, -1, 2)
    wire.send(2, gain_at(0, 0, 0), gain_at(0, 0, 0), pc.mate())
    wire.arrive(2, gain_at(1, 0, 0), pc.mate())
    for v in (0, 1):
        for i, d in enumerate(steps):
            wire.send(3 + v * 3 + i, gain_at(v, 0, 0), gain_at(v, 0, 0), pc.step("x", d))
    for v in (0, 1):
        for i, d in enumerate(steps):
            wire.arrive(3 + v * 3 + i, gain_at(v, -d if d < 2 else 2, 0), pc.step("x", -d if d < 2 else 2))
    for v in (0, 1):
        for m, dx in enumerate((0, 1, -1, 2)):
            for i, d in enumerate(steps):
                wire.send(9 + (v * 4 + m) * 3 + i, gain_at(v, dx, 0), gain_at(v, dx, 0), pc.step("z", d))
    for v in (0, 1):
        for m, dx in enumerate((0, 1, -1, 2)):
            for i, d in enumerate(steps):
                there = -d if d < 2 else 2
                wire.arrive(9 + (v * 4 + m) * 3 + i, gain_at(v, dx, there), pc.step("z", there))
    wire.drain()


def backward_call(*args):
    rs = [dma(RS_SEMS)] * 2
    small = [dma(3 * CHUNKS)] * 2
    return pl.pallas_call(
        backward_kernel,
        out_shape=(
            sds((128, D), F32), sds((128, D), F32), sds((64, 1, 640), F32), sds((64, 512), F32),
            sds((64, 2, 1408), F32), sds((64, 1408), F32), sds((32, 8, 128), F32),
        ),
        in_specs=[spec(SM)] * 3 + [spec(VM)] + [spec(HB)] * 2 + [spec(VM)] + [spec(HB)] * 4 + [spec(VM)] * 2
        + [spec(HB)] * 10 + [spec(VM)] * 3,
        out_specs=(spec(VM),) * 7,
        scratch_shapes=[
            vm((32, 64, 1408), BF), vm((31 * 64, 1408), BF), vm((32, 64, 1536), BF), vm((31 * 64, 1536), BF),
            vm((4, 128, D), BF), vm((4, 128, D), BF), vm((4, 128, D), BF), vm((512, 1408), BF), vm((512, 1408), BF),
            vm((4, 128, D), BF), vm((128, D), F32), vm((4, 2, 64, 128), F32), vm((4, 2, 64, 128), F32),
            vm((4, 2, 64, 512), BF), vm((4, 2, 64, 512), F32), vm((4, 2, 64, 512), F32), vm((32, 64, 512), BF),
            vm((32, 64, 640), BF), vm((16, 256, 128), BF), vm((16, 256, 128), BF),
            vm((128, D), F32), vm((4, 2, 64, 640), BF), vm((64, 1024), F32), vm((16, 4, 64, 128), F32),
            vm((2, 512, 128), F32), vm((2, 512, 128), BF), vm((2, 512, 128), BF), vm((2, 8, 512), F32), vm((2, 64, 512), F32),
        ] + fold_scratch() + [vm((4, 8, 128), F32)]
        + rs * 8 + small * 4 + [dma(33)] * 2 + [dma(16), dma(4), pltpu.SemaphoreType.REGULAR((7,))],
        compiler_params=params(2),
        name="backward_rows",
    )(*args)


def rope_tables(positions):
    half_width = HD // 2
    inverse = ROPE_BASE ** (-(jnp.arange(half_width, dtype=F32) * 2.0 / HD))
    angles = positions.astype(F32)[..., None] * inverse
    cosine, sine = jnp.cos(angles), jnp.sin(angles)
    signed = jnp.concatenate([-sine, sine], -1)
    return (jnp.concatenate([cosine] * 4, -1), jnp.concatenate([signed] * 2, -1))


def adamw_step(master, first_state, second_state, gradient, rate_value):
    first_new = BETA_FIRST * first_state + (1.0 - BETA_FIRST) * gradient
    second_new = BETA_SECOND * second_state + (1.0 - BETA_SECOND) * gradient * gradient
    first_fix = 1.0 - BETA_FIRST**STEP
    second_fix = 1.0 - BETA_SECOND**STEP
    update = first_new / first_fix / (jnp.sqrt(second_new / second_fix) + ADAM_EPS)
    return (master - rate_value * (update + WEIGHT_DECAY * master), first_new, second_new)


def per_device(
    tokens, cotangent, block_pairs, offsets,
    qkv_master, qkv_first, qkv_second,
    proj_master, proj_first, proj_second,
    inner_master, inner_first, inner_second,
    down_master, down_first, down_second,
    gains, gain_first, gain_second,
):
    offsets = offsets.astype(jnp.int32)
    g1, g2 = gains[:, 0][None], gains[:, 1][None]
    qkv_piece = qkv_master[:, 0].astype(BF)
    gate_piece, up_piece = inner_master[:, 0].astype(BF), inner_master[:, 1].astype(BF)
    down_piece = down_master.astype(BF).T
    proj_piece = proj_master.astype(BF).T
    place = lax.axis_index("ctx").astype(jnp.int32)
    pick, home, pairs, turns = table_call(block_pairs.reshape(4, 64).astype(jnp.int32), offsets, place[None])
    own_pairs = lax.dynamic_index_in_dim(block_pairs, place, 1, keepdims=False)
    positions = (own_pairs[:, :, None] * BLK + jnp.arange(BLK, dtype=jnp.int32)).reshape(4, 2, 64)
    cosine, sine = rope_tables(positions)

    (a_all, q, o, inverse, nat, tail_all, qkv_full, proj_full, middle, hb, act, dgate, dup, dh, out_part) = forward_call(
        pick, home, turns, tokens[0], cotangent[0], jnp.concatenate([g1, g2], 0), cosine, sine,
        qkv_piece, proj_piece, down_piece, gate_piece, up_piece,
    )
    input_grad, output, qkv_sum, proj_sum, inner_sum, down_sum, gain_sums = backward_call(
        pick, pairs, turns, jnp.concatenate([g1, g2], 0), dh, tail_all, act, hb,
        dgate, dup, middle, cotangent[0], tokens[0], cosine, sine, q, o, inverse, nat, proj_full, qkv_full, a_all, out_part, qkv_piece, gate_piece, up_piece,
    )
    gain_sums = gain_sums[:, 0]
    pieces = jnp.arange(32, dtype=jnp.int32)

    def natural(sums, offset):
        here = ((pieces[None] + offset + 32 - pieces[:, None]) & 31) == 0
        return jnp.sum(jnp.where(here[:, :, None], sums[None], 0.0), 1).reshape(D)

    gain_grad = jnp.stack([natural(gain_sums[:, :64], offsets[0]), natural(gain_sums[:, 64:], offsets[2])], 1) / gains

    rate_rows = 2.0 / math.sqrt(D)
    rate_proj = 1.0
    rate_down = 2.0 / math.sqrt(FF)
    qkv_out = adamw_step(qkv_master, qkv_first, qkv_second, qkv_sum, rate_rows)
    proj_out = adamw_step(proj_master, proj_first, proj_second, proj_sum.T, rate_proj)
    inner_out = adamw_step(inner_master, inner_first, inner_second, inner_sum, rate_rows)
    down_out = adamw_step(down_master, down_first, down_second, down_sum.T, rate_down)
    gain_out = adamw_step(gains, gain_first, gain_second, gain_grad, GAIN_RATE)
    return (output[None], input_grad[None], *qkv_out, *proj_out, *inner_out, *down_out, *gain_out)


def solution(mesh):
    rows, every = P("wsh", "ctx", None), P()
    qkv, inner, cols = P("ctx", "wsh", None), P("ctx", None, "wsh"), P("wsh", "ctx")
    return jax.shard_map(
        per_device,
        mesh=mesh,
        in_specs=(rows, rows, every, every) + (qkv,) * 3 + (cols,) * 3 + (inner,) * 3 + (cols,) * 3 + (every,) * 3,
        out_specs=(rows, rows) + (qkv,) * 3 + (cols,) * 3 + (inner,) * 3 + (cols,) * 3 + (every,) * 3,
        check_vma=False,
    )
```
